128 devices in a mesh: ctx: 16 (over x_lo, z, core), tp: 8 (over x_hi, y).
Axes of the slice: x: 4 (x_hi: 2, x_lo: 2; x = x_hi * 2 + x_lo), y: 4, z: 4, core: 2. Of those that a mesh axis runs over, the one named last changes fastest.
Arguments:
- text_embed: bfloat16 [16384, 3584], P('ctx', 'tp'), may hold values from -6 to 6
- frame_features: bfloat16 [8192, 1152], P(('ctx', 'tp')), may hold values from -6 to 6
- frame_positions: int32 [8192], P(('ctx', 'tp')), may hold values from 0 to 16383, as said below
- span_order: int32 [32], replicated, may hold values from 0 to 31, as said below
- projector: bfloat16 [1152, 3584], replicated, may hold values from -0.1875 to 0.1875
- norm_gain: bfloat16 [3584], P('tp'), may hold values from 0.099609375 to 1.8984375
- query_weight: bfloat16 [3584, 2048], P(None, 'tp'), may hold values from -1 to 1
- key_weight: bfloat16 [3584, 512], replicated, may hold values from -0.125 to 0.125
- value_weight: bfloat16 [3584, 512], replicated, may hold values from -0.09375 to 0.09375
- out_weight: bfloat16 [2048, 3584], P('tp'), may hold values from -0.5 to 0.5
Outputs:
- mixed: bfloat16 [16384, 3584], P('ctx', 'tp')
The draws below stay inside these ranges and needn't reach their ends.
Inputs may be any that keep to these rules, and one draw needn't show every extreme that they name: `span_order`: each span of the sequence once. `frame_positions`: distinct; the 64 frame tokens of one device lie in the rows of exactly 8 indices of ctx, 8 in each.
All inputs are finite; a program needn't handle non-finite values.
Results may differ from the reference program's by a relative error of at most 0.028.
The reference program's roundings to bfloat16 on the way count: a program that leaves them out, or rounds other values in their place, can miss the bound.
Values may be sent and summed in bfloat16 or wider, within the bound.
A program may use at most 128 MiB of HBM per device.

```python
import math
import jax
import jax.numpy as jnp
from jax import lax

D = 3584
VIS = 1152
HS = 128
KVH = 4
QHD = 2
CAP = 8
CH = 512
FT_DEV = 64
QH = 16
SEQ = 16384
NF = 8192
N_CTX = 16
N_TP = 8
DEVICES = 128


def span_sequence(key):
    return jax.random.permutation(key, 2 * N_CTX).astype(jnp.int32)


def draw_span_order(key, part):
    return span_sequence(key)


def draw_frame_positions(key, part):
    order = span_sequence(key)
    key = jax.random.fold_in(key, 5)
    first, second, third = jax.random.split(key, 3)
    groups = FT_DEV // CAP
    senders = DEVICES
    favour = jax.random.randint(first, (N_CTX,), 1, 5).astype(jnp.int32)
    scores = jax.random.randint(second, (senders, N_CTX), 0, 4096).astype(jnp.int32) * favour[None, :] * N_CTX + jnp.arange(N_CTX, dtype=jnp.int32)[None, :]
    chosen = lax.top_k(scores, groups)[1].astype(jnp.int32)
    target = jnp.repeat(chosen, CAP, axis=1).reshape(-1)
    onehot = (target[:, None] == jnp.arange(N_CTX, dtype=jnp.int32)[None, :]).astype(jnp.int32)
    before = jnp.cumsum(onehot, axis=0) - onehot
    rank = jnp.sum(before * onehot, axis=1)
    row_keys = jax.random.split(third, N_CTX)
    shuffles = jax.vmap(lambda k: jax.random.permutation(k, 2 * CH))(row_keys).astype(jnp.int32)
    row = shuffles[target, rank]
    slot = 2 * target + row // CH
    return (order[slot] * CH + row % CH).astype(jnp.int32)


def draw_query_weight(key, part):
    key = jax.random.fold_in(key, 11)
    scale = 1.5 / D ** 0.5
    values = jax.random.normal(key, (D, QH * HS), jnp.float32) * scale
    return jnp.clip(values, -1.0, 1.0).astype(jnp.bfloat16)


def level_of(key, extent, cuts, least, top_value):
    loudness = 1.0
    for position, shards_of in cuts:
        draws = jax.random.uniform(jax.random.fold_in(jax.random.fold_in(key, 6), position), (shards_of,), jnp.float32, least / len(cuts), top_value / len(cuts))
        loudness = loudness * jnp.repeat(jnp.exp(draws), extent[position] // shards_of).reshape((-1,) + (1,) * (len(extent) - 1 - position))
    return loudness


def gaussian(rng, extent, deviation, limit, cuts=(), kind=jnp.bfloat16):
    gain = level_of(rng, extent, cuts, -0.22, 0.18) if cuts else 1.0
    values = jax.random.normal(rng, extent, jnp.float32) * deviation * gain
    return jnp.minimum(jnp.maximum(values, -limit), limit).astype(kind)


def setup_inputs(seed: int = 0) -> dict:
    streams_of = jax.random.split(jax.random.key(seed), 11)
    return {
        "text_embed": gaussian(streams_of[0], (SEQ, D), 1.0, 6.0, ((0, 16), (1, 8))),
        "frame_features": gaussian(streams_of[1], (NF, VIS), 1.0, 6.0, ((0, 128),)),
        "frame_positions": draw_frame_positions(jax.random.fold_in(streams_of[10], 71), 0),
        "span_order": draw_span_order(jax.random.fold_in(streams_of[10], 71), 0),
        "projector": gaussian(streams_of[4], (VIS, D), VIS ** -0.5, 0.1875),
        "norm_gain": jnp.clip(1.0 + 0.18 * jax.random.normal(streams_of[5], (D,), jnp.float32), 0.099609375, 1.8984375).astype(jnp.bfloat16),
        "query_weight": draw_query_weight(jax.random.fold_in(streams_of[10], 71), 0),
        "key_weight": gaussian(streams_of[7], (D, KVH * HS), (D // 2) ** -0.5, 0.125),
        "value_weight": gaussian(streams_of[8], (D, KVH * HS), D ** -0.5, 0.09375),
        "out_weight": gaussian(streams_of[9], (QH * HS, D), HS ** -0.5, 0.5, ((0, 8),)),
    }


def rotate(field, positions):
    half = field.shape[-1] // 2
    freqs = 1000000.0 ** (-(jnp.arange(half, dtype=jnp.float32) * 2.0 / field.shape[-1]))
    angles = positions.astype(jnp.float32)[:, None] * freqs[None, :]
    cosine = jnp.cos(angles)[:, None, :]
    sine = jnp.sin(angles)[:, None, :]
    first = field[..., :half]
    second = field[..., half:]
    return jnp.concatenate([first * cosine - second * sine, second * cosine + first * sine], axis=-1)

def reference(text_embed, frame_features, frame_positions, span_order, projector, norm_gain, query_weight, key_weight, value_weight, out_weight):
    length, width = text_embed.shape
    slots = span_order.shape[0]
    slot_of = jnp.zeros((slots,), jnp.int32).at[span_order].set(jnp.arange(slots, dtype=jnp.int32))
    storage = slot_of[frame_positions // CH] * CH + frame_positions % CH
    projected = jax.nn.gelu(jnp.dot(frame_features, projector, preferred_element_type=jnp.float32), approximate=False).astype(jnp.bfloat16)
    placed = text_embed.at[storage].set(projected)
    placed_f = placed.astype(jnp.float32)
    meansq = lax.optimization_barrier(jnp.mean(placed_f * placed_f, axis=1, keepdims=True))
    normed = (placed_f * lax.rsqrt(meansq + 1e-06) * norm_gain.astype(jnp.float32)[None, :]).astype(jnp.bfloat16)
    rows = jnp.arange(length, dtype=jnp.int32)
    positions = span_order[rows // CH] * CH + rows % CH
    query = jnp.dot(normed, query_weight, preferred_element_type=jnp.float32).reshape(length, QH, HS)
    keys = jnp.dot(normed, key_weight, preferred_element_type=jnp.float32).reshape(length, KVH, HS)
    values = jnp.dot(normed, value_weight, preferred_element_type=jnp.float32).reshape(length, KVH, HS).astype(jnp.bfloat16)
    query = rotate(query, positions).astype(jnp.bfloat16)
    keys = rotate(keys, positions).astype(jnp.bfloat16)
    scale = 1.0 / math.sqrt(HS)
    blocks = length // CH

    def one_head(head):
        q_head = lax.dynamic_index_in_dim(query, head, 1, keepdims=False)
        kv_head = head * KVH // QH
        k_head = lax.dynamic_index_in_dim(keys, kv_head, 1, keepdims=False)
        v_head = lax.dynamic_index_in_dim(values, kv_head, 1, keepdims=False)

        def one_block(block):
            start = (block * CH).astype(jnp.int32)
            q_block = lax.dynamic_slice_in_dim(q_head, start, CH, 0)
            q_pos = lax.dynamic_slice_in_dim(positions, start, CH, 0)
            scores = jnp.dot(q_block, k_head.T, preferred_element_type=jnp.float32) * scale
            allowed = positions[None, :] <= q_pos[:, None]
            largest = lax.optimization_barrier(jnp.max(jnp.where(allowed, scores, -jnp.inf), axis=1, keepdims=True))
            weights = jnp.where(allowed, jnp.exp(scores - largest), 0.0)
            total = lax.optimization_barrier(jnp.sum(weights, axis=1, keepdims=True))
            summed = jnp.dot(weights.astype(jnp.bfloat16), v_head, preferred_element_type=jnp.float32)
            return (summed / total).astype(jnp.bfloat16)
        return lax.map(one_block, jnp.arange(blocks, dtype=jnp.int32)).reshape(length, HS)
    attended = lax.map(one_head, jnp.arange(QH, dtype=jnp.int32))
    attended = jnp.transpose(attended, (1, 0, 2)).reshape(length, QH * HS)
    group = QHD * HS
    summed = jnp.zeros((length, width), jnp.float32)
    for index in range(N_TP):
        part = jnp.dot(attended[:, index * group:(index + 1) * group], out_weight[index * group:(index + 1) * group], preferred_element_type=jnp.float32).astype(jnp.bfloat16)
        part = lax.optimization_barrier(part)
        summed = summed + part.astype(jnp.float32)
    return (placed_f + summed).astype(jnp.bfloat16)
```

```python
import functools
import math

import jax
import jax.numpy as jnp
from jax import lax
from jax.experimental import pallas as pl
from jax.experimental.pallas import tpu as pltpu
from jax.sharding import PartitionSpec as P

HS = 128
KVH = 4
CAP = 8
CH = 512
N_CTX = 16
N_TP = 8
PAIRS = 8
OFF = 64
HALF = 32
MESH = pl.DeviceIdType.MESH
LOG2E = math.log2(math.e)


def signal(sem, ctx, tp):
    pl.semaphore_signal(sem, inc=1, device_id=(ctx, tp), device_id_type=MESH)


def push(src, dst, send_sem, recv_sem, ctx, tp):
    return pltpu.make_async_remote_copy(
        src_ref=src, dst_ref=dst, send_sem=send_sem, recv_sem=recv_sem,
        device_id=(ctx, tp), device_id_type=MESH,
    )


def rows_kernel(placed, gain, rows, normed, gains, send, recv, fsend, frecv, gsend, grecv):
    c = lax.axis_index("ctx")
    t = lax.axis_index("tp")
    pair = c // 2
    core = c % 2
    sibling = pair * 2 + 1 - core
    own = t == pair
    barrier = pltpu.get_barrier_semaphore()
    signal(barrier, sibling, t)
    for j in range(N_TP):
        if_self = jnp.logical_and(own, j == t)

        @pl.when(jnp.logical_not(if_self))
        def _():
            signal(barrier, 2 * t + core, j)

    pl.semaphore_wait(barrier, jnp.where(own, PAIRS, PAIRS + 1))

    def block(d):
        e = lax.rem(pair + d, PAIRS)
        return push(placed.at[:, e], rows.at[core, t], send.at[d], recv.at[t], 2 * e + core, pair)

    def gain_block(d):
        e = lax.rem(pair + d, PAIRS)
        return push(gain, gains.at[t], gsend.at[d], grecv.at[t], 2 * e + core, pair)

    @pl.when(own)
    def _():
        pltpu.make_async_copy(placed.at[:, pair], rows.at[core, t], recv.at[t]).start()
        pltpu.make_async_copy(gain, gains.at[t], grecv.at[t]).start()

    @pl.when(jnp.logical_not(own))
    def _():
        block(0).start()
        gain_block(0).start()

    for d in range(1, PAIRS):
        block(d).start()
        gain_block(d).start()

    def forward(j):
        return push(rows.at[core, j], rows.at[core, j], fsend.at[j], frecv.at[j], sibling, t)

    for d in range(N_TP):
        j = lax.rem(t + d, N_TP)
        push(rows.at[core, j], rows.at[core, j], send.at[0], recv.at[j], sibling, t).wait_recv()
        forward(j).start()
    for j in range(N_TP):
        push(gain, gains.at[j], gsend.at[0], grecv.at[j], sibling, t).wait_recv()

    def receive(j):
        push(
            rows.at[1 - core, j], rows.at[1 - core, j], fsend.at[j], frecv.at[j], sibling, t
        ).wait_recv()

    width = N_TP * placed.shape[-1]

    def normalise(a):
        total = jnp.zeros((2 * OFF, 1), jnp.float32)
        for j in range(N_TP):
            x = rows[a, j].reshape(2 * OFF, -1).astype(jnp.float32)
            total = total + jnp.sum(x * x, axis=1, keepdims=True)
        inverse = lax.rsqrt(total / width + 1e-06)
        for j in range(N_TP):
            x = rows[a, j].reshape(2 * OFF, -1).astype(jnp.float32)
            g = gains[j, 0:1, :].astype(jnp.float32)
            normed[j, a] = (x * inverse * g).astype(jnp.bfloat16)

    normalise(core)
    for j in range(N_TP):
        receive(j)
    normalise(1 - core)

    @pl.when(jnp.logical_not(own))
    def _():
        block(0).wait_send()
        gain_block(0).wait_send()

    for d in range(1, PAIRS):
        block(d).wait_send()
        gain_block(d).wait_send()
    for j in range(N_TP):
        forward(j).wait_send()


def rows_exchange(placed, gain):
    part = placed.shape[-1]
    vm = pl.BlockSpec(memory_space=pltpu.VMEM)
    return pl.pallas_call(
        rows_kernel,
        out_shape=(
            jax.ShapeDtypeStruct((2, N_TP, 2, OFF, part), jnp.bfloat16),
            jax.ShapeDtypeStruct((N_TP, 2, 2 * OFF, part), jnp.bfloat16),
        ),
        in_specs=[vm, vm],
        out_specs=(vm, vm),
        scratch_shapes=[
            pltpu.VMEM((N_TP, 16, part), jnp.bfloat16),
            pltpu.SemaphoreType.DMA((PAIRS,)),
            pltpu.SemaphoreType.DMA((N_TP,)),
            pltpu.SemaphoreType.DMA((N_TP,)),
            pltpu.SemaphoreType.DMA((N_TP,)),
            pltpu.SemaphoreType.DMA((PAIRS,)),
            pltpu.SemaphoreType.DMA((N_TP,)),
        ],
        compiler_params=pltpu.CompilerParams(
            collective_id=1, has_side_effects=True, vmem_limit_bytes=24 * 2**20
        ),
        name="rows",
    )(placed, gain)


def qkv_kernel(
    normed, query_weight, key_weight, value_weight, cosine, sine, kv_cosine, kv_sine,
    query_out, kv_out, weight, query, kv, wsem, qsend, qrecv, ksend, krecv,
):
    c = lax.axis_index("ctx")
    t = lax.axis_index("tp")
    pair = c // 2
    core = c % 2
    q_cols = N_TP * HS
    kv_cols = KVH * HS

    def load(j):
        return pltpu.make_async_copy(
            query_weight.at[j], weight.at[:, pl.ds(j * HS, HS)], wsem.at[j]
        )

    kv_slot = weight.at[:, pl.ds(q_cols, kv_cols)]

    @pl.when(core == 0)
    def _():
        pltpu.make_async_copy(key_weight, kv_slot, wsem.at[N_TP]).start()

    @pl.when(core == 1)
    def _():
        pltpu.make_async_copy(value_weight, kv_slot, wsem.at[N_TP]).start()

    for j in range(N_TP):
        load(j).start()

    barrier = pltpu.get_barrier_semaphore()
    for k in range(2):
        for d in range(N_TP):
            if d == 0:

                @pl.when(core != k)
                def _():
                    signal(barrier, 2 * pair + k, t)

            else:
                signal(barrier, 2 * pair + k, lax.rem(t + d, N_TP))
    pl.semaphore_wait(barrier, 2 * N_TP - 1)

    part = normed.shape[-1]

    def product(start, cols):
        total = jnp.zeros((4 * OFF, cols), jnp.float32)
        for j in range(N_TP):
            x = normed[j].reshape(4 * OFF, part)
            total = total + jnp.dot(
                x, weight[j * part : (j + 1) * part, start : start + cols],
                preferred_element_type=jnp.float32,
            )
        return total

    def rotated(x, cos, sin):
        return (x * cos + pltpu.roll(x, HS // 2, 1) * sin).astype(jnp.bfloat16)

    def kv_push(d):
        j = lax.rem(t + d, N_TP)
        return push(kv.at[j // 2], kv_out.at[t], ksend.at[d], krecv.at[t], c, j)

    def q_push(d, k):
        j = lax.rem(t + d, N_TP)
        return push(
            query.at[j, :, pl.ds(k * HALF, HALF), :], query_out.at[core, t],
            qsend.at[d, k], qrecv.at[core, t], 2 * pair + k, j,
        )

    pltpu.make_async_copy(key_weight, kv_slot, wsem.at[N_TP]).wait()
    total = product(q_cols, kv_cols)
    for h in range(KVH):
        kv[h] = rotated(total[:, h * HS : (h + 1) * HS], kv_cosine[...], kv_sine[...]).reshape(
            4, OFF, HS
        )
    pltpu.make_async_copy(kv.at[t // 2], kv_out.at[t], krecv.at[t]).start()
    for d in range(1, N_TP):
        kv_push(d).start()
    for g in range(2):
        for j in range(4 * g, 4 * g + 4):
            load(j).wait()
        total = product(g * 4 * HS, 4 * HS)
        for h in range(4):
            query[4 * g + h] = rotated(
                total[:, h * HS : (h + 1) * HS], cosine[...], sine[...]
            ).reshape(4, OFF, HS)
    for d in range(N_TP):
        for k in range(2):
            if d == 0:

                @pl.when(core == k)
                def _():
                    pltpu.make_async_copy(
                        query.at[t, :, pl.ds(k * HALF, HALF), :], query_out.at[core, t],
                        qrecv.at[core, t],
                    ).start()

                @pl.when(core != k)
                def _():
                    q_push(0, k).start()

            else:
                q_push(d, k).start()
    for j in range(N_TP):
        push(kv.at[0], kv_out.at[j], ksend.at[0], krecv.at[j], c, t).wait_recv()
        for k in range(2):
            push(
                query_out.at[k, j], query_out.at[k, j], qsend.at[0, 0], qrecv.at[k, j], c, t
            ).wait_recv()
    for d in range(N_TP):
        if d > 0:
            kv_push(d).wait_send()
        for k in range(2):
            if d == 0:

                @pl.when(core != k)
                def _():
                    q_push(0, k).wait_send()

            else:
                q_push(d, k).wait_send()


def qkv_exchange(normed, query_weight, key_weight, value_weight, tables):
    width = key_weight.shape[0]
    vm = pl.BlockSpec(memory_space=pltpu.VMEM)
    anywhere = pl.BlockSpec(memory_space=pl.ANY)
    return pl.pallas_call(
        qkv_kernel,
        out_shape=(
            jax.ShapeDtypeStruct((2, N_TP, 4, HALF, HS), jnp.bfloat16),
            jax.ShapeDtypeStruct((N_TP, 4, OFF, HS), jnp.bfloat16),
        ),
        in_specs=[vm, anywhere, anywhere, anywhere, vm, vm, vm, vm],
        out_specs=(vm, vm),
        scratch_shapes=[
            pltpu.VMEM((width, (N_TP + KVH) * HS), jnp.bfloat16),
            pltpu.VMEM((N_TP, 4, OFF, HS), jnp.bfloat16),
            pltpu.VMEM((KVH, 4, OFF, HS), jnp.bfloat16),
            pltpu.SemaphoreType.DMA((N_TP + 1,)),
            pltpu.SemaphoreType.DMA((N_TP, 2)),
            pltpu.SemaphoreType.DMA((2, N_TP)),
            pltpu.SemaphoreType.DMA((N_TP,)),
            pltpu.SemaphoreType.DMA((N_TP,)),
        ],
        compiler_params=pltpu.CompilerParams(
            collective_id=2, has_side_effects=True, vmem_limit_bytes=40 * 2**20
        ),
        name="qkv",
    )(normed, query_weight, key_weight, value_weight, *tables)


def attention_kernel(slot_of, offset, query, kv, out):
    scale = LOG2E / math.sqrt(HS)
    first = offset[0]

    def chunk(i, unused):
        q = jnp.concatenate(
            [query[:, slot_of[4 * i + a]].reshape(2 * HALF, HS) for a in range(4)], axis=0
        )

        def keys_of(j, which):
            return jnp.concatenate(
                [kv[:, which, slot_of[4 * j + a]].reshape(CH, HS) for a in range(4)], axis=0
            )

        def scores_of(j):
            return lax.dot_general(
                q, keys_of(j, 0), (((1,), (1,)), ((), ())), preferred_element_type=jnp.float32
            )

        def update(state, s, j):
            largest_old, total_old, summed_old = state
            largest = jnp.maximum(largest_old, jnp.max(s, axis=1, keepdims=True))
            weights = jnp.exp2((s - largest) * scale)
            factor = jnp.exp2((largest_old - largest) * scale)
            total = total_old * factor + jnp.sum(weights, axis=1, keepdims=True)
            summed = summed_old * factor + jnp.dot(
                weights.astype(jnp.bfloat16), keys_of(j, 1), preferred_element_type=jnp.float32
            )
            return largest, total, summed

        rows = 8 * HALF
        initial = (
            jnp.full((rows, 1), -1e30, jnp.float32),
            jnp.zeros((rows, 1), jnp.float32),
            jnp.zeros((rows, HS), jnp.float32),
        )
        s = scores_of(i)
        row = lax.broadcasted_iota(jnp.int32, (rows, 1), 0)
        limit = row // (2 * HALF) * CH + first + row % HALF
        col = lax.broadcasted_iota(jnp.int32, s.shape, 1)
        s = jnp.where(col <= limit, s, -1e30)
        state = update(initial, s, i)
        state = lax.fori_loop(0, i, lambda j, st: update(st, scores_of(j), j), state)
        attended = (state[2] / state[1]).astype(jnp.bfloat16).reshape(4, 2, HALF, HS)
        for a in range(4):
            out[slot_of[4 * i + a]] = jnp.concatenate([attended[a, 0], attended[a, 1]], axis=1)
        return unused

    lax.fori_loop(0, 8, chunk, 0)


def attention(slot_of, offset, query, kv):
    vm = pl.BlockSpec(memory_space=pltpu.VMEM)
    sm = pl.BlockSpec(memory_space=pltpu.SMEM)
    return pl.pallas_call(
        attention_kernel,
        out_shape=jax.ShapeDtypeStruct((32, HALF, 2 * HS), jnp.bfloat16),
        in_specs=[sm, sm, vm, vm],
        out_specs=vm,
        compiler_params=pltpu.CompilerParams(vmem_limit_bytes=48 * 2**20),
        name="attention",
    )(slot_of, offset, query, kv)


def out_kernel(
    attended, out_weight, rows, out, heads, weight, result,
    wsem, hsend, hrecv, fsend, frecv, rsend, rrecv,
):
    c = lax.axis_index("ctx")
    t = lax.axis_index("tp")
    pair = c // 2
    core = c % 2
    sibling = pair * 2 + 1 - core
    side = t // 4
    parts = out_weight.shape[1]

    def load(g):
        return pltpu.make_async_copy(out_weight.at[g], weight.at[g], wsem.at[g])

    for g in range(N_TP):
        load(g).start()

    barrier = pltpu.get_barrier_semaphore()
    signal(barrier, sibling, t)
    for d in range(1, N_TP):
        signal(barrier, c, lax.rem(t + d, N_TP))
    home = jnp.logical_and(t == pair, side == core)
    for d in range(PAIRS):
        e = lax.rem(pair + d, PAIRS)
        if d == 0:

            @pl.when(jnp.logical_not(home))
            def _():
                signal(barrier, 2 * e + side, pair)

        else:
            signal(barrier, 2 * e + side, pair)
    pl.semaphore_wait(barrier, 1 + N_TP - 1 + 2 * parts - jnp.where(home, 1, 0))

    mine = pl.ds(core * HALF, HALF)
    theirs = pl.ds((1 - core) * HALF, HALF)

    def gather(d):
        j = lax.rem(t + d, N_TP)
        return push(
            attended.at[pl.ds(4 * j, 4)], heads.at[t, :, mine, :], hsend.at[d], hrecv.at[t], c, j
        )

    pltpu.make_async_copy(
        attended.at[pl.ds(4 * t, 4)], heads.at[t, :, mine, :], hrecv.at[t]
    ).start()
    for d in range(1, N_TP):
        gather(d).start()

    def forward(j):
        return push(
            heads.at[j, :, mine, :], heads.at[j, :, mine, :], fsend.at[j], frecv.at[j], sibling, t
        )

    for d in range(N_TP):
        j = lax.rem(t + N_TP - d, N_TP)
        push(
            heads.at[j, :, mine, :], heads.at[j, :, mine, :], hsend.at[0], hrecv.at[j], sibling, t
        ).wait_recv()
        forward(j).start()
    for j in range(N_TP):
        push(
            heads.at[j, :, theirs, :], heads.at[j, :, theirs, :], fsend.at[j], frecv.at[j],
            sibling, t,
        ).wait_recv()
    for g in range(N_TP):
        load(g).wait()

    part = out.shape[-1]

    def send_home(j, a):
        return push(
            result.at[j, a], out.at[:, pl.ds(OFF * pair, OFF), :], rsend.at[j, a], rrecv.at[pair],
            2 * t + a, parts * core + j,
        )

    def is_home(j, a):
        return jnp.logical_and(home, jnp.logical_and(a == core, parts * core + j == t))

    for j in range(parts):
        total = jnp.zeros((4 * OFF, part), jnp.float32)
        for g in range(N_TP):
            x = heads[g].reshape(4 * OFF, 2 * HS)
            total = total + jnp.dot(
                x, weight[g, j], preferred_element_type=jnp.float32
            ).astype(jnp.bfloat16).astype(jnp.float32)
        for a in range(2):
            placed = rows[a, parts * core + j].reshape(2 * OFF, part).astype(jnp.float32)
            result[j, a] = (placed + total[a * 2 * OFF : (a + 1) * 2 * OFF]).astype(
                jnp.bfloat16
            ).reshape(2, OFF, part)

            @pl.when(is_home(j, a))
            def _():
                pltpu.make_async_copy(
                    result.at[j, a], out.at[:, pl.ds(OFF * pair, OFF), :], rrecv.at[pair]
                ).start()

            @pl.when(jnp.logical_not(is_home(j, a)))
            def _():
                send_home(j, a).start()

    for e in range(PAIRS):
        push(
            result.at[0, 0], out.at[:, pl.ds(OFF * e, OFF), :], rsend.at[0, 0], rrecv.at[e],
            sibling, t,
        ).wait_recv()
    for d in range(1, N_TP):
        gather(d).wait_send()
    for j in range(N_TP):
        forward(j).wait_send()
    for j in range(parts):
        for a in range(2):

            @pl.when(jnp.logical_not(is_home(j, a)))
            def _():
                send_home(j, a).wait_send()


def out_exchange(attended, out_weight, rows):
    part = rows.shape[-1]
    parts = out_weight.shape[1]
    vm = pl.BlockSpec(memory_space=pltpu.VMEM)
    anywhere = pl.BlockSpec(memory_space=pl.ANY)
    return pl.pallas_call(
        out_kernel,
        out_shape=jax.ShapeDtypeStruct((2, CH, part), jnp.bfloat16),
        in_specs=[vm, anywhere, vm],
        out_specs=vm,
        scratch_shapes=[
            pltpu.VMEM((N_TP, 4, OFF, 2 * HS), jnp.bfloat16),
            pltpu.VMEM((N_TP, parts, 2 * HS, part), jnp.bfloat16),
            pltpu.VMEM((parts, 2, 2, OFF, part), jnp.bfloat16),
            pltpu.SemaphoreType.DMA((N_TP,)),
            pltpu.SemaphoreType.DMA((N_TP,)),
            pltpu.SemaphoreType.DMA((N_TP,)),
            pltpu.SemaphoreType.DMA((N_TP,)),
            pltpu.SemaphoreType.DMA((N_TP,)),
            pltpu.SemaphoreType.DMA((parts, 2)),
            pltpu.SemaphoreType.DMA((PAIRS,)),
        ],
        compiler_params=pltpu.CompilerParams(
            collective_id=3, has_side_effects=True, vmem_limit_bytes=40 * 2**20
        ),
        name="out",
    )(attended, out_weight, rows)


def place_frames(text_embed, frame_features, frame_positions, slot_of, projector):
    tok_rows, part = text_embed.shape
    tokens = frame_positions.shape[0]
    spans = jnp.arange(slot_of.shape[0], dtype=jnp.int32)
    slot = jnp.sum(
        jnp.where((frame_positions // CH)[:, None] == spans[None, :], slot_of[None, :], 0), axis=1
    )
    target = slot // 2
    target_row = slot % 2 * CH + frame_positions % CH
    index = jnp.arange(tokens, dtype=jnp.int32)
    earlier = jnp.logical_and(target[None, :] == target[:, None], index[None, :] < index[:, None])
    place = jnp.sum(earlier.astype(jnp.int32), axis=1)
    entry = target * CAP + place
    entries = N_CTX * CAP
    chosen = jnp.arange(entries, dtype=jnp.int32)[:, None] == entry[None, :]
    sorted_features = jnp.dot(
        chosen.astype(jnp.bfloat16), frame_features, preferred_element_type=jnp.float32
    ).astype(jnp.bfloat16)
    row = jnp.sum(jnp.where(chosen, target_row[None, :] + 1, 0), axis=1) - 1
    projected = jax.nn.gelu(
        jnp.dot(sorted_features, projector, preferred_element_type=jnp.float32), approximate=False
    ).astype(jnp.bfloat16)
    outgoing = jnp.transpose(
        projected.reshape(N_CTX, CAP, N_TP, part), (0, 2, 1, 3)
    )
    row = row.reshape(N_CTX, 1, CAP, 1)
    high = jnp.broadcast_to(jnp.where(row < 0, -1, row // 32), (N_CTX, N_TP, CAP, 32))
    low = jnp.broadcast_to(jnp.where(row < 0, 0, row % 32), (N_CTX, N_TP, CAP, 32))
    outgoing = jnp.concatenate(
        [outgoing, high.astype(jnp.bfloat16), low.astype(jnp.bfloat16)], axis=3
    )
    arrived = lax.all_to_all(
        outgoing.reshape(N_CTX * N_TP, CAP, part + 64),
        ("ctx", "tp"),
        split_axis=0,
        concat_axis=0,
        tiled=True,
    ).reshape(N_CTX * N_TP * CAP, part + 64)
    at = (
        arrived[:, part].astype(jnp.float32) * 32.0 + arrived[:, part + 32].astype(jnp.float32)
    ).astype(jnp.int32)
    hit = jnp.arange(tok_rows, dtype=jnp.int32)[:, None] == at[None, :]
    inserted = jnp.dot(
        hit.astype(jnp.bfloat16), arrived[:, :part], preferred_element_type=jnp.float32
    ).astype(jnp.bfloat16)
    return jnp.where(jnp.any(hit, axis=1)[:, None], inserted, text_embed)


def per_device(
    text_embed,
    frame_features,
    frame_positions,
    span_order,
    projector,
    norm_gain,
    query_weight,
    key_weight,
    value_weight,
    out_weight,
):
    tok_rows, part = text_embed.shape
    c = lax.axis_index("ctx")
    t = lax.axis_index("tp")
    pair = c // 2
    core = c % 2
    q_half = lax.all_gather(lax.dynamic_slice_in_dim(query_weight, core * HS, HS, 1), "tp")
    out_cols = out_weight.shape[1] // 2
    out_half = jnp.transpose(
        lax.dynamic_slice_in_dim(out_weight, core * out_cols, out_cols, 1).reshape(
            2 * HS, N_TP // 2, part
        ),
        (1, 0, 2),
    )
    out_half = lax.all_gather(out_half, "tp")

    slots = span_order.shape[0]
    index = jnp.arange(slots, dtype=jnp.int32)
    slot_of = jnp.sum(
        jnp.where(span_order[None, :] == index[:, None], index[None, :], 0), axis=1
    )
    placed = place_frames(text_embed, frame_features, frame_positions, slot_of, projector)
    gain = jnp.broadcast_to(norm_gain[None, :], (16, part))
    rows, normed = rows_exchange(placed.reshape(2, PAIRS, OFF, part), gain)

    spans = lax.dynamic_slice_in_dim(span_order, 4 * t, 4, 0)
    positions = (
        spans[:, None] * CH + OFF * pair + jnp.arange(OFF, dtype=jnp.int32)[None, :]
    ).reshape(-1)
    half = HS // 2
    freqs = 1000000.0 ** (-(jnp.arange(half, dtype=jnp.float32) * 2.0 / HS))
    angles = positions.astype(jnp.float32)[:, None] * freqs[None, :]
    cos = jnp.cos(angles)
    sin = jnp.sin(angles)
    cosine = jnp.concatenate([cos, cos], axis=1)
    sine = jnp.concatenate([-sin, sin], axis=1)
    kv_cosine = jnp.where(core == 0, cosine, 1.0)
    kv_sine = jnp.where(core == 0, sine, 0.0)
    query, kv = qkv_exchange(
        normed, q_half, key_weight, value_weight, (cosine, sine, kv_cosine, kv_sine)
    )
    kv_all = lax.all_gather(kv.reshape(32, OFF, HS), "ctx").reshape(PAIRS, 2, 32, OFF, HS)
    attended = attention(
        slot_of, (HALF * c).reshape(1), query.reshape(2, 32, HALF, HS), kv_all
    )
    mixed = out_exchange(attended, out_half, rows)
    return mixed.reshape(tok_rows, part)


def solution(mesh):
    in_specs = (
        P("ctx", "tp"),
        P(("ctx", "tp"), None),
        P(("ctx", "tp")),
        P(),
        P(),
        P("tp"),
        P(None, "tp"),
        P(),
        P(),
        P("tp", None),
    )
    out_specs = P("ctx", "tp")
    return jax.shard_map(
        per_device, mesh=mesh, in_specs=in_specs, out_specs=out_specs, check_vma=False
    )
```

```python
import functools
import math

import jax
import jax.numpy as jnp
from jax import lax
from jax.experimental import pallas as pl
from jax.experimental.pallas import tpu as pltpu
from jax.sharding import PartitionSpec as P

HS = 128
KVH = 4
CAP = 8
CH = 512
N_CTX = 16
N_TP = 8
PAIRS = 8
OFF = 64
HALF = 32
MESH = pl.DeviceIdType.MESH
LOG2E = math.log2(math.e)


def signal(sem, ctx, tp):
    pl.semaphore_signal(sem, inc=1, device_id=(ctx, tp), device_id_type=MESH)


def push(src, dst, send_sem, recv_sem, ctx, tp):
    return pltpu.make_async_remote_copy(
        src_ref=src, dst_ref=dst, send_sem=send_sem, recv_sem=recv_sem,
        device_id=(ctx, tp), device_id_type=MESH,
    )


def rows_kernel(placed, gain, rows, normed, gains, send, recv, fsend, frecv, gsend, grecv):
    c = lax.axis_index("ctx")
    t = lax.axis_index("tp")
    core = c % 2
    sibling = c + 1 - 2 * core
    barrier = pltpu.get_barrier_semaphore()
    signal(barrier, sibling, t)
    for d in range(1, N_TP):
        signal(barrier, c, lax.rem(t + d, N_TP))
    pl.semaphore_wait(barrier, N_TP)

    def block(d):
        j = lax.rem(t + d, N_TP)
        return push(placed.at[:, j], rows.at[core, t], send.at[d], recv.at[t], c, j)

    def gain_block(d):
        j = lax.rem(t + d, N_TP)
        return push(gain, gains.at[t], gsend.at[d], grecv.at[t], c, j)

    pltpu.make_async_copy(placed.at[:, t], rows.at[core, t], recv.at[t]).start()
    pltpu.make_async_copy(gain, gains.at[t], grecv.at[t]).start()
    for d in range(1, N_TP):
        block(d).start()
        gain_block(d).start()

    def forward(j):
        return push(rows.at[core, j], rows.at[core, j], fsend.at[j], frecv.at[j], sibling, t)

    for d in range(N_TP):
        j = lax.rem(t + d, N_TP)
        push(rows.at[core, j], rows.at[core, j], send.at[0], recv.at[j], sibling, t).wait_recv()
        forward(j).start()
    for j in range(N_TP):
        push(gain, gains.at[j], gsend.at[0], grecv.at[j], sibling, t).wait_recv()

    def receive(j):
        push(
            rows.at[1 - core, j], rows.at[1 - core, j], fsend.at[j], frecv.at[j], sibling, t
        ).wait_recv()

    width = N_TP * placed.shape[-1]

    def normalise(a):
        total = jnp.zeros((2 * OFF, 1), jnp.float32)
        for j in range(N_TP):
            x = rows[a, j].reshape(2 * OFF, -1).astype(jnp.float32)
            total = total + jnp.sum(x * x, axis=1, keepdims=True)
        inverse = lax.rsqrt(total / width + 1e-06)
        for j in range(N_TP):
            x = rows[a, j].reshape(2 * OFF, -1).astype(jnp.float32)
            g = gains[j, 0:1, :].astype(jnp.float32)
            normed[j, a] = (x * inverse * g).astype(jnp.bfloat16)

    normalise(core)
    for j in range(N_TP):
        receive(j)
    normalise(1 - core)

    for d in range(1, PAIRS):
        block(d).wait_send()
        gain_block(d).wait_send()
    for j in range(N_TP):
        forward(j).wait_send()


def rows_exchange(placed, gain):
    part = placed.shape[-1]
    vm = pl.BlockSpec(memory_space=pltpu.VMEM)
    return pl.pallas_call(
        rows_kernel,
        out_shape=(
            jax.ShapeDtypeStruct((2, N_TP, 2, OFF, part), jnp.bfloat16),
            jax.ShapeDtypeStruct((N_TP, 2, 2 * OFF, part), jnp.bfloat16),
        ),
        in_specs=[vm, vm],
        out_specs=(vm, vm),
        scratch_shapes=[
            pltpu.VMEM((N_TP, 16, part), jnp.bfloat16),
            pltpu.SemaphoreType.DMA((PAIRS,)),
            pltpu.SemaphoreType.DMA((N_TP,)),
            pltpu.SemaphoreType.DMA((N_TP,)),
            pltpu.SemaphoreType.DMA((N_TP,)),
            pltpu.SemaphoreType.DMA((PAIRS,)),
            pltpu.SemaphoreType.DMA((N_TP,)),
        ],
        compiler_params=pltpu.CompilerParams(
            collective_id=1, has_side_effects=True, vmem_limit_bytes=24 * 2**20
        ),
        name="rows",
    )(placed, gain)


def qkv_kernel(
    normed, query_weight, key_weight, value_weight, cosine, sine, kv_cosine, kv_sine,
    query_out, kv_out, weight, query, kv, wsem, qsend, qrecv, ksend, krecv,
):
    c = lax.axis_index("ctx")
    t = lax.axis_index("tp")
    pair = c // 2
    core = c % 2
    q_cols = N_TP * HS
    kv_cols = KVH * HS

    def load(j):
        return pltpu.make_async_copy(
            query_weight.at[j], weight.at[:, pl.ds(j * HS, HS)], wsem.at[j]
        )

    kv_slot = weight.at[:, pl.ds(q_cols, kv_cols)]

    @pl.when(core == 0)
    def _():
        pltpu.make_async_copy(key_weight, kv_slot, wsem.at[N_TP]).start()

    @pl.when(core == 1)
    def _():
        pltpu.make_async_copy(value_weight, kv_slot, wsem.at[N_TP]).start()

    for j in range(N_TP):
        load(j).start()

    own = t == pair
    barrier = pltpu.get_barrier_semaphore()
    for k in range(2):
        for d in range(PAIRS):
            e = lax.rem(pair + d, PAIRS)
            if d == 0:

                @pl.when(jnp.logical_not(jnp.logical_and(own, core == k)))
                def _():
                    signal(barrier, 2 * e + k, pair)

            else:
                signal(barrier, 2 * e + k, pair)
    pl.semaphore_wait(barrier, 2 * N_TP - jnp.where(own, 1, 0))

    part = normed.shape[-1]

    def product(start, cols):
        total = jnp.zeros((4 * OFF, cols), jnp.float32)
        for j in range(N_TP):
            x = normed[j].reshape(4 * OFF, part)
            total = total + jnp.dot(
                x, weight[j * part : (j + 1) * part, start : start + cols],
                preferred_element_type=jnp.float32,
            )
        return total

    def rotated(x, cos, sin):
        return (x * cos + pltpu.roll(x, HS // 2, 1) * sin).astype(jnp.bfloat16)

    def kv_push(d):
        j = lax.rem(t + d, N_TP)
        return push(kv.at[j // 2], kv_out.at[pair], ksend.at[d], krecv.at[pair], 2 * t + core, j)

    def q_push(d, k):
        j = lax.rem(t + d, N_TP)
        return push(
            query.at[j, :, pl.ds(k * HALF, HALF), :], query_out.at[core, pair],
            qsend.at[d, k], qrecv.at[core, pair], 2 * t + k, j,
        )

    pltpu.make_async_copy(key_weight, kv_slot, wsem.at[N_TP]).wait()
    total = product(q_cols, kv_cols)
    for h in range(KVH):
        kv[h] = rotated(total[:, h * HS : (h + 1) * HS], kv_cosine[...], kv_sine[...]).reshape(
            4, OFF, HS
        )

    @pl.when(own)
    def _():
        pltpu.make_async_copy(kv.at[t // 2], kv_out.at[pair], krecv.at[pair]).start()

    @pl.when(jnp.logical_not(own))
    def _():
        kv_push(0).start()

    for d in range(1, N_TP):
        kv_push(d).start()
    for g in range(2):
        for j in range(4 * g, 4 * g + 4):
            load(j).wait()
        total = product(g * 4 * HS, 4 * HS)
        for h in range(4):
            query[4 * g + h] = rotated(
                total[:, h * HS : (h + 1) * HS], cosine[...], sine[...]
            ).reshape(4, OFF, HS)
    for d in range(N_TP):
        for k in range(2):
            if d == 0:
                here = jnp.logical_and(own, core == k)

                @pl.when(here)
                def _():
                    pltpu.make_async_copy(
                        query.at[t, :, pl.ds(k * HALF, HALF), :], query_out.at[core, pair],
                        qrecv.at[core, pair],
                    ).start()

                @pl.when(jnp.logical_not(here))
                def _():
                    q_push(0, k).start()

            else:
                q_push(d, k).start()
    for e in range(PAIRS):
        push(kv.at[0], kv_out.at[e], ksend.at[0], krecv.at[e], c, t).wait_recv()
        for k in range(2):
            push(
                query_out.at[k, e], query_out.at[k, e], qsend.at[0, 0], qrecv.at[k, e], c, t
            ).wait_recv()
    for d in range(N_TP):
        if d == 0:

            @pl.when(jnp.logical_not(own))
            def _():
                kv_push(0).wait_send()

        else:
            kv_push(d).wait_send()
        for k in range(2):
            if d == 0:

                @pl.when(jnp.logical_not(jnp.logical_and(own, core == k)))
                def _():
                    q_push(0, k).wait_send()

            else:
                q_push(d, k).wait_send()


def qkv_exchange(normed, query_weight, key_weight, value_weight, tables):
    width = key_weight.shape[0]
    vm = pl.BlockSpec(memory_space=pltpu.VMEM)
    anywhere = pl.BlockSpec(memory_space=pl.ANY)
    return pl.pallas_call(
        qkv_kernel,
        out_shape=(
            jax.ShapeDtypeStruct((2, N_TP, 4, HALF, HS), jnp.bfloat16),
            jax.ShapeDtypeStruct((N_TP, 4, OFF, HS), jnp.bfloat16),
        ),
        in_specs=[vm, anywhere, anywhere, anywhere, vm, vm, vm, vm],
        out_specs=(vm, vm),
        scratch_shapes=[
            pltpu.VMEM((width, (N_TP + KVH) * HS), jnp.bfloat16),
            pltpu.VMEM((N_TP, 4, OFF, HS), jnp.bfloat16),
            pltpu.VMEM((KVH, 4, OFF, HS), jnp.bfloat16),
            pltpu.SemaphoreType.DMA((N_TP + 1,)),
            pltpu.SemaphoreType.DMA((N_TP, 2)),
            pltpu.SemaphoreType.DMA((2, N_TP)),
            pltpu.SemaphoreType.DMA((N_TP,)),
            pltpu.SemaphoreType.DMA((N_TP,)),
        ],
        compiler_params=pltpu.CompilerParams(
            collective_id=2, has_side_effects=True, vmem_limit_bytes=40 * 2**20
        ),
        name="qkv",
    )(normed, query_weight, key_weight, value_weight, *tables)


def attention_kernel(
    slot_of, query, kv_own, out, kv, q, summed, largest, total, send, recv, pass_send,
):
    scale = LOG2E / math.sqrt(HS)
    c = lax.axis_index("ctx")
    t = lax.axis_index("tp")
    pair = c // 2
    core = c % 2
    sibling = c + 1 - 2 * core
    base = pair // 4 * 4
    other = 4 - base
    z = pair % 4
    up = lax.rem(z + 1, 4)
    down = lax.rem(z + 3, 4)
    far = lax.rem(z + 2, 4)
    z_up, z_down, z_far = base + up, base + down, base + far
    x_own, x_up, x_down, x_far = other + z, other + up, other + down, other + far

    barrier = pltpu.get_barrier_semaphore()
    signal(barrier, sibling, t)
    for e in (z_up, z_down, z_far, x_own):
        signal(barrier, 2 * e + core, t)
    for j in range(32):
        kv[pair, core, j * OFF : (j + 1) * OFF] = kv_own[slot_of[j]]
    pl.semaphore_wait(barrier, 5)

    def transfer(e, to, index):
        block = kv.at[e, core]
        return push(block, block, send.at[index], recv.at[e, core], 2 * to + core, t)

    def share(e):
        block = kv.at[e, core]
        return push(block, block, pass_send.at[e], recv.at[e, core], sibling, t)

    def arrive(e, which):
        block = kv.at[e, which]
        push(block, block, send.at[0], recv.at[e, which], sibling, t).wait_recv()

    share(pair).start()
    moves = (
        (pair, x_own), (pair, z_up), (pair, z_down), (pair, z_far),
        (x_own, z_up), (x_own, z_down), (z_far, x_own),
    )
    for index in range(3):
        transfer(*moves[index], index).start()
    for j in range(32):
        q[j * OFF : (j + 1) * OFF] = query[:, slot_of[j]].reshape(2 * HALF, HS)

    rows = 8 * HALF
    row = lax.broadcasted_iota(jnp.int32, (rows, 1), 0)
    limit = row // OFF * CH + HALF * c + row % HALF
    col = lax.broadcasted_iota(jnp.int32, (1, 4 * OFF), 1)

    def update(e, first):
        at = col // OFF * CH + OFF * e + col % OFF
        for i in range(8):
            here = slice(i * rows, (i + 1) * rows)
            width = 4 * OFF * (i + 1)
            s = lax.dot_general(
                q[here], kv[e, 0, :width], (((1,), (1,)), ((), ())),
                preferred_element_type=jnp.float32,
            )
            edge = jnp.where(at <= limit, s[:, width - 4 * OFF :], -1e30)
            s = edge if i == 0 else jnp.concatenate([s[:, : width - 4 * OFF], edge], axis=1)
            top = jnp.max(s, axis=1, keepdims=True)
            if not first:
                top = jnp.maximum(top, largest[here])
            weights = jnp.exp2((s - top) * scale)
            added = jnp.sum(weights, axis=1, keepdims=True)
            product = jnp.dot(
                weights.astype(jnp.bfloat16), kv[e, 1, :width], preferred_element_type=jnp.float32
            )
            if not first:
                factor = jnp.exp2((largest[here] - top) * scale)
                added = added + total[here] * factor
                product = product + summed[here] * factor
            largest[here] = top
            total[here] = added
            summed[here] = product

    arrive(pair, 1 - core)
    update(pair, True)
    transfer(*moves[3], 3).start()
    arrive(x_own, core)
    transfer(*moves[4], 4).start()
    transfer(*moves[5], 5).start()
    share(x_own).start()
    arrive(z_up, core)
    share(z_up).start()
    arrive(z_down, core)
    share(z_down).start()

    order = (x_own, z_up, z_down, x_up, x_down, z_far, x_far)

    def step(n, unused):
        e = order[6]
        for index in range(6):
            e = jnp.where(n == index, order[index], e)

        @pl.when(n == 2)
        def _():
            arrive(x_up, core)
            share(x_up).start()

        @pl.when(n == 3)
        def _():
            arrive(x_down, core)
            share(x_down).start()
            arrive(z_far, core)
            transfer(*moves[6], 6).start()
            share(z_far).start()

        @pl.when(n == 6)
        def _():
            arrive(x_far, core)
            share(x_far).start()

        arrive(e, 1 - core)
        update(e, False)
        return unused

    lax.fori_loop(0, 7, step, 0)
    for i in range(8):
        here = slice(i * rows, (i + 1) * rows)
        attended = (summed[here] / total[here]).astype(jnp.bfloat16).reshape(4, 2, HALF, HS)
        for a in range(4):
            out[4 * i + a] = jnp.concatenate([attended[a, 0], attended[a, 1]], axis=1)
    for index in range(7):
        transfer(*moves[index], index).wait_send()
    for e in range(PAIRS):
        share(e).wait_send()


def attention(slot_of, query, kv):
    vm = pl.BlockSpec(memory_space=pltpu.VMEM)
    sm = pl.BlockSpec(memory_space=pltpu.SMEM)
    keys = 32 * OFF
    return pl.pallas_call(
        attention_kernel,
        out_shape=jax.ShapeDtypeStruct((32, HALF, 2 * HS), jnp.bfloat16),
        in_specs=[sm, vm, vm],
        out_specs=vm,
        scratch_shapes=[
            pltpu.VMEM((PAIRS, 2, keys, HS), jnp.bfloat16),
            pltpu.VMEM((keys, HS), jnp.bfloat16),
            pltpu.VMEM((keys, HS), jnp.float32),
            pltpu.VMEM((keys, 1), jnp.float32),
            pltpu.VMEM((keys, 1), jnp.float32),
            pltpu.SemaphoreType.DMA((7,)),
            pltpu.SemaphoreType.DMA((PAIRS, 2)),
            pltpu.SemaphoreType.DMA((PAIRS,)),
        ],
        compiler_params=pltpu.CompilerParams(
            collective_id=4, has_side_effects=True, vmem_limit_bytes=48 * 2**20
        ),
        name="attention",
    )(slot_of, query, kv)


def out_kernel(
    span_order, attended, out_weight, rows, out, sorted_heads, heads, weight, result,
    wsem, hsend, hrecv, fsend, frecv, rsend, rrecv,
):
    c = lax.axis_index("ctx")
    t = lax.axis_index("tp")
    pair = c // 2
    core = c % 2
    sibling = c + 1 - 2 * core
    side = t // 4
    parts = out_weight.shape[1]

    def load(g):
        return pltpu.make_async_copy(out_weight.at[g], weight.at[g], wsem.at[g])

    for g in range(N_TP):
        load(g).start()

    own = t == pair
    home = side == core
    barrier = pltpu.get_barrier_semaphore()
    signal(barrier, sibling, t)
    for d in range(N_TP):
        j = lax.rem(t + d, N_TP)
        if d == 0:

            @pl.when(jnp.logical_not(own))
            def _():
                signal(barrier, 2 * t + core, j)

            @pl.when(jnp.logical_not(home))
            def _():
                signal(barrier, 2 * pair + side, j)

        else:
            signal(barrier, 2 * t + core, j)
            signal(barrier, 2 * pair + side, j)
    for j in range(32):
        sorted_heads[j] = attended[span_order[j]]
    pl.semaphore_wait(
        barrier, 1 + PAIRS - jnp.where(own, 1, 0) + 2 * parts - jnp.where(home, 1, 0)
    )

    mine = pl.ds(core * HALF, HALF)
    theirs = pl.ds((1 - core) * HALF, HALF)

    def gather(d):
        e = lax.rem(pair + d, PAIRS)
        return push(
            sorted_heads.at[pl.ds(4 * e, 4)], heads.at[t, :, mine, :], hsend.at[d], hrecv.at[t],
            2 * e + core, pair,
        )

    @pl.when(own)
    def _():
        pltpu.make_async_copy(
            sorted_heads.at[pl.ds(4 * pair, 4)], heads.at[t, :, mine, :], hrecv.at[t]
        ).start()

    @pl.when(jnp.logical_not(own))
    def _():
        gather(0).start()

    for d in range(1, PAIRS):
        gather(d).start()

    def forward(j):
        return push(
            heads.at[j, :, mine, :], heads.at[j, :, mine, :], fsend.at[j], frecv.at[j], sibling, t
        )

    for d in range(N_TP):
        j = lax.rem(t + d, N_TP)
        push(
            heads.at[j, :, mine, :], heads.at[j, :, mine, :], hsend.at[0], hrecv.at[j], sibling, t
        ).wait_recv()
        forward(j).start()
    for j in range(N_TP):
        push(
            heads.at[j, :, theirs, :], heads.at[j, :, theirs, :], fsend.at[j], frecv.at[j],
            sibling, t,
        ).wait_recv()
    for g in range(N_TP):
        load(g).wait()

    part = out.shape[-1]

    def send_home(j, a):
        return push(
            result.at[j, a], out.at[:, pl.ds(OFF * t, OFF), :], rsend.at[j, a], rrecv.at[t],
            2 * pair + a, parts * core + j,
        )

    def is_home(j, a):
        return jnp.logical_and(home, jnp.logical_and(a == core, parts * core + j == t))

    for j in range(parts):
        total = jnp.zeros((4 * OFF, part), jnp.float32)
        for g in range(N_TP):
            x = heads[g].reshape(4 * OFF, 2 * HS)
            total = total + jnp.dot(
                x, weight[g, j], preferred_element_type=jnp.float32
            ).astype(jnp.bfloat16).astype(jnp.float32)
        for a in range(2):
            placed = rows[a, parts * core + j].reshape(2 * OFF, part).astype(jnp.float32)
            result[j, a] = (placed + total[a * 2 * OFF : (a + 1) * 2 * OFF]).astype(
                jnp.bfloat16
            ).reshape(2, OFF, part)

            @pl.when(is_home(j, a))
            def _():
                pltpu.make_async_copy(
                    result.at[j, a], out.at[:, pl.ds(OFF * t, OFF), :], rrecv.at[t]
                ).start()

            @pl.when(jnp.logical_not(is_home(j, a)))
            def _():
                send_home(j, a).start()

    for e in range(PAIRS):
        push(
            result.at[0, 0], out.at[:, pl.ds(OFF * e, OFF), :], rsend.at[0, 0], rrecv.at[e],
            sibling, t,
        ).wait_recv()

    @pl.when(jnp.logical_not(own))
    def _():
        gather(0).wait_send()

    for d in range(1, PAIRS):
        gather(d).wait_send()
    for j in range(N_TP):
        forward(j).wait_send()
    for j in range(parts):
        for a in range(2):

            @pl.when(jnp.logical_not(is_home(j, a)))
            def _():
                send_home(j, a).wait_send()


def out_exchange(span_order, attended, out_weight, rows):
    part = rows.shape[-1]
    parts = out_weight.shape[1]
    vm = pl.BlockSpec(memory_space=pltpu.VMEM)
    anywhere = pl.BlockSpec(memory_space=pl.ANY)
    return pl.pallas_call(
        out_kernel,
        out_shape=jax.ShapeDtypeStruct((2, CH, part), jnp.bfloat16),
        in_specs=[pl.BlockSpec(memory_space=pltpu.SMEM), vm, anywhere, vm],
        out_specs=vm,
        scratch_shapes=[
            pltpu.VMEM((32, HALF, 2 * HS), jnp.bfloat16),
            pltpu.VMEM((N_TP, 4, OFF, 2 * HS), jnp.bfloat16),
            pltpu.VMEM((N_TP, parts, 2 * HS, part), jnp.bfloat16),
            pltpu.VMEM((parts, 2, 2, OFF, part), jnp.bfloat16),
            pltpu.SemaphoreType.DMA((N_TP,)),
            pltpu.SemaphoreType.DMA((N_TP,)),
            pltpu.SemaphoreType.DMA((N_TP,)),
            pltpu.SemaphoreType.DMA((N_TP,)),
            pltpu.SemaphoreType.DMA((N_TP,)),
            pltpu.SemaphoreType.DMA((parts, 2)),
            pltpu.SemaphoreType.DMA((PAIRS,)),
        ],
        compiler_params=pltpu.CompilerParams(
            collective_id=3, has_side_effects=True, vmem_limit_bytes=40 * 2**20
        ),
        name="out",
    )(span_order, attended, out_weight, rows)


def place_frames(text_embed, frame_features, frame_positions, slot_of, projector):
    tok_rows, part = text_embed.shape
    tokens = frame_positions.shape[0]
    spans = jnp.arange(slot_of.shape[0], dtype=jnp.int32)
    slot = jnp.sum(
        jnp.where((frame_positions // CH)[:, None] == spans[None, :], slot_of[None, :], 0), axis=1
    )
    target = slot // 2
    target_row = slot % 2 * CH + frame_positions % CH
    index = jnp.arange(tokens, dtype=jnp.int32)
    earlier = jnp.logical_and(target[None, :] == target[:, None], index[None, :] < index[:, None])
    place = jnp.sum(earlier.astype(jnp.int32), axis=1)
    entry = target * CAP + place
    entries = N_CTX * CAP
    chosen = jnp.arange(entries, dtype=jnp.int32)[:, None] == entry[None, :]
    sorted_features = jnp.dot(
        chosen.astype(jnp.bfloat16), frame_features, preferred_element_type=jnp.float32
    ).astype(jnp.bfloat16)
    row = jnp.sum(jnp.where(chosen, target_row[None, :] + 1, 0), axis=1) - 1
    projected = jax.nn.gelu(
        jnp.dot(sorted_features, projector, preferred_element_type=jnp.float32), approximate=False
    ).astype(jnp.bfloat16)
    outgoing = jnp.transpose(
        projected.reshape(N_CTX, CAP, N_TP, part), (0, 2, 1, 3)
    )
    row = row.reshape(N_CTX, 1, CAP, 1)
    high = jnp.broadcast_to(jnp.where(row < 0, -1, row // 32), (N_CTX, N_TP, CAP, 32))
    low = jnp.broadcast_to(jnp.where(row < 0, 0, row % 32), (N_CTX, N_TP, CAP, 32))
    outgoing = jnp.concatenate(
        [outgoing, high.astype(jnp.bfloat16), low.astype(jnp.bfloat16)], axis=3
    )
    arrived = lax.all_to_all(
        outgoing.reshape(N_CTX * N_TP, CAP, part + 64),
        ("ctx", "tp"),
        split_axis=0,
        concat_axis=0,
        tiled=True,
    ).reshape(N_CTX * N_TP * CAP, part + 64)
    at = (
        arrived[:, part].astype(jnp.float32) * 32.0 + arrived[:, part + 32].astype(jnp.float32)
    ).astype(jnp.int32)
    hit = jnp.arange(tok_rows, dtype=jnp.int32)[:, None] == at[None, :]
    inserted = jnp.dot(
        hit.astype(jnp.bfloat16), arrived[:, :part], preferred_element_type=jnp.float32
    ).astype(jnp.bfloat16)
    return jnp.where(jnp.any(hit, axis=1)[:, None], inserted, text_embed)


def per_device(
    text_embed,
    frame_features,
    frame_positions,
    span_order,
    projector,
    norm_gain,
    query_weight,
    key_weight,
    value_weight,
    out_weight,
):
    tok_rows, part = text_embed.shape
    c = lax.axis_index("ctx")
    t = lax.axis_index("tp")
    pair = c // 2
    core = c % 2
    q_half = lax.all_gather(lax.dynamic_slice_in_dim(query_weight, core * HS, HS, 1), "tp")
    out_cols = out_weight.shape[1] // 2
    out_half = jnp.transpose(
        lax.dynamic_slice_in_dim(out_weight, core * out_cols, out_cols, 1).reshape(
            2 * HS, N_TP // 2, part
        ),
        (1, 0, 2),
    )
    slots = span_order.shape[0]
    index = jnp.arange(slots, dtype=jnp.int32)
    slot_of = jnp.sum(
        jnp.where(span_order[None, :] == index[:, None], index[None, :], 0), axis=1
    )
    placed = place_frames(text_embed, frame_features, frame_positions, slot_of, projector)
    gain = jnp.broadcast_to(norm_gain[None, :], (16, part))
    rows, normed = rows_exchange(placed.reshape(2, PAIRS, OFF, part), gain)

    spans = lax.dynamic_slice_in_dim(span_order, 4 * pair, 4, 0)
    positions = (
        spans[:, None] * CH + OFF * t + jnp.arange(OFF, dtype=jnp.int32)[None, :]
    ).reshape(-1)
    half = HS // 2
    freqs = 1000000.0 ** (-(jnp.arange(half, dtype=jnp.float32) * 2.0 / HS))
    angles = positions.astype(jnp.float32)[:, None] * freqs[None, :]
    cos = jnp.cos(angles)
    sin = jnp.sin(angles)
    cosine = jnp.concatenate([cos, cos], axis=1)
    sine = jnp.concatenate([-sin, sin], axis=1)
    kv_cosine = jnp.where(core == 0, cosine, 1.0)
    kv_sine = jnp.where(core == 0, sine, 0.0)
    query, kv = qkv_exchange(
        normed, q_half, key_weight, value_weight, (cosine, sine, kv_cosine, kv_sine)
    )
    kv, out_half = lax.optimization_barrier((kv, out_half))
    out_half = lax.all_gather(out_half, "tp")
    attended = attention(
        slot_of, query.reshape(2, 32, HALF, HS), kv.reshape(32, OFF, HS)
    )
    mixed = out_exchange(span_order, attended, out_half, rows)
    return mixed.reshape(tok_rows, part)


def solution(mesh):
    in_specs = (
        P("ctx", "tp"),
        P(("ctx", "tp"), None),
        P(("ctx", "tp")),
        P(),
        P(),
        P("tp"),
        P(None, "tp"),
        P(),
        P(),
        P("tp", None),
    )
    out_specs = P("ctx", "tp")
    return jax.shard_map(
        per_device, mesh=mesh, in_specs=in_specs, out_specs=out_specs, check_vma=False
    )
```

```python
import functools
import math

import jax
import jax.numpy as jnp
from jax import lax
from jax.experimental import pallas as pl
from jax.experimental.pallas import tpu as pltpu
from jax.sharding import PartitionSpec as P

HS = 128
KVH = 4
CAP = 8
CH = 512
N_CTX = 16
N_TP = 8
PAIRS = 8
OFF = 64
HALF = 32
MESH = pl.DeviceIdType.MESH
LOG2E = math.log2(math.e)


def signal(sem, ctx, tp):
    pl.semaphore_signal(sem, inc=1, device_id=(ctx, tp), device_id_type=MESH)


def push(src, dst, send_sem, recv_sem, ctx, tp):
    return pltpu.make_async_remote_copy(
        src_ref=src, dst_ref=dst, send_sem=send_sem, recv_sem=recv_sem,
        device_id=(ctx, tp), device_id_type=MESH,
    )


def add4(a, b):
    return lax.rem(a + b + 4, 4)


def pair_of(e, t):
    return lax.rem(e // 4 + t // 4, 2) * 4 + add4(lax.rem(e, 4), lax.rem(t, 4))


def class_of(e, pair):
    return lax.rem(e // 4 + pair // 4, 2) * 4 + add4(lax.rem(pair, 4), -lax.rem(e, 4))


def rows_kernel(placed, gain, rows, normed, gains, send, recv, fsend, frecv, gsend, grecv):
    c = lax.axis_index("ctx")
    t = lax.axis_index("tp")
    core = c % 2
    sibling = c + 1 - 2 * core
    barrier = pltpu.get_barrier_semaphore()
    signal(barrier, sibling, t)
    for d in range(1, N_TP):
        signal(barrier, c, lax.rem(t + d, N_TP))
    pl.semaphore_wait(barrier, N_TP)

    def block(d):
        j = lax.rem(t + d, N_TP)
        return push(placed.at[:, j], rows.at[core, t], send.at[d], recv.at[t], c, j)

    def gain_block(d):
        j = lax.rem(t + d, N_TP)
        return push(gain, gains.at[t], gsend.at[d], grecv.at[t], c, j)

    pltpu.make_async_copy(placed.at[:, t], rows.at[core, t], recv.at[t]).start()
    pltpu.make_async_copy(gain, gains.at[t], grecv.at[t]).start()
    for d in range(1, N_TP):
        block(d).start()
        gain_block(d).start()

    def forward(j):
        return push(rows.at[core, j], rows.at[core, j], fsend.at[j], frecv.at[j], sibling, t)

    for d in range(N_TP):
        j = lax.rem(t + d, N_TP)
        push(rows.at[core, j], rows.at[core, j], send.at[0], recv.at[j], sibling, t).wait_recv()
        forward(j).start()
    for j in range(N_TP):
        push(gain, gains.at[j], gsend.at[0], grecv.at[j], sibling, t).wait_recv()

    def receive(j):
        push(
            rows.at[1 - core, j], rows.at[1 - core, j], fsend.at[j], frecv.at[j], sibling, t
        ).wait_recv()

    width = N_TP * placed.shape[-1]

    def normalise(a):
        total = jnp.zeros((2 * OFF, 1), jnp.float32)
        for j in range(N_TP):
            x = rows[a, j].reshape(2 * OFF, -1).astype(jnp.float32)
            total = total + jnp.sum(x * x, axis=1, keepdims=True)
        inverse = lax.rsqrt(total / width + 1e-06)
        for j in range(N_TP):
            x = rows[a, j].reshape(2 * OFF, -1).astype(jnp.float32)
            g = gains[j, 0:1, :].astype(jnp.float32)
            normed[j, a] = (x * inverse * g).astype(jnp.bfloat16)

    normalise(core)
    for j in range(N_TP):
        receive(j)
    normalise(1 - core)

    for d in range(1, PAIRS):
        block(d).wait_send()
        gain_block(d).wait_send()
    for j in range(N_TP):
        forward(j).wait_send()


def rows_exchange(placed, gain):
    part = placed.shape[-1]
    vm = pl.BlockSpec(memory_space=pltpu.VMEM)
    return pl.pallas_call(
        rows_kernel,
        out_shape=(
            jax.ShapeDtypeStruct((2, N_TP, 2, OFF, part), jnp.bfloat16),
            jax.ShapeDtypeStruct((N_TP, 2, 2 * OFF, part), jnp.bfloat16),
        ),
        in_specs=[vm, vm],
        out_specs=(vm, vm),
        scratch_shapes=[
            pltpu.VMEM((N_TP, 16, part), jnp.bfloat16),
            pltpu.SemaphoreType.DMA((PAIRS,)),
            pltpu.SemaphoreType.DMA((N_TP,)),
            pltpu.SemaphoreType.DMA((N_TP,)),
            pltpu.SemaphoreType.DMA((N_TP,)),
            pltpu.SemaphoreType.DMA((PAIRS,)),
            pltpu.SemaphoreType.DMA((N_TP,)),
        ],
        compiler_params=pltpu.CompilerParams(
            collective_id=1, has_side_effects=True, vmem_limit_bytes=24 * 2**20
        ),
        name="rows",
    )(placed, gain)


def qkv_kernel(
    normed, query_weight, key_weight, value_weight, cosine, sine, kv_cosine, kv_sine,
    query_out, kv_out, weight, query, kv, wsem, qsend, qrecv, ksend, krecv,
):
    c = lax.axis_index("ctx")
    t = lax.axis_index("tp")
    pair = c // 2
    core = c % 2
    q_cols = N_TP * HS
    kv_cols = KVH * HS

    def load(j):
        return pltpu.make_async_copy(
            query_weight.at[j], weight.at[:, pl.ds(j * HS, HS)], wsem.at[j]
        )

    kv_slot = weight.at[:, pl.ds(q_cols, kv_cols)]

    @pl.when(core == 0)
    def _():
        pltpu.make_async_copy(key_weight, kv_slot, wsem.at[N_TP]).start()

    @pl.when(core == 1)
    def _():
        pltpu.make_async_copy(value_weight, kv_slot, wsem.at[N_TP]).start()

    for j in range(N_TP):
        load(j).start()

    goal = pair_of(pair, t)
    own = t == 0
    barrier = pltpu.get_barrier_semaphore()
    for k in range(2):
        for d in range(PAIRS):
            e = lax.rem(pair + d, PAIRS)
            if d == 0:

                @pl.when(jnp.logical_not(jnp.logical_and(own, core == k)))
                def _():
                    signal(barrier, 2 * e + k, 0)

            else:
                signal(barrier, 2 * e + k, class_of(e, pair))
    pl.semaphore_wait(barrier, 2 * N_TP - jnp.where(own, 1, 0))

    part = normed.shape[-1]

    def product(start, cols):
        total = jnp.zeros((4 * OFF, cols), jnp.float32)
        for j in range(N_TP):
            x = normed[j].reshape(4 * OFF, part)
            total = total + jnp.dot(
                x, weight[j * part : (j + 1) * part, start : start + cols],
                preferred_element_type=jnp.float32,
            )
        return total

    def rotated(x, cos, sin):
        return (x * cos + pltpu.roll(x, HS // 2, 1) * sin).astype(jnp.bfloat16)

    def kv_push(d):
        j = lax.rem(t + d, N_TP)
        return push(kv.at[j // 2], kv_out.at[pair], ksend.at[d], krecv.at[pair], 2 * goal + core, j)

    def q_push(d, k):
        j = lax.rem(t + d, N_TP)
        return push(
            query.at[j, :, pl.ds(k * HALF, HALF), :], query_out.at[core, pair],
            qsend.at[d, k], qrecv.at[core, pair], 2 * goal + k, j,
        )

    pltpu.make_async_copy(key_weight, kv_slot, wsem.at[N_TP]).wait()
    total = product(q_cols, kv_cols)
    for h in range(KVH):
        kv[h] = rotated(total[:, h * HS : (h + 1) * HS], kv_cosine[...], kv_sine[...]).reshape(
            4, OFF, HS
        )

    @pl.when(own)
    def _():
        pltpu.make_async_copy(kv.at[t // 2], kv_out.at[pair], krecv.at[pair]).start()

    @pl.when(jnp.logical_not(own))
    def _():
        kv_push(0).start()

    for d in range(1, N_TP):
        kv_push(d).start()
    for g in range(2):
        for j in range(4 * g, 4 * g + 4):
            load(j).wait()
        total = product(g * 4 * HS, 4 * HS)
        for h in range(4):
            query[4 * g + h] = rotated(
                total[:, h * HS : (h + 1) * HS], cosine[...], sine[...]
            ).reshape(4, OFF, HS)
    for d in range(N_TP):
        for k in range(2):
            if d == 0:
                here = jnp.logical_and(own, core == k)

                @pl.when(here)
                def _():
                    pltpu.make_async_copy(
                        query.at[t, :, pl.ds(k * HALF, HALF), :], query_out.at[core, pair],
                        qrecv.at[core, pair],
                    ).start()

                @pl.when(jnp.logical_not(here))
                def _():
                    q_push(0, k).start()

            else:
                q_push(d, k).start()
    for e in range(PAIRS):
        push(kv.at[0], kv_out.at[e], ksend.at[0], krecv.at[e], c, t).wait_recv()
        for k in range(2):
            push(
                query_out.at[k, e], query_out.at[k, e], qsend.at[0, 0], qrecv.at[k, e], c, t
            ).wait_recv()
    for d in range(N_TP):
        if d == 0:

            @pl.when(jnp.logical_not(own))
            def _():
                kv_push(0).wait_send()

        else:
            kv_push(d).wait_send()
        for k in range(2):
            if d == 0:

                @pl.when(jnp.logical_not(jnp.logical_and(own, core == k)))
                def _():
                    q_push(0, k).wait_send()

            else:
                q_push(d, k).wait_send()


def qkv_exchange(normed, query_weight, key_weight, value_weight, tables):
    width = key_weight.shape[0]
    vm = pl.BlockSpec(memory_space=pltpu.VMEM)
    anywhere = pl.BlockSpec(memory_space=pl.ANY)
    return pl.pallas_call(
        qkv_kernel,
        out_shape=(
            jax.ShapeDtypeStruct((2, N_TP, 4, HALF, HS), jnp.bfloat16),
            jax.ShapeDtypeStruct((N_TP, 4, OFF, HS), jnp.bfloat16),
        ),
        in_specs=[vm, anywhere, anywhere, anywhere, vm, vm, vm, vm],
        out_specs=(vm, vm),
        scratch_shapes=[
            pltpu.VMEM((width, (N_TP + KVH) * HS), jnp.bfloat16),
            pltpu.VMEM((N_TP, 4, OFF, HS), jnp.bfloat16),
            pltpu.VMEM((KVH, 4, OFF, HS), jnp.bfloat16),
            pltpu.SemaphoreType.DMA((N_TP + 1,)),
            pltpu.SemaphoreType.DMA((N_TP, 2)),
            pltpu.SemaphoreType.DMA((2, N_TP)),
            pltpu.SemaphoreType.DMA((N_TP,)),
            pltpu.SemaphoreType.DMA((N_TP,)),
        ],
        compiler_params=pltpu.CompilerParams(
            collective_id=2, has_side_effects=True, vmem_limit_bytes=40 * 2**20
        ),
        name="qkv",
    )(normed, query_weight, key_weight, value_weight, *tables)


def attention_kernel(
    slot_of, query, kv_own, out_weight, out, gathered,
    kv, q, summed, largest, total, limit, send, recv, pass_send, wsend, wrecv, own_sem,
):
    scale = LOG2E / math.sqrt(HS)
    c = lax.axis_index("ctx")
    t = lax.axis_index("tp")
    pair = c // 2
    core = c % 2
    sibling = c + 1 - 2 * core
    base = pair // 4 * 4
    other = 4 - base
    z = pair % 4
    up = lax.rem(z + 1, 4)
    down = lax.rem(z + 3, 4)
    far = lax.rem(z + 2, 4)
    z_up, z_down, z_far = base + up, base + down, base + far
    x_own, x_up, x_down, x_far = other + z, other + up, other + down, other + far

    y = lax.rem(t, 4)
    side = t - y
    across = 4 - side
    t_up, t_down, t_far = (side + add4(y, n) for n in (1, 3, 2))
    a_own, a_up, a_down, a_far = (across + add4(y, n) for n in (0, 1, 3, 2))
    x_next = 2 * x_own + core

    barrier = pltpu.get_barrier_semaphore()
    signal(barrier, sibling, t)
    for e in (z_up, z_down, z_far, x_own):
        signal(barrier, 2 * e + core, t)
    signal(barrier, x_next, a_own)
    for j in (t_up, t_down, t_far):
        signal(barrier, c, j)
    for j in range(32):
        kv[pair, core, j * OFF : (j + 1) * OFF] = kv_own[slot_of[j]]
    pl.semaphore_wait(barrier, 9)

    cols = gathered.shape[-1]
    quarter_rows = gathered.shape[1] // 4
    own_weight = out_weight.at[:, pl.ds(pl.multiple_of(cols * core, HS), cols)]

    def quarter(ref, n):
        return ref.at[pl.ds(quarter_rows * n, quarter_rows)]

    def wmove(m):
        whole = lambda g: (gathered.at[g], gathered.at[g])
        part = lambda g: (quarter(gathered.at[g], z), quarter(gathered.at[g], z))
        src, dst, ctx, tp = (
            (own_weight, gathered.at[t], x_next, a_own),
            (own_weight, gathered.at[t], c, t_up),
            (own_weight, gathered.at[t], c, t_down),
            (quarter(own_weight, z), quarter(gathered.at[t], z), c, t_far),
            (*whole(a_own), c, t_up),
            (*whole(a_own), c, t_down),
            (*part(a_own), c, t_far),
            (*part(t_far), 2 * z_up + core, t),
            (*part(t_far), 2 * z_down + core, t),
            (*part(t_far), 2 * z_far + core, t),
            (*part(a_far), 2 * z_up + core, t),
            (*part(a_far), 2 * z_down + core, t),
            (*part(a_far), 2 * z_far + core, t),
        )[m]
        return push(src, dst, wsend.at[m], wrecv.at[m], ctx, tp)

    def warrive(m):
        ref = (
            gathered.at[a_own], gathered.at[t_down], gathered.at[t_up],
            quarter(gathered.at[t_far], z),
            gathered.at[a_down], gathered.at[a_up], quarter(gathered.at[a_far], z),
            quarter(gathered.at[t_far], down), quarter(gathered.at[t_far], up),
            quarter(gathered.at[t_far], far),
            quarter(gathered.at[a_far], down), quarter(gathered.at[a_far], up),
            quarter(gathered.at[a_far], far),
        )[m]
        push(ref, ref, wsend.at[m], wrecv.at[m], sibling, t).wait_recv()

    def transfer(e, to, index):
        block = kv.at[e, core]
        return push(block, block, send.at[index], recv.at[e, core], 2 * to + core, t)

    def share(e):
        block = kv.at[e, core]
        return push(block, block, pass_send.at[e], recv.at[e, core], sibling, t)

    def arrive(e, which):
        block = kv.at[e, which]
        push(block, block, send.at[0], recv.at[e, which], sibling, t).wait_recv()

    share(pair).start()
    moves = (
        (pair, x_own), (pair, z_up), (pair, z_down), (pair, z_far),
        (x_own, z_up), (x_own, z_down), (z_far, x_own),
    )
    for index in range(3):
        transfer(*moves[index], index).start()
    for m in (0, 3, 1, 2):
        wmove(m).start()
    own_copy = pltpu.make_async_copy(own_weight, gathered.at[t], own_sem)
    own_copy.start()
    for j in range(32):
        q[j * OFF : (j + 1) * OFF] = query[:, slot_of[j]].reshape(2 * HALF, HS)

    rows = 8 * HALF
    row = lax.broadcasted_iota(jnp.int32, (rows, 1), 0)
    col = lax.broadcasted_iota(jnp.int32, (1, 4 * OFF), 1)

    def starts(index, i, e):
        value = jnp.zeros(index.shape, jnp.int32)
        for a in range(4):
            start = a * CH + OFF * class_of(slot_of[4 * i + a] // 4, e)
            value = jnp.where(index // OFF == a, start, value)
        return value

    for i in range(8):
        limit[i * rows : (i + 1) * rows] = (
            starts(row, i, pair) + HALF * core + row % HALF
        )

    def update(e, first):
        for i in range(8):
            at = starts(col, i, e) + col % OFF
            here = slice(i * rows, (i + 1) * rows)
            width = 4 * OFF * (i + 1)
            s = lax.dot_general(
                q[here], kv[e, 0, :width], (((1,), (1,)), ((), ())),
                preferred_element_type=jnp.float32,
            )
            edge = jnp.where(at <= limit[here], s[:, width - 4 * OFF :], -1e30)
            s = edge if i == 0 else jnp.concatenate([s[:, : width - 4 * OFF], edge], axis=1)
            top = jnp.max(s, axis=1, keepdims=True)
            if not first:
                top = jnp.maximum(top, largest[here])
            weights = jnp.exp2((s - top) * scale)
            added = jnp.sum(weights, axis=1, keepdims=True)
            product = jnp.dot(
                weights.astype(jnp.bfloat16), kv[e, 1, :width], preferred_element_type=jnp.float32
            )
            if not first:
                factor = jnp.exp2((largest[here] - top) * scale)
                added = added + total[here] * factor
                product = product + summed[here] * factor
            largest[here] = top
            total[here] = added
            summed[here] = product

    arrive(pair, 1 - core)
    update(pair, True)
    transfer(*moves[3], 3).start()
    arrive(x_own, core)
    transfer(*moves[4], 4).start()
    transfer(*moves[5], 5).start()
    share(x_own).start()
    arrive(z_up, core)
    share(z_up).start()
    arrive(z_down, core)
    share(z_down).start()

    order = (x_own, z_up, z_down, x_up, x_down, z_far, x_far)

    def step(n, unused):
        e = order[6]
        for index in range(6):
            e = jnp.where(n == index, order[index], e)

        @pl.when(n == 2)
        def _():
            warrive(3)
            for m in (7, 8, 9):
                wmove(m).start()
            arrive(x_up, core)
            share(x_up).start()

        @pl.when(n == 3)
        def _():
            arrive(x_down, core)
            share(x_down).start()
            arrive(z_far, core)
            transfer(*moves[6], 6).start()
            share(z_far).start()

        @pl.when(n == 4)
        def _():
            warrive(0)
            for m in (6, 4, 5):
                wmove(m).start()

        @pl.when(n == 6)
        def _():
            arrive(x_far, core)
            share(x_far).start()

        arrive(e, 1 - core)
        update(e, False)
        return unused

    lax.fori_loop(0, 7, step, 0)
    for i in range(8):
        here = slice(i * rows, (i + 1) * rows)
        attended = (summed[here] / total[here]).astype(jnp.bfloat16).reshape(4, 2, HALF, HS)
        for a in range(4):
            out[4 * i + a] = jnp.concatenate([attended[a, 0], attended[a, 1]], axis=1)
    warrive(6)
    for m in (10, 11, 12):
        wmove(m).start()
    for m in (1, 2, 4, 5, 7, 8, 9, 10, 11, 12):
        warrive(m)
    own_copy.wait()
    for index in range(7):
        transfer(*moves[index], index).wait_send()
    for e in range(PAIRS):
        share(e).wait_send()
    for m in range(13):
        wmove(m).wait_send()


def attention(slot_of, query, kv, out_weight):
    anywhere = pl.BlockSpec(memory_space=pl.ANY)
    depth, width = out_weight.shape
    vm = pl.BlockSpec(memory_space=pltpu.VMEM)
    sm = pl.BlockSpec(memory_space=pltpu.SMEM)
    keys = 32 * OFF
    return pl.pallas_call(
        attention_kernel,
        out_shape=(
            jax.ShapeDtypeStruct((32, HALF, 2 * HS), jnp.bfloat16),
            jax.ShapeDtypeStruct((N_TP, depth, width // 2), jnp.bfloat16),
        ),
        in_specs=[sm, vm, vm, anywhere],
        out_specs=(vm, anywhere),
        scratch_shapes=[
            pltpu.VMEM((PAIRS, 2, keys, HS), jnp.bfloat16),
            pltpu.VMEM((keys, HS), jnp.bfloat16),
            pltpu.VMEM((keys, HS), jnp.float32),
            pltpu.VMEM((keys, 1), jnp.float32),
            pltpu.VMEM((keys, 1), jnp.float32),
            pltpu.VMEM((keys, 1), jnp.int32),
            pltpu.SemaphoreType.DMA((7,)),
            pltpu.SemaphoreType.DMA((PAIRS, 2)),
            pltpu.SemaphoreType.DMA((PAIRS,)),
            pltpu.SemaphoreType.DMA((13,)),
            pltpu.SemaphoreType.DMA((13,)),
            pltpu.SemaphoreType.DMA,
        ],
        compiler_params=pltpu.CompilerParams(
            collective_id=4, has_side_effects=True, vmem_limit_bytes=48 * 2**20
        ),
        name="attention",
    )(slot_of, query, kv, out_weight)


def out_kernel(
    span_order, attended, out_weight, rows, out, sorted_heads, heads, weight, product, result,
    wsem, hsend, hrecv, fsend, frecv, rsend, rrecv,
):
    c = lax.axis_index("ctx")
    t = lax.axis_index("tp")
    pair = c // 2
    core = c % 2
    sibling = c + 1 - 2 * core
    side = t // 4
    parts = N_TP // 2

    def load(g):
        return pltpu.make_async_copy(out_weight.at[g], weight.at[g], wsem.at[g])

    for g in range(N_TP):
        load(g).start()

    own = t == 0
    home = side == core
    origin = pair_of(pair, t)
    barrier = pltpu.get_barrier_semaphore()
    signal(barrier, sibling, t)
    for d in range(N_TP):
        j = lax.rem(t + d, N_TP)
        if d == 0:

            @pl.when(jnp.logical_not(own))
            def _():
                signal(barrier, 2 * origin + core, j)

            @pl.when(jnp.logical_not(home))
            def _():
                signal(barrier, 2 * pair + side, j)

        else:
            signal(barrier, 2 * origin + core, j)
            signal(barrier, 2 * pair + side, j)
    for j in range(32):
        sorted_heads[j] = attended[span_order[j]]
    pl.semaphore_wait(
        barrier, 1 + PAIRS - jnp.where(own, 1, 0) + 2 * parts - jnp.where(home, 1, 0)
    )

    mine = pl.ds(core * HALF, HALF)
    theirs = pl.ds((1 - core) * HALF, HALF)

    def gather(d):
        e = lax.rem(pair + d, PAIRS)
        return push(
            sorted_heads.at[pl.ds(4 * e, 4)], heads.at[t, :, mine, :], hsend.at[d], hrecv.at[t],
            2 * e + core, class_of(e, pair),
        )

    @pl.when(own)
    def _():
        pltpu.make_async_copy(
            sorted_heads.at[pl.ds(4 * pair, 4)], heads.at[t, :, mine, :], hrecv.at[t]
        ).start()

    @pl.when(jnp.logical_not(own))
    def _():
        gather(0).start()

    for d in range(1, PAIRS):
        gather(d).start()

    def forward(j):
        return push(
            heads.at[j, :, mine, :], heads.at[j, :, mine, :], fsend.at[j], frecv.at[j], sibling, t
        )

    for d in range(N_TP):
        j = lax.rem(t + d, N_TP)
        push(
            heads.at[j, :, mine, :], heads.at[j, :, mine, :], hsend.at[0], hrecv.at[j], sibling, t
        ).wait_recv()
        forward(j).start()
    for j in range(N_TP):
        push(
            heads.at[j, :, theirs, :], heads.at[j, :, theirs, :], fsend.at[j], frecv.at[j],
            sibling, t,
        ).wait_recv()
    for g in range(N_TP):
        load(g).wait()

    part = out.shape[-1]

    def send_home(j, a):
        return push(
            result.at[j, a], out.at[:, pl.ds(OFF * t, OFF), :], rsend.at[j, a], rrecv.at[t],
            2 * pair + a, parts * core + j,
        )

    def is_home(j, a):
        return jnp.logical_and(home, jnp.logical_and(a == core, parts * core + j == t))

    block = 2 * HS

    def project(n):
        total = jnp.zeros((4 * OFF, block), jnp.float32)
        for g in range(N_TP):
            x = heads[g].reshape(4 * OFF, 2 * HS)
            total = total + jnp.dot(
                x, weight[g, :, n * block : (n + 1) * block], preferred_element_type=jnp.float32
            ).astype(jnp.bfloat16).astype(jnp.float32)
        product[:, n * block : (n + 1) * block] = total

    ready = 0
    for j in range(parts):
        while ready * block < (j + 1) * part:
            project(ready)
            ready += 1
        start = j * part // HS * HS
        shift = j * part - start
        window = -(-(part + shift) // HS) * HS
        total = product[:, start : start + window]
        if shift:
            total = pltpu.roll(total, window - shift, 1)
        total = total[:, :part]
        for a in range(2):
            placed = rows[a, parts * core + j].reshape(2 * OFF, part).astype(jnp.float32)
            result[j, a] = (placed + total[a * 2 * OFF : (a + 1) * 2 * OFF]).astype(
                jnp.bfloat16
            ).reshape(2, OFF, part)

            @pl.when(is_home(j, a))
            def _():
                pltpu.make_async_copy(
                    result.at[j, a], out.at[:, pl.ds(OFF * t, OFF), :], rrecv.at[t]
                ).start()

            @pl.when(jnp.logical_not(is_home(j, a)))
            def _():
                send_home(j, a).start()

    for e in range(PAIRS):
        push(
            result.at[0, 0], out.at[:, pl.ds(OFF * e, OFF), :], rsend.at[0, 0], rrecv.at[e],
            sibling, t,
        ).wait_recv()

    @pl.when(jnp.logical_not(own))
    def _():
        gather(0).wait_send()

    for d in range(1, PAIRS):
        gather(d).wait_send()
    for j in range(N_TP):
        forward(j).wait_send()
    for j in range(parts):
        for a in range(2):

            @pl.when(jnp.logical_not(is_home(j, a)))
            def _():
                send_home(j, a).wait_send()


def out_exchange(span_order, attended, out_weight, rows):
    part = rows.shape[-1]
    parts = N_TP // 2
    vm = pl.BlockSpec(memory_space=pltpu.VMEM)
    anywhere = pl.BlockSpec(memory_space=pl.ANY)
    return pl.pallas_call(
        out_kernel,
        out_shape=jax.ShapeDtypeStruct((2, CH, part), jnp.bfloat16),
        in_specs=[pl.BlockSpec(memory_space=pltpu.SMEM), vm, anywhere, vm],
        out_specs=vm,
        scratch_shapes=[
            pltpu.VMEM((32, HALF, 2 * HS), jnp.bfloat16),
            pltpu.VMEM((N_TP, 4, OFF, 2 * HS), jnp.bfloat16),
            pltpu.VMEM(out_weight.shape, jnp.bfloat16),
            pltpu.VMEM((4 * OFF, parts * part), jnp.float32),
            pltpu.VMEM((parts, 2, 2, OFF, part), jnp.bfloat16),
            pltpu.SemaphoreType.DMA((N_TP,)),
            pltpu.SemaphoreType.DMA((N_TP,)),
            pltpu.SemaphoreType.DMA((N_TP,)),
            pltpu.SemaphoreType.DMA((N_TP,)),
            pltpu.SemaphoreType.DMA((N_TP,)),
            pltpu.SemaphoreType.DMA((parts, 2)),
            pltpu.SemaphoreType.DMA((PAIRS,)),
        ],
        compiler_params=pltpu.CompilerParams(
            collective_id=3, has_side_effects=True, vmem_limit_bytes=40 * 2**20
        ),
        name="out",
    )(span_order, attended, out_weight, rows)


def place_frames(text_embed, frame_features, frame_positions, slot_of, projector):
    tok_rows, part = text_embed.shape
    tokens = frame_positions.shape[0]
    spans = jnp.arange(slot_of.shape[0], dtype=jnp.int32)
    slot = jnp.sum(
        jnp.where((frame_positions // CH)[:, None] == spans[None, :], slot_of[None, :], 0), axis=1
    )
    target = slot // 2
    target_row = slot % 2 * CH + frame_positions % CH
    index = jnp.arange(tokens, dtype=jnp.int32)
    earlier = jnp.logical_and(target[None, :] == target[:, None], index[None, :] < index[:, None])
    place = jnp.sum(earlier.astype(jnp.int32), axis=1)
    entry = target * CAP + place
    entries = N_CTX * CAP
    chosen = jnp.arange(entries, dtype=jnp.int32)[:, None] == entry[None, :]
    sorted_features = jnp.dot(
        chosen.astype(jnp.bfloat16), frame_features, preferred_element_type=jnp.float32
    ).astype(jnp.bfloat16)
    row = jnp.sum(jnp.where(chosen, target_row[None, :] + 1, 0), axis=1) - 1
    projected = jax.nn.gelu(
        jnp.dot(sorted_features, projector, preferred_element_type=jnp.float32), approximate=False
    ).astype(jnp.bfloat16)
    outgoing = jnp.transpose(
        projected.reshape(N_CTX, CAP, N_TP, part), (0, 2, 1, 3)
    )
    row = row.reshape(N_CTX, 1, CAP, 1)
    high = jnp.broadcast_to(jnp.where(row < 0, -1, row // 32), (N_CTX, N_TP, CAP, 32))
    low = jnp.broadcast_to(jnp.where(row < 0, 0, row % 32), (N_CTX, N_TP, CAP, 32))
    outgoing = jnp.concatenate(
        [outgoing, high.astype(jnp.bfloat16), low.astype(jnp.bfloat16)], axis=3
    )
    arrived = lax.all_to_all(
        outgoing.reshape(N_CTX * N_TP, CAP, part + 64),
        ("ctx", "tp"),
        split_axis=0,
        concat_axis=0,
        tiled=True,
    ).reshape(N_CTX * N_TP * CAP, part + 64)
    at = (
        arrived[:, part].astype(jnp.float32) * 32.0 + arrived[:, part + 32].astype(jnp.float32)
    ).astype(jnp.int32)
    hit = jnp.arange(tok_rows, dtype=jnp.int32)[:, None] == at[None, :]
    inserted = jnp.dot(
        hit.astype(jnp.bfloat16), arrived[:, :part], preferred_element_type=jnp.float32
    ).astype(jnp.bfloat16)
    return jnp.where(jnp.any(hit, axis=1)[:, None], inserted, text_embed)


def per_device(
    text_embed,
    frame_features,
    frame_positions,
    span_order,
    projector,
    norm_gain,
    query_weight,
    key_weight,
    value_weight,
    out_weight,
):
    tok_rows, part = text_embed.shape
    c = lax.axis_index("ctx")
    t = lax.axis_index("tp")
    pair = c // 2
    core = c % 2
    q_half = lax.all_gather(lax.dynamic_slice_in_dim(query_weight, core * HS, HS, 1), "tp")
    slots = span_order.shape[0]
    index = jnp.arange(slots, dtype=jnp.int32)
    slot_of = jnp.sum(
        jnp.where(span_order[None, :] == index[:, None], index[None, :], 0), axis=1
    )
    placed = place_frames(text_embed, frame_features, frame_positions, slot_of, projector)
    gain = jnp.broadcast_to(norm_gain[None, :], (16, part))
    rows, normed = rows_exchange(placed.reshape(2, PAIRS, OFF, part), gain)

    spans = lax.dynamic_slice_in_dim(span_order, 4 * pair, 4, 0)
    positions = (
        spans[:, None] * CH + OFF * t + jnp.arange(OFF, dtype=jnp.int32)[None, :]
    ).reshape(-1)
    half = HS // 2
    freqs = 1000000.0 ** (-(jnp.arange(half, dtype=jnp.float32) * 2.0 / HS))
    angles = positions.astype(jnp.float32)[:, None] * freqs[None, :]
    cos = jnp.cos(angles)
    sin = jnp.sin(angles)
    cosine = jnp.concatenate([cos, cos], axis=1)
    sine = jnp.concatenate([-sin, sin], axis=1)
    kv_cosine = jnp.where(core == 0, cosine, 1.0)
    kv_sine = jnp.where(core == 0, sine, 0.0)
    query, kv = qkv_exchange(
        normed, q_half, key_weight, value_weight, (cosine, sine, kv_cosine, kv_sine)
    )
    attended, gathered = attention(
        slot_of, query.reshape(2, 32, HALF, HS), kv.reshape(32, OFF, HS), out_weight
    )
    mixed = out_exchange(span_order, attended, gathered, rows)
    return mixed.reshape(tok_rows, part)


def solution(mesh):
    in_specs = (
        P("ctx", "tp"),
        P(("ctx", "tp"), None),
        P(("ctx", "tp")),
        P(),
        P(),
        P("tp"),
        P(None, "tp"),
        P(),
        P(),
        P("tp", None),
    )
    out_specs = P("ctx", "tp")
    return jax.shard_map(
        per_device, mesh=mesh, in_specs=in_specs, out_specs=out_specs, check_vma=False
    )
```

```python
import functools
import math

import jax
import jax.numpy as jnp
from jax import lax
from jax.experimental import pallas as pl
from jax.experimental.pallas import tpu as pltpu
from jax.sharding import PartitionSpec as P

HS = 128
KVH = 4
CAP = 8
CH = 512
N_CTX = 16
N_TP = 8
PAIRS = 8
OFF = 64
HALF = 32
MESH = pl.DeviceIdType.MESH
LOG2E = math.log2(math.e)


def signal(sem, ctx, tp):
    pl.semaphore_signal(sem, inc=1, device_id=(ctx, tp), device_id_type=MESH)


def push(src, dst, send_sem, recv_sem, ctx, tp):
    return pltpu.make_async_remote_copy(
        src_ref=src, dst_ref=dst, send_sem=send_sem, recv_sem=recv_sem,
        device_id=(ctx, tp), device_id_type=MESH,
    )


def add4(a, b):
    return lax.rem(a + b + 4, 4)


def pair_of(e, t):
    return lax.rem(e // 4 + t // 4, 2) * 4 + add4(lax.rem(e, 4), lax.rem(t, 4))


def class_of(e, pair):
    return lax.rem(e // 4 + pair // 4, 2) * 4 + add4(lax.rem(pair, 4), -lax.rem(e, 4))


def intake_kernel(
    text, gain, features, pos_row, pos_col, order_row, order_col, cosine, sine,
    projector, query_weight, key_weight, value_weight,
    rows, query_out, kv_out,
    pweight, projected, outgoing, incoming, placed, gains, normed, weight, kv_weight, query, kv,
    psem, own_sem, kv_sem, fr_send, fr_recv, wsend, wrecv,
    send, recv, fsend, frecv, gsend, grecv, qsend, qrecv, ksend, krecv,
):
    c = lax.axis_index("ctx")
    t = lax.axis_index("tp")
    pair = c // 2
    core = c % 2
    sibling = c + 1 - 2 * core
    devices = N_CTX * N_TP
    me = c * N_TP + t
    part = text.shape[-1]
    width = N_TP * part
    base = pair // 4 * 4
    z = pair % 4
    z_up, z_down, z_far = (base + add4(z, n) for n in (1, 3, 2))
    y = lax.rem(t, 4)
    side = t - y
    across = 4 - side
    t_up, t_down, t_far = (side + add4(y, n) for n in (1, 3, 2))
    a_own, a_up, a_down, a_far = (across + add4(y, n) for n in (0, 1, 3, 2))
    x_next = 2 * (4 - base + z) + core

    own_copy = pltpu.make_async_copy(
        query_weight.at[:, pl.ds(pl.multiple_of(HS * core, HS), HS)], weight.at[t], own_sem
    )
    own_copy.start()
    block = 4 * HS
    blocks = width // block

    def load(n):
        cols = pl.ds(n * block, block)
        return pltpu.make_async_copy(projector.at[:, cols], pweight.at[:, cols], psem.at[n])

    for n in range(blocks):
        load(n).start()

    @pl.when(core == 0)
    def _():
        pltpu.make_async_copy(key_weight, kv_weight, kv_sem).start()

    @pl.when(core == 1)
    def _():
        pltpu.make_async_copy(value_weight, kv_weight, kv_sem).start()

    barrier = pltpu.get_barrier_semaphore()

    def greet(d, unused):
        other = lax.rem(me + d, devices)
        signal(barrier, other // N_TP, lax.rem(other, N_TP))
        return unused

    lax.fori_loop(1, devices, greet, 0)

    f32 = jnp.float32
    spans = order_row.shape[1]
    tokens = pos_row.shape[1]
    entries = N_CTX * CAP
    slot_row = jnp.sum(
        jnp.where(
            order_col[...] == pos_row[...] // CH,
            lax.broadcasted_iota(jnp.int32, (spans, tokens), 0).astype(f32), 0.0,
        ),
        axis=0, keepdims=True,
    ).astype(jnp.int32)
    slot_col = jnp.sum(
        jnp.where(
            order_row[...] == pos_col[...] // CH,
            lax.broadcasted_iota(jnp.int32, (tokens, spans), 1).astype(f32), 0.0,
        ),
        axis=1, keepdims=True,
    ).astype(jnp.int32)
    first = lax.broadcasted_iota(jnp.int32, (tokens, tokens), 0)
    second = lax.broadcasted_iota(jnp.int32, (tokens, tokens), 1)
    earlier = jnp.logical_and(slot_col // 2 == slot_row // 2, first < second)
    place = jnp.sum(jnp.where(earlier, 1.0, 0.0), axis=0, keepdims=True).astype(jnp.int32)
    entry = slot_row // 2 * CAP + place
    chosen = lax.broadcasted_iota(jnp.int32, (entries, tokens), 0) == entry
    ordered = jnp.dot(
        jnp.where(chosen, 1.0, 0.0).astype(jnp.bfloat16), features[...],
        preferred_element_type=f32,
    ).astype(jnp.bfloat16)
    token_row = (slot_row % 2 * CH + pos_row[...] % CH + 1).astype(f32)
    row_at = jnp.sum(jnp.where(chosen, token_row, 0.0), axis=1, keepdims=True) - 1.0
    row_at = row_at.astype(jnp.int32)
    high = (row_at >> 5).astype(f32)
    low = (row_at & 31).astype(f32)

    pl.semaphore_wait(barrier, devices - 1)

    depth = weight.shape[1]
    direct = pl.ds(0, depth // 2)

    def eighth(n):
        return pl.ds(depth // 2 + depth // 8 * n, depth // 8)

    def quarter(n):
        return pl.ds(depth // 4 * n, depth // 4)

    def wmove(m):
        if m == 0:
            ref, ctx, tp = weight.at[t], x_next, a_own
        elif m < 11:
            shard = t if m < 6 else a_own
            cut, tp = (
                (direct, t_up), (direct, t_down), (eighth(z), t_up), (eighth(z), t_down),
                (quarter(z), t_far),
            )[(m - 1) % 5]
            ref, ctx = weight.at[shard, cut], c
        else:
            n = m - 11
            shard = (t_up, t_down, t_far, a_up, a_down, a_far)[n // 3]
            cut = quarter(z) if n // 3 % 3 == 2 else eighth(z)
            ref, tp = weight.at[shard, cut], t
            ctx = 2 * (z_up, z_down, z_far)[n % 3] + core
        return push(ref, ref, wsend.at[m], wrecv.at[m], ctx, tp)

    def warrive(m):
        if m == 0:
            ref = weight.at[a_own]
        elif m < 11:
            n = (m - 1) % 5
            shard = ((t_down, t_up, t_down, t_up, t_far), (a_down, a_up, a_down, a_up, a_far))[
                (m - 1) // 5
            ][n]
            cut = (direct, direct, eighth(z), eighth(z), quarter(z))[n]
            ref = weight.at[shard, cut]
        else:
            n = m - 11
            shard = (t_up, t_down, t_far, a_up, a_down, a_far)[n // 3]
            origin = (add4(z, 3), add4(z, 1), add4(z, 2))[n % 3]
            cut = quarter(origin) if n // 3 % 3 == 2 else eighth(origin)
            ref = weight.at[shard, cut]
        push(ref, ref, wsend.at[m], wrecv.at[m], sibling, t).wait_recv()

    own_copy.wait()
    for m in (0, 5, 3, 4, 1, 2):
        wmove(m).start()

    for n in range(blocks):
        load(n).wait()
        cols = slice(n * block, (n + 1) * block)
        x = jnp.dot(ordered, pweight[:, cols], preferred_element_type=f32)
        projected[:, cols] = 0.5 * x * (1.0 + lax.erf(x * math.sqrt(0.5)))
    lane = lax.broadcasted_iota(jnp.int32, (entries, block), 1)
    tail = jnp.where(lane < part + 32, high, jnp.where(lane < part + 48, low, 1.0))
    for j in range(N_TP):
        start = j * part // HS * HS
        shift = j * part - start
        x = projected[:, start : start + block]
        if shift:
            x = pltpu.roll(x, block - shift, 1)
        x = jnp.where(lane < part, x, tail)
        halves = [
            x[:, n * 2 * HS : (n + 1) * 2 * HS].reshape(N_CTX, CAP, 2 * HS) for n in range(2)
        ]
        outgoing[:, j] = jnp.concatenate(halves, axis=1).astype(jnp.bfloat16)

    here = pltpu.make_async_copy(outgoing.at[c, t], incoming.at[me], fr_recv)
    here.start()

    def deliver(d, unused):
        other = lax.rem(me + d, devices)
        oc = other // N_TP
        ot = lax.rem(other, N_TP)
        push(outgoing.at[oc, ot], incoming.at[me], fr_send, fr_recv, oc, ot).start()
        return unused

    lax.fori_loop(1, devices, deliver, 0)
    for m in (3, 4, 5):
        warrive(m)
    for m in range(11, 20):
        wmove(m).start()
    warrive(0)
    for m in (10, 8, 9, 6, 7):
        wmove(m).start()
    pltpu.make_async_copy(incoming, incoming, fr_recv).wait()

    arrived = incoming[...].astype(f32)
    slots = devices * CAP
    left = arrived[:, :CAP].reshape(slots, 2 * HS)
    right = arrived[:, CAP:].reshape(slots, 2 * HS)
    edge = part - 2 * HS
    at = right[:, edge : edge + 1] * 32.0 + right[:, edge + 32 : edge + 33]
    at = jnp.transpose(jnp.broadcast_to(at, (slots, HS)))[0:1, :]
    left = left.astype(jnp.bfloat16)
    right = right.astype(jnp.bfloat16)
    group = CH // 2
    for n in range(4):
        a, b = n // 2, n % 2 * 4
        row = lax.broadcasted_iota(jnp.int32, (group, 1), 0) + n * group
        hit = jnp.where(row.astype(f32) == at, 1.0, 0.0).astype(jnp.bfloat16)
        new_left = jnp.dot(hit, left, preferred_element_type=f32)
        new_right = jnp.dot(hit, right, preferred_element_type=f32)
        framed = new_right[:, 2 * HS - 1 :] > 0.5
        old = text[a, b : b + 4].reshape(group, part).astype(f32)
        placed[a, b : b + 4, :, : 2 * HS] = (
            jnp.where(framed, new_left, old[:, : 2 * HS]).astype(jnp.bfloat16)
        ).reshape(4, OFF, 2 * HS)
        placed[a, b : b + 4, :, 2 * HS :] = (
            jnp.where(framed, new_right[:, :edge], old[:, 2 * HS :]).astype(jnp.bfloat16)
        ).reshape(4, OFF, edge)

    def row_block(d):
        j = lax.rem(t + d, N_TP)
        return push(placed.at[:, j], rows.at[core, t], send.at[d], recv.at[t], c, j)

    def gain_block(d):
        j = lax.rem(t + d, N_TP)
        return push(gain, gains.at[t], gsend.at[d], grecv.at[t], c, j)

    pltpu.make_async_copy(placed.at[:, t], rows.at[core, t], recv.at[t]).start()
    pltpu.make_async_copy(gain, gains.at[t], grecv.at[t]).start()
    for d in range(1, N_TP):
        row_block(d).start()
        gain_block(d).start()

    def forward(j):
        return push(rows.at[core, j], rows.at[core, j], fsend.at[j], frecv.at[j], sibling, t)

    for d in range(N_TP):
        j = lax.rem(t + d, N_TP)
        push(rows.at[core, j], rows.at[core, j], send.at[0], recv.at[j], sibling, t).wait_recv()
        forward(j).start()
    for j in range(N_TP):
        push(gain, gains.at[j], gsend.at[0], grecv.at[j], sibling, t).wait_recv()
    for m in (8, 9, 10):
        warrive(m)
    for m in range(20, 29):
        wmove(m).start()

    def normalise(a):
        total = jnp.zeros((2 * OFF, 1), f32)
        for j in range(N_TP):
            x = rows[a, j].reshape(2 * OFF, part).astype(f32)
            total = total + jnp.sum(x * x, axis=1, keepdims=True)
        inverse = lax.rsqrt(total / width + 1e-06)
        for j in range(N_TP):
            x = rows[a, j].reshape(2 * OFF, part).astype(f32)
            g = gains[j, 0:1, :].astype(f32)
            normed[j, a] = (x * inverse * g).astype(jnp.bfloat16)

    normalise(core)
    for j in range(N_TP):
        push(
            rows.at[1 - core, j], rows.at[1 - core, j], fsend.at[j], frecv.at[j], sibling, t
        ).wait_recv()
    normalise(1 - core)

    def product(piece):
        total = None
        for j in range(N_TP):
            x = normed[j].reshape(4 * OFF, part)
            term = jnp.dot(x, piece(slice(j * part, (j + 1) * part)), preferred_element_type=f32)
            total = term if total is None else total + term
        return total

    def rotated(x, cos, sin):
        return (x * cos + pltpu.roll(x, HS // 2, 1) * sin).astype(jnp.bfloat16).reshape(4, OFF, HS)

    goal = pair_of(pair, t)
    own = t == 0

    def kv_push(d):
        j = lax.rem(t + d, N_TP)
        return push(kv.at[j // 2], kv_out.at[pair], ksend.at[d], krecv.at[pair], 2 * goal + core, j)

    def q_push(j, k):
        return push(
            query.at[j, :, pl.ds(k * HALF, HALF), :], query_out.at[core, pair],
            qsend.at[j, k], qrecv.at[core, pair], 2 * goal + k, j,
        )

    pltpu.make_async_copy(key_weight, kv_weight, kv_sem).wait()
    cos = cosine[...]
    sin = sine[...]
    kv_cos = jnp.where(core == 0, cos, 1.0)
    kv_sin = jnp.where(core == 0, sin, 0.0)
    for h in range(0, KVH, 2):
        total = product(lambda cut: kv_weight[cut, h * HS : (h + 2) * HS])
        for n in range(2):
            kv[h + n] = rotated(total[:, n * HS : (n + 1) * HS], kv_cos, kv_sin)

    @pl.when(own)
    def _():
        pltpu.make_async_copy(kv.at[t // 2], kv_out.at[pair], krecv.at[pair]).start()

    @pl.when(jnp.logical_not(own))
    def _():
        kv_push(0).start()

    for d in range(1, N_TP):
        kv_push(d).start()

    def is_here(j, k):
        return jnp.logical_and(own, jnp.logical_and(j == t, core == k))

    def heads(begin):
        for h in range(0, 4, 2):
            j0, j1 = begin + h, begin + h + 1
            total = product(
                lambda cut: jnp.concatenate([weight[j0, cut], weight[j1, cut]], axis=1)
            )
            for n, j in enumerate((j0, j1)):
                query[j] = rotated(total[:, n * HS : (n + 1) * HS], cos, sin)
                for k in range(2):

                    @pl.when(is_here(j, k))
                    def _():
                        pltpu.make_async_copy(
                            query.at[j, :, pl.ds(k * HALF, HALF), :], query_out.at[core, pair],
                            qrecv.at[core, pair],
                        ).start()

                    @pl.when(jnp.logical_not(is_here(j, k)))
                    def _():
                        q_push(j, k).start()

    for m in (1, 2, *range(11, 20)):
        warrive(m)
    heads(side)
    for m in (6, 7, *range(20, 29)):
        warrive(m)
    heads(across)

    for e in range(PAIRS):
        push(kv.at[0], kv_out.at[e], ksend.at[0], krecv.at[e], c, t).wait_recv()
        for k in range(2):
            push(
                query_out.at[k, e], query_out.at[k, e], qsend.at[0, 0], qrecv.at[k, e], c, t
            ).wait_recv()
    pltpu.make_async_copy(
        incoming.at[pl.ds(0, devices - 1)], incoming.at[pl.ds(0, devices - 1)], fr_send
    ).wait()
    for m in range(29):
        wmove(m).wait_send()
    for d in range(1, N_TP):
        row_block(d).wait_send()
        gain_block(d).wait_send()
    for j in range(N_TP):
        forward(j).wait_send()

    @pl.when(jnp.logical_not(own))
    def _():
        kv_push(0).wait_send()

    for d in range(1, N_TP):
        kv_push(d).wait_send()
    for j in range(N_TP):
        for k in range(2):

            @pl.when(jnp.logical_not(is_here(j, k)))
            def _():
                q_push(j, k).wait_send()


def intake(
    text_embed, norm_gain, frame_features, frame_positions, span_order, tables,
    projector, query_weight, key_weight, value_weight,
):
    tok_rows, part = text_embed.shape
    depth = query_weight.shape[0]
    entries = N_CTX * CAP
    devices = N_CTX * N_TP
    vm = pl.BlockSpec(memory_space=pltpu.VMEM)
    anywhere = pl.BlockSpec(memory_space=pl.ANY)
    dma = pltpu.SemaphoreType.DMA
    bf16 = jnp.bfloat16
    return pl.pallas_call(
        intake_kernel,
        out_shape=(
            jax.ShapeDtypeStruct((2, N_TP, 2, OFF, part), bf16),
            jax.ShapeDtypeStruct((2, N_TP, 4, HALF, HS), bf16),
            jax.ShapeDtypeStruct((N_TP, 4, OFF, HS), bf16),
        ),
        in_specs=[vm] * 9 + [anywhere] * 4,
        out_specs=(vm, vm, vm),
        scratch_shapes=[
            pltpu.VMEM(projector.shape, bf16),
            pltpu.VMEM((entries, depth), jnp.float32),
            pltpu.VMEM((N_CTX, N_TP, 2 * CAP, 2 * HS), bf16),
            pltpu.VMEM((devices, 2 * CAP, 2 * HS), bf16),
            pltpu.VMEM((2, PAIRS, OFF, part), bf16),
            pltpu.VMEM((N_TP, 16, part), bf16),
            pltpu.VMEM((N_TP, 2, 2 * OFF, part), bf16),
            pltpu.VMEM((N_TP, depth, HS), bf16),
            pltpu.VMEM(key_weight.shape, bf16),
            pltpu.VMEM((N_TP, 4, OFF, HS), bf16),
            pltpu.VMEM((KVH, 4, OFF, HS), bf16),
            dma((depth // (4 * HS),)),
            dma,
            dma,
            dma,
            dma,
            dma((29,)),
            dma((29,)),
            dma((N_TP,)),
            dma((N_TP,)),
            dma((N_TP,)),
            dma((N_TP,)),
            dma((N_TP,)),
            dma((N_TP,)),
            dma((N_TP, 2)),
            dma((2, N_TP)),
            dma((N_TP,)),
            dma((N_TP,)),
        ],
        compiler_params=pltpu.CompilerParams(
            collective_id=1, has_side_effects=True, vmem_limit_bytes=48 * 2**20
        ),
        name="intake",
    )(
        text_embed.reshape(2, PAIRS, OFF, part),
        jnp.broadcast_to(norm_gain[None, :], (16, part)),
        frame_features,
        frame_positions.reshape(1, -1),
        frame_positions.reshape(-1, 1),
        span_order.reshape(1, -1),
        span_order.reshape(-1, 1),
        *tables,
        projector,
        query_weight,
        key_weight,
        value_weight,
    )


def attention_kernel(
    slot_of, query, kv_own, out_weight, out, gathered,
    kv, q, summed, largest, total, limit, send, recv, pass_send, wsend, wrecv, own_sem,
):
    scale = LOG2E / math.sqrt(HS)
    c = lax.axis_index("ctx")
    t = lax.axis_index("tp")
    pair = c // 2
    core = c % 2
    sibling = c + 1 - 2 * core
    base = pair // 4 * 4
    other = 4 - base
    z = pair % 4
    up = lax.rem(z + 1, 4)
    down = lax.rem(z + 3, 4)
    far = lax.rem(z + 2, 4)
    z_up, z_down, z_far = base + up, base + down, base + far
    x_own, x_up, x_down, x_far = other + z, other + up, other + down, other + far

    y = lax.rem(t, 4)
    side = t - y
    across = 4 - side
    t_up, t_down, t_far = (side + add4(y, n) for n in (1, 3, 2))
    a_own, a_up, a_down, a_far = (across + add4(y, n) for n in (0, 1, 3, 2))
    x_next = 2 * x_own + core

    barrier = pltpu.get_barrier_semaphore()
    signal(barrier, sibling, t)
    for e in (z_up, z_down, z_far, x_own):
        signal(barrier, 2 * e + core, t)
    signal(barrier, x_next, a_own)
    for j in (t_up, t_down, t_far):
        signal(barrier, c, j)
    for j in range(32):
        kv[pair, core, j * OFF : (j + 1) * OFF] = kv_own[slot_of[j]]
    pl.semaphore_wait(barrier, 9)

    cols = gathered.shape[-1]
    quarter_rows = gathered.shape[1] // 4
    own_weight = out_weight.at[:, pl.ds(pl.multiple_of(cols * core, HS), cols)]

    def quarter(ref, n):
        return ref.at[pl.ds(quarter_rows * n, quarter_rows)]

    def wmove(m):
        whole = lambda g: (gathered.at[g], gathered.at[g])
        part = lambda g: (quarter(gathered.at[g], z), quarter(gathered.at[g], z))
        src, dst, ctx, tp = (
            (own_weight, gathered.at[t], x_next, a_own),
            (own_weight, gathered.at[t], c, t_up),
            (own_weight, gathered.at[t], c, t_down),
            (quarter(own_weight, z), quarter(gathered.at[t], z), c, t_far),
            (*whole(a_own), c, t_up),
            (*whole(a_own), c, t_down),
            (*part(a_own), c, t_far),
            (*part(t_far), 2 * z_up + core, t),
            (*part(t_far), 2 * z_down + core, t),
            (*part(t_far), 2 * z_far + core, t),
            (*part(a_far), 2 * z_up + core, t),
            (*part(a_far), 2 * z_down + core, t),
            (*part(a_far), 2 * z_far + core, t),
        )[m]
        return push(src, dst, wsend.at[m], wrecv.at[m], ctx, tp)

    def warrive(m):
        ref = (
            gathered.at[a_own], gathered.at[t_down], gathered.at[t_up],
            quarter(gathered.at[t_far], z),
            gathered.at[a_down], gathered.at[a_up], quarter(gathered.at[a_far], z),
            quarter(gathered.at[t_far], down), quarter(gathered.at[t_far], up),
            quarter(gathered.at[t_far], far),
            quarter(gathered.at[a_far], down), quarter(gathered.at[a_far], up),
            quarter(gathered.at[a_far], far),
        )[m]
        push(ref, ref, wsend.at[m], wrecv.at[m], sibling, t).wait_recv()

    def transfer(e, to, index):
        block = kv.at[e, core]
        return push(block, block, send.at[index], recv.at[e, core], 2 * to + core, t)

    def share(e):
        block = kv.at[e, core]
        return push(block, block, pass_send.at[e], recv.at[e, core], sibling, t)

    def arrive(e, which):
        block = kv.at[e, which]
        push(block, block, send.at[0], recv.at[e, which], sibling, t).wait_recv()

    share(pair).start()
    moves = (
        (pair, x_own), (pair, z_up), (pair, z_down), (pair, z_far),
        (x_own, z_up), (x_own, z_down), (z_far, x_own),
    )
    for index in range(3):
        transfer(*moves[index], index).start()
    for m in (0, 3, 1, 2):
        wmove(m).start()
    own_copy = pltpu.make_async_copy(own_weight, gathered.at[t], own_sem)
    own_copy.start()
    for j in range(32):
        q[j * OFF : (j + 1) * OFF] = query[:, slot_of[j]].reshape(2 * HALF, HS)

    rows = 8 * HALF
    row = lax.broadcasted_iota(jnp.int32, (rows, 1), 0)
    col = lax.broadcasted_iota(jnp.int32, (1, 4 * OFF), 1)

    def starts(index, i, e):
        value = jnp.zeros(index.shape, jnp.int32)
        for a in range(4):
            start = a * CH + OFF * class_of(slot_of[4 * i + a] // 4, e)
            value = jnp.where(index // OFF == a, start, value)
        return value

    for i in range(8):
        limit[i * rows : (i + 1) * rows] = (
            starts(row, i, pair) + HALF * core + row % HALF
        )

    def update(e, first):
        for i in range(8):
            at = starts(col, i, e) + col % OFF
            here = slice(i * rows, (i + 1) * rows)
            width = 4 * OFF * (i + 1)
            s = lax.dot_general(
                q[here], kv[e, 0, :width], (((1,), (1,)), ((), ())),
                preferred_element_type=jnp.float32,
            )
            edge = jnp.where(at <= limit[here], s[:, width - 4 * OFF :], -1e30)
            s = edge if i == 0 else jnp.concatenate([s[:, : width - 4 * OFF], edge], axis=1)
            top = jnp.max(s, axis=1, keepdims=True)
            if not first:
                top = jnp.maximum(top, largest[here])
            weights = jnp.exp2((s - top) * scale)
            added = jnp.sum(weights, axis=1, keepdims=True)
            product = jnp.dot(
                weights.astype(jnp.bfloat16), kv[e, 1, :width], preferred_element_type=jnp.float32
            )
            if not first:
                factor = jnp.exp2((largest[here] - top) * scale)
                added = added + total[here] * factor
                product = product + summed[here] * factor
            largest[here] = top
            total[here] = added
            summed[here] = product

    arrive(pair, 1 - core)
    update(pair, True)
    transfer(*moves[3], 3).start()
    arrive(x_own, core)
    transfer(*moves[4], 4).start()
    transfer(*moves[5], 5).start()
    share(x_own).start()
    arrive(z_up, core)
    share(z_up).start()
    arrive(z_down, core)
    share(z_down).start()

    order = (x_own, z_up, z_down, x_up, x_down, z_far, x_far)

    def step(n, unused):
        e = order[6]
        for index in range(6):
            e = jnp.where(n == index, order[index], e)

        @pl.when(n == 2)
        def _():
            warrive(3)
            for m in (7, 8, 9):
                wmove(m).start()
            arrive(x_up, core)
            share(x_up).start()

        @pl.when(n == 3)
        def _():
            arrive(x_down, core)
            share(x_down).start()
            arrive(z_far, core)
            transfer(*moves[6], 6).start()
            share(z_far).start()

        @pl.when(n == 4)
        def _():
            warrive(0)
            for m in (6, 4, 5):
                wmove(m).start()

        @pl.when(n == 6)
        def _():
            arrive(x_far, core)
            share(x_far).start()

        arrive(e, 1 - core)
        update(e, False)
        return unused

    lax.fori_loop(0, 7, step, 0)
    for i in range(8):
        here = slice(i * rows, (i + 1) * rows)
        attended = (summed[here] / total[here]).astype(jnp.bfloat16).reshape(4, 2, HALF, HS)
        for a in range(4):
            out[4 * i + a] = jnp.concatenate([attended[a, 0], attended[a, 1]], axis=1)
    warrive(6)
    for m in (10, 11, 12):
        wmove(m).start()
    for m in (1, 2, 4, 5, 7, 8, 9, 10, 11, 12):
        warrive(m)
    own_copy.wait()
    for index in range(7):
        transfer(*moves[index], index).wait_send()
    for e in range(PAIRS):
        share(e).wait_send()
    for m in range(13):
        wmove(m).wait_send()


def attention(slot_of, query, kv, out_weight):
    anywhere = pl.BlockSpec(memory_space=pl.ANY)
    depth, width = out_weight.shape
    vm = pl.BlockSpec(memory_space=pltpu.VMEM)
    sm = pl.BlockSpec(memory_space=pltpu.SMEM)
    keys = 32 * OFF
    return pl.pallas_call(
        attention_kernel,
        out_shape=(
            jax.ShapeDtypeStruct((32, HALF, 2 * HS), jnp.bfloat16),
            jax.ShapeDtypeStruct((N_TP, depth, width // 2), jnp.bfloat16),
        ),
        in_specs=[sm, vm, vm, anywhere],
        out_specs=(vm, anywhere),
        scratch_shapes=[
            pltpu.VMEM((PAIRS, 2, keys, HS), jnp.bfloat16),
            pltpu.VMEM((keys, HS), jnp.bfloat16),
            pltpu.VMEM((keys, HS), jnp.float32),
            pltpu.VMEM((keys, 1), jnp.float32),
            pltpu.VMEM((keys, 1), jnp.float32),
            pltpu.VMEM((keys, 1), jnp.int32),
            pltpu.SemaphoreType.DMA((7,)),
            pltpu.SemaphoreType.DMA((PAIRS, 2)),
            pltpu.SemaphoreType.DMA((PAIRS,)),
            pltpu.SemaphoreType.DMA((13,)),
            pltpu.SemaphoreType.DMA((13,)),
            pltpu.SemaphoreType.DMA,
        ],
        compiler_params=pltpu.CompilerParams(
            collective_id=4, has_side_effects=True, vmem_limit_bytes=48 * 2**20
        ),
        name="attention",
    )(slot_of, query, kv, out_weight)


def out_kernel(
    span_order, attended, out_weight, rows, out, sorted_heads, heads, weight, product, result,
    wsem, hsend, hrecv, fsend, frecv, rsend, rrecv,
):
    c = lax.axis_index("ctx")
    t = lax.axis_index("tp")
    pair = c // 2
    core = c % 2
    sibling = c + 1 - 2 * core
    side = t // 4
    parts = N_TP // 2

    def load(g):
        return pltpu.make_async_copy(out_weight.at[g], weight.at[g], wsem.at[g])

    for g in range(N_TP):
        load(g).start()

    own = t == 0
    home = side == core
    origin = pair_of(pair, t)
    barrier = pltpu.get_barrier_semaphore()
    signal(barrier, sibling, t)
    for d in range(N_TP):
        j = lax.rem(t + d, N_TP)
        if d == 0:

            @pl.when(jnp.logical_not(own))
            def _():
                signal(barrier, 2 * origin + core, j)

            @pl.when(jnp.logical_not(home))
            def _():
                signal(barrier, 2 * pair + side, j)

        else:
            signal(barrier, 2 * origin + core, j)
            signal(barrier, 2 * pair + side, j)
    for j in range(32):
        sorted_heads[j] = attended[span_order[j]]
    pl.semaphore_wait(
        barrier, 1 + PAIRS - jnp.where(own, 1, 0) + 2 * parts - jnp.where(home, 1, 0)
    )

    mine = pl.ds(core * HALF, HALF)
    theirs = pl.ds((1 - core) * HALF, HALF)

    def gather(d):
        e = lax.rem(pair + d, PAIRS)
        return push(
            sorted_heads.at[pl.ds(4 * e, 4)], heads.at[t, :, mine, :], hsend.at[d], hrecv.at[t],
            2 * e + core, class_of(e, pair),
        )

    @pl.when(own)
    def _():
        pltpu.make_async_copy(
            sorted_heads.at[pl.ds(4 * pair, 4)], heads.at[t, :, mine, :], hrecv.at[t]
        ).start()

    @pl.when(jnp.logical_not(own))
    def _():
        gather(0).start()

    for d in range(1, PAIRS):
        gather(d).start()

    def forward(j):
        return push(
            heads.at[j, :, mine, :], heads.at[j, :, mine, :], fsend.at[j], frecv.at[j], sibling, t
        )

    for d in range(N_TP):
        j = lax.rem(t + d, N_TP)
        push(
            heads.at[j, :, mine, :], heads.at[j, :, mine, :], hsend.at[0], hrecv.at[j], sibling, t
        ).wait_recv()
        forward(j).start()
    for j in range(N_TP):
        push(
            heads.at[j, :, theirs, :], heads.at[j, :, theirs, :], fsend.at[j], frecv.at[j],
            sibling, t,
        ).wait_recv()
    for g in range(N_TP):
        load(g).wait()

    part = out.shape[-1]

    def send_home(j, a):
        return push(
            result.at[j, a], out.at[:, pl.ds(OFF * t, OFF), :], rsend.at[j, a], rrecv.at[t],
            2 * pair + a, parts * core + j,
        )

    def is_home(j, a):
        return jnp.logical_and(home, jnp.logical_and(a == core, parts * core + j == t))

    block = 2 * HS

    def project(n):
        total = jnp.zeros((4 * OFF, block), jnp.float32)
        for g in range(N_TP):
            x = heads[g].reshape(4 * OFF, 2 * HS)
            total = total + jnp.dot(
                x, weight[g, :, n * block : (n + 1) * block], preferred_element_type=jnp.float32
            ).astype(jnp.bfloat16).astype(jnp.float32)
        product[:, n * block : (n + 1) * block] = total

    ready = 0
    for j in range(parts):
        while ready * block < (j + 1) * part:
            project(ready)
            ready += 1
        start = j * part // HS * HS
        shift = j * part - start
        window = -(-(part + shift) // HS) * HS
        total = product[:, start : start + window]
        if shift:
            total = pltpu.roll(total, window - shift, 1)
        total = total[:, :part]
        for a in range(2):
            placed = rows[a, parts * core + j].reshape(2 * OFF, part).astype(jnp.float32)
            result[j, a] = (placed + total[a * 2 * OFF : (a + 1) * 2 * OFF]).astype(
                jnp.bfloat16
            ).reshape(2, OFF, part)

            @pl.when(is_home(j, a))
            def _():
                pltpu.make_async_copy(
                    result.at[j, a], out.at[:, pl.ds(OFF * t, OFF), :], rrecv.at[t]
                ).start()

            @pl.when(jnp.logical_not(is_home(j, a)))
            def _():
                send_home(j, a).start()

    for e in range(PAIRS):
        push(
            result.at[0, 0], out.at[:, pl.ds(OFF * e, OFF), :], rsend.at[0, 0], rrecv.at[e],
            sibling, t,
        ).wait_recv()

    @pl.when(jnp.logical_not(own))
    def _():
        gather(0).wait_send()

    for d in range(1, PAIRS):
        gather(d).wait_send()
    for j in range(N_TP):
        forward(j).wait_send()
    for j in range(parts):
        for a in range(2):

            @pl.when(jnp.logical_not(is_home(j, a)))
            def _():
                send_home(j, a).wait_send()


def out_exchange(span_order, attended, out_weight, rows):
    part = rows.shape[-1]
    parts = N_TP // 2
    vm = pl.BlockSpec(memory_space=pltpu.VMEM)
    anywhere = pl.BlockSpec(memory_space=pl.ANY)
    return pl.pallas_call(
        out_kernel,
        out_shape=jax.ShapeDtypeStruct((2, CH, part), jnp.bfloat16),
        in_specs=[pl.BlockSpec(memory_space=pltpu.SMEM), vm, anywhere, vm],
        out_specs=vm,
        scratch_shapes=[
            pltpu.VMEM((32, HALF, 2 * HS), jnp.bfloat16),
            pltpu.VMEM((N_TP, 4, OFF, 2 * HS), jnp.bfloat16),
            pltpu.VMEM(out_weight.shape, jnp.bfloat16),
            pltpu.VMEM((4 * OFF, parts * part), jnp.float32),
            pltpu.VMEM((parts, 2, 2, OFF, part), jnp.bfloat16),
            pltpu.SemaphoreType.DMA((N_TP,)),
            pltpu.SemaphoreType.DMA((N_TP,)),
            pltpu.SemaphoreType.DMA((N_TP,)),
            pltpu.SemaphoreType.DMA((N_TP,)),
            pltpu.SemaphoreType.DMA((N_TP,)),
            pltpu.SemaphoreType.DMA((parts, 2)),
            pltpu.SemaphoreType.DMA((PAIRS,)),
        ],
        compiler_params=pltpu.CompilerParams(
            collective_id=3, has_side_effects=True, vmem_limit_bytes=40 * 2**20
        ),
        name="out",
    )(span_order, attended, out_weight, rows)


def per_device(
    text_embed,
    frame_features,
    frame_positions,
    span_order,
    projector,
    norm_gain,
    query_weight,
    key_weight,
    value_weight,
    out_weight,
):
    tok_rows, part = text_embed.shape
    c = lax.axis_index("ctx")
    t = lax.axis_index("tp")
    pair = c // 2
    slots = span_order.shape[0]
    index = jnp.arange(slots, dtype=jnp.int32)
    slot_of = jnp.sum(
        jnp.where(span_order[None, :] == index[:, None], index[None, :], 0), axis=1
    )
    spans = lax.dynamic_slice_in_dim(span_order, 4 * pair, 4, 0)
    positions = (
        spans[:, None] * CH + OFF * t + jnp.arange(OFF, dtype=jnp.int32)[None, :]
    ).reshape(-1)
    half = HS // 2
    freqs = 1000000.0 ** (-(jnp.arange(half, dtype=jnp.float32) * 2.0 / HS))
    angles = positions.astype(jnp.float32)[:, None] * freqs[None, :]
    cos = jnp.cos(angles)
    sin = jnp.sin(angles)
    cosine = jnp.concatenate([cos, cos], axis=1)
    sine = jnp.concatenate([-sin, sin], axis=1)
    rows, query, kv = intake(
        text_embed, norm_gain, frame_features, frame_positions, span_order, (cosine, sine),
        projector, query_weight, key_weight, value_weight,
    )
    attended, gathered = attention(
        slot_of, query.reshape(2, 32, HALF, HS), kv.reshape(32, OFF, HS), out_weight
    )
    mixed = out_exchange(span_order, attended, gathered, rows)
    return mixed.reshape(tok_rows, part)


def solution(mesh):
    in_specs = (
        P("ctx", "tp"),
        P(("ctx", "tp"), None),
        P(("ctx", "tp")),
        P(),
        P(),
        P("tp"),
        P(None, "tp"),
        P(),
        P(),
        P("tp", None),
    )
    out_specs = P("ctx", "tp")
    return jax.shard_map(
        per_device, mesh=mesh, in_specs=in_specs, out_specs=out_specs, check_vma=False
    )
```

```python
import functools
import math

import jax
import jax.numpy as jnp
from jax import lax
from jax.experimental import pallas as pl
from jax.experimental.pallas import tpu as pltpu
from jax.sharding import PartitionSpec as P

HS = 128
KVH = 4
CAP = 8
CH = 512
N_CTX = 16
N_TP = 8
PAIRS = 8
OFF = 64
HALF = 32
MESH = pl.DeviceIdType.MESH
LOG2E = math.log2(math.e)


def signal(sem, ctx, tp):
    pl.semaphore_signal(sem, inc=1, device_id=(ctx, tp), device_id_type=MESH)


def push(src, dst, send_sem, recv_sem, ctx, tp):
    return pltpu.make_async_remote_copy(
        src_ref=src, dst_ref=dst, send_sem=send_sem, recv_sem=recv_sem,
        device_id=(ctx, tp), device_id_type=MESH,
    )


def add4(a, b):
    return lax.rem(a + b + 4, 4)


def pair_of(e, t):
    return lax.rem(e // 4 + t // 4, 2) * 4 + add4(lax.rem(e, 4), lax.rem(t, 4))


def class_of(e, pair):
    return lax.rem(e // 4 + pair // 4, 2) * 4 + add4(lax.rem(pair, 4), -lax.rem(e, 4))


def intake_kernel(
    text, gain, features, pos_row, pos_col, order_row, order_col, cosine, sine,
    projector, query_weight, key_weight, value_weight,
    rows_out, query_out, kv_out,
    pweight, outgoing, incoming, placed, rows, gains, normed, weight, kv_weight, query, kv,
    psem, own_sem, kv_sem, fr_send, fr_recv, wsend, wrecv, csend, crecv,
    send, recv, gsend, grecv, osem, osend, orecv, qsend, qrecv, ksend, krecv,
):
    c = lax.axis_index("ctx")
    t = lax.axis_index("tp")
    pair = c // 2
    core = c % 2
    sibling = c + 1 - 2 * core
    devices = N_CTX * N_TP
    me = c * N_TP + t
    part = text.shape[-1]
    width = N_TP * part
    base = pair // 4 * 4
    z = pair % 4
    z_up, z_down, z_far = (base + add4(z, n) for n in (1, 3, 2))
    y = lax.rem(t, 4)
    side = t - y
    half = t // 4
    y_up, y_down, y_far = (add4(y, n) for n in (1, 3, 2))

    own_copy = pltpu.make_async_copy(
        query_weight.at[:, pl.ds(pl.multiple_of(HS * core, HS), HS)], weight.at[core, y], own_sem
    )
    own_copy.start()
    block = 4 * HS

    def load(d):
        j = lax.rem(t + d, N_TP)
        start = pl.multiple_of((j * part) // HS * HS, HS)
        return pltpu.make_async_copy(
            projector.at[:, pl.ds(start, block)], pweight.at[d], psem.at[d]
        )

    for d in range(N_TP):
        load(d).start()
    kv_cols = pl.ds(pl.multiple_of(2 * HS * half, HS), 2 * HS)
    kv_loads = [
        pltpu.make_async_copy(ref.at[:, kv_cols], kv_weight.at[n], kv_sem.at[n])
        for n, ref in enumerate((key_weight, value_weight))
    ]
    for one in kv_loads:
        one.start()

    barrier = pltpu.get_barrier_semaphore()

    def greet(d, unused):
        other = lax.rem(me + d, devices)
        signal(barrier, other // N_TP, lax.rem(other, N_TP))
        return unused

    lax.fori_loop(1, devices, greet, 0)

    f32 = jnp.float32
    spans = order_row.shape[1]
    tokens = pos_row.shape[1]
    entries = N_CTX * CAP
    slot_row = jnp.sum(
        jnp.where(
            order_col[...] == pos_row[...] // CH,
            lax.broadcasted_iota(jnp.int32, (spans, tokens), 0).astype(f32), 0.0,
        ),
        axis=0, keepdims=True,
    ).astype(jnp.int32)
    slot_col = jnp.sum(
        jnp.where(
            order_row[...] == pos_col[...] // CH,
            lax.broadcasted_iota(jnp.int32, (tokens, spans), 1).astype(f32), 0.0,
        ),
        axis=1, keepdims=True,
    ).astype(jnp.int32)
    first = lax.broadcasted_iota(jnp.int32, (tokens, tokens), 0)
    second = lax.broadcasted_iota(jnp.int32, (tokens, tokens), 1)
    earlier = jnp.logical_and(slot_col // 2 == slot_row // 2, first < second)
    place = jnp.sum(jnp.where(earlier, 1.0, 0.0), axis=0, keepdims=True).astype(jnp.int32)
    entry = slot_row // 2 * CAP + place
    chosen = lax.broadcasted_iota(jnp.int32, (entries, tokens), 0) == entry
    ordered = jnp.dot(
        jnp.where(chosen, 1.0, 0.0).astype(jnp.bfloat16), features[...],
        preferred_element_type=f32,
    ).astype(jnp.bfloat16)
    token_row = (slot_row % 2 * CH + pos_row[...] % CH + 1).astype(f32)
    row_at = jnp.sum(jnp.where(chosen, token_row, 0.0), axis=1, keepdims=True) - 1.0
    row_at = row_at.astype(jnp.int32)
    high = (row_at >> 5).astype(f32)
    low = (row_at & 31).astype(f32)
    lane = lax.broadcasted_iota(jnp.int32, (entries, block), 1)
    tail = jnp.where(lane < part + 32, high, jnp.where(lane < part + 48, low, 1.0))

    pl.semaphore_wait(barrier, devices - 1)

    depth = weight.shape[2]
    direct = pl.ds(0, depth // 2)

    def eighth(n):
        return pl.ds(depth // 2 + depth // 8 * n, depth // 8)

    def quarter(n):
        return pl.ds(depth // 4 * n, depth // 4)

    def wmove(m):
        if m < 5:
            cut, tp = (
                (direct, y_up), (direct, y_down), (eighth(z), y_up), (eighth(z), y_down),
                (quarter(z), y_far),
            )[m]
            ref, ctx, tp = weight.at[core, y, cut], c, side + tp
        else:
            n = m - 5
            cut = quarter(z) if n // 3 == 2 else eighth(z)
            ref, tp = weight.at[core, (y_up, y_down, y_far)[n // 3], cut], t
            ctx = 2 * (z_up, z_down, z_far)[n % 3] + core
        return push(ref, ref, wsend.at[m], wrecv.at[m], ctx, tp)

    def warrive(m):
        if m < 5:
            shard = (y_down, y_up, y_down, y_up, y_far)[m]
            cut = (direct, direct, eighth(z), eighth(z), quarter(z))[m]
        else:
            n = m - 5
            shard = (y_up, y_down, y_far)[n // 3]
            origin = (add4(z, 3), add4(z, 1), add4(z, 2))[n % 3]
            cut = quarter(origin) if n // 3 == 2 else eighth(origin)
        ref = weight.at[core, shard, cut]
        push(ref, ref, wsend.at[m], wrecv.at[m], sibling, t).wait_recv()

    def share(n):
        ref = weight.at[core, add4(y, n)]
        return push(ref, ref, csend.at[n], crecv.at[n], sibling, t)

    def shared(n):
        ref = weight.at[1 - core, add4(y, n)]
        push(ref, ref, csend.at[n], crecv.at[n], sibling, t).wait_recv()

    own_copy.wait()
    for m in (4, 2, 3, 0, 1):
        wmove(m).start()
    share(0).start()

    for d in range(N_TP):
        j = lax.rem(t + d, N_TP)
        load(d).wait()
        x = jnp.dot(ordered, pweight[d], preferred_element_type=f32)
        x = 0.5 * x * (1.0 + lax.erf(x * math.sqrt(0.5)))
        shift = j * part - (j * part) // HS * HS
        x = jnp.where(shift > 0, pltpu.roll(x, block - HS // 2, 1), x)
        x = jnp.where(lane < part, x, tail)
        halves = [
            x[:, n * 2 * HS : (n + 1) * 2 * HS].reshape(N_CTX, CAP, 2 * HS) for n in range(2)
        ]
        outgoing[d] = jnp.concatenate(halves, axis=1).astype(jnp.bfloat16)

        def deliver(n, unused):
            oc = lax.rem(c + n, N_CTX)
            push(outgoing.at[d, oc], incoming.at[me], fr_send, fr_recv, oc, j).start()
            return unused

        if d == 0:
            pltpu.make_async_copy(outgoing.at[0, c], incoming.at[me], fr_recv).start()
        else:
            push(outgoing.at[d, c], incoming.at[me], fr_send, fr_recv, c, j).start()
        lax.fori_loop(1, N_CTX, deliver, 0)

    for m in (2, 3, 4):
        warrive(m)
    for m in range(5, 14):
        wmove(m).start()
    pltpu.make_async_copy(incoming, incoming, fr_recv).wait()

    def row_block(n, across):
        j = add4(y, n)
        tp = j + (4 - side if across else side)
        return push(
            placed.at[:, j], rows.at[t], send.at[n, across], recv.at[t], c, tp
        )

    def gain_block(d):
        return push(gain, gains.at[t], gsend.at[d], grecv.at[t], c, lax.rem(t + d, N_TP))

    pltpu.make_async_copy(gain, gains.at[t], grecv.at[t]).start()
    for d in range(1, N_TP):
        gain_block(d).start()
    arrived = incoming[...].astype(f32)
    slots = devices * CAP
    left = arrived[:, :CAP].reshape(slots, 2 * HS)
    right = arrived[:, CAP:].reshape(slots, 2 * HS)
    edge = part - 2 * HS
    at = right[:, edge : edge + 1] * 32.0 + right[:, edge + 32 : edge + 33]
    at = jnp.transpose(jnp.broadcast_to(at, (slots, HS)))[0:1, :]
    left = left.astype(jnp.bfloat16)
    right = right.astype(jnp.bfloat16)
    group = 2 * HS
    offset = lax.broadcasted_iota(jnp.int32, (group, 1), 0)
    offset = offset // HS * CH + offset % HS
    for n in range(4):
        j = add4(y, n)
        row = offset + j * HS
        hit = jnp.where(row.astype(f32) == at, 1.0, 0.0).astype(jnp.bfloat16)
        new_left = jnp.dot(hit, left, preferred_element_type=f32)
        new_right = jnp.dot(hit, right, preferred_element_type=f32)
        framed = new_right[:, 2 * HS - 1 :] > 0.5
        old = text[:, j].reshape(group, part).astype(f32)
        placed[:, j, :, : 2 * HS] = (
            jnp.where(framed, new_left, old[:, : 2 * HS]).astype(jnp.bfloat16)
        ).reshape(2, HS, 2 * HS)
        placed[:, j, :, 2 * HS :] = (
            jnp.where(framed, new_right[:, :edge], old[:, 2 * HS :]).astype(jnp.bfloat16)
        ).reshape(2, HS, edge)
        row_block(n, 1).start()
        if n == 0:
            pltpu.make_async_copy(placed.at[:, y], rows.at[t], recv.at[t]).start()
        else:
            row_block(n, 0).start()

    for m in (0, 1, *range(5, 14)):
        warrive(m)
    for n in range(1, 4):
        share(n).start()
    for one in kv_loads:
        one.wait()

    total = jnp.zeros((group, 1), f32)
    for d in range(N_TP):
        j = lax.rem(t + d, N_TP)
        push(gain, gains.at[j], gsend.at[0], grecv.at[j], sibling, t).wait_recv()
        push(rows.at[j], rows.at[j], send.at[0, 0], recv.at[j], sibling, t).wait_recv()
        x = rows[j].reshape(group, part).astype(f32)
        total = total + jnp.sum(x * x, axis=1, keepdims=True)

    def keep(n):
        return pltpu.make_async_copy(
            rows.at[4 * core + n, :, pl.ds(OFF * half, OFF)], rows_out.at[core, n], osem.at[n]
        )

    def give(n):
        return push(
            rows.at[4 * (1 - core) + n, :, pl.ds(OFF * half, OFF)], rows_out.at[core, n],
            osend.at[n], orecv.at[n], sibling, t,
        )

    for n in range(4):
        keep(n).start()
        give(n).start()

    inverse = lax.rsqrt(total / width + 1e-06)
    for j in range(N_TP):
        x = rows[j].reshape(group, part).astype(f32)
        normed[j] = (x * inverse * gains[j, 0:1, :].astype(f32)).astype(jnp.bfloat16)

    def product(piece):
        total = None
        for j in range(N_TP):
            term = jnp.dot(
                normed[j], piece(slice(j * part, (j + 1) * part)), preferred_element_type=f32
            )
            total = term if total is None else total + term
        return total

    def rotated(x, cos, sin):
        return (x * cos + pltpu.roll(x, HS // 2, 1) * sin).astype(jnp.bfloat16).reshape(2, HS, HS)

    goal = [pair_of(pair, 4 * n + y) for n in range(2)]
    mine = pl.ds(2 * core, 2)

    def kv_push(n, which, m):
        return push(
            kv.at[which, m // 2, :, pl.ds(OFF * n, OFF), :], kv_out.at[pair, mine],
            ksend.at[n, which, m], krecv.at[pair, core], 2 * goal[n] + which, side + m,
        )

    def q_push(n, k, m):
        return push(
            query.at[m, :, :, pl.ds(OFF * n + HALF * k, HALF), :], query_out.at[:, pair, mine],
            qsend.at[n, k, m], qrecv.at[pair, core], 2 * goal[n] + k, side + m,
        )

    def is_here(n, k, m):
        return jnp.logical_and(goal[n] == pair, jnp.logical_and(core == k, y == m))

    cos = cosine[...]
    sin = sine[...]
    for which in range(2):
        out = product(lambda cut: kv_weight[which, cut, :])
        for h in range(2):
            x = out[:, h * HS : (h + 1) * HS]
            kv[which, h] = rotated(x, cos, sin) if which == 0 else x.astype(
                jnp.bfloat16
            ).reshape(2, HS, HS)
        for m in range(4):
            for n in range(2):

                @pl.when(is_here(n, which, m))
                def _():
                    pltpu.make_async_copy(
                        kv.at[which, m // 2, :, pl.ds(OFF * n, OFF), :], kv_out.at[pair, mine],
                        krecv.at[pair, core],
                    ).start()

                @pl.when(jnp.logical_not(is_here(n, which, m)))
                def _():
                    kv_push(n, which, m).start()

    for m0 in range(4):
        m = add4(y, m0)
        shared(m0)
        out = product(
            lambda cut: jnp.concatenate([weight[0, m, cut], weight[1, m, cut]], axis=1)
        )
        for h in range(2):
            query[m, h] = rotated(out[:, h * HS : (h + 1) * HS], cos, sin)
        for n in range(2):
            for k in range(2):
                if m0 == 0:
                    here = jnp.logical_and(goal[n] == pair, core == k)

                    @pl.when(here)
                    def _():
                        pltpu.make_async_copy(
                            query.at[m, :, :, pl.ds(OFF * n + HALF * k, HALF), :],
                            query_out.at[:, pair, mine], qrecv.at[pair, core],
                        ).start()

                    @pl.when(jnp.logical_not(here))
                    def _():
                        q_push(n, k, m).start()

                else:
                    q_push(n, k, m).start()

    for e in range(PAIRS):
        for a in range(2):
            two = pl.ds(2 * a, 2)
            ref = kv_out.at[e, two]
            push(ref, ref, ksend.at[0, 0, 0], krecv.at[e, a], sibling, t).wait_recv()
            ref = query_out.at[:, e, two]
            push(ref, ref, qsend.at[0, 0, 0], qrecv.at[e, a], sibling, t).wait_recv()
    for n in range(4):
        keep(n).wait()
        push(
            rows_out.at[1 - core, n], rows_out.at[1 - core, n], osend.at[n], orecv.at[n], sibling, t
        ).wait_recv()
        give(n).wait_send()
    pltpu.make_async_copy(
        incoming.at[pl.ds(0, devices - 1)], incoming.at[pl.ds(0, devices - 1)], fr_send
    ).wait()
    for m in range(14):
        wmove(m).wait_send()
    for n in range(4):
        share(n).wait_send()
        row_block(n, 1).wait_send()
        if n:
            row_block(n, 0).wait_send()
    for d in range(1, N_TP):
        gain_block(d).wait_send()
    for n in range(2):
        for k in range(2):
            for m in range(4):

                @pl.when(jnp.logical_not(is_here(n, k, m)))
                def _():
                    kv_push(n, k, m).wait_send()
                    q_push(n, k, m).wait_send()


def intake(
    text_embed, norm_gain, frame_features, frame_positions, span_order, tables,
    projector, query_weight, key_weight, value_weight,
):
    tok_rows, part = text_embed.shape
    depth = query_weight.shape[0]
    devices = N_CTX * N_TP
    vm = pl.BlockSpec(memory_space=pltpu.VMEM)
    anywhere = pl.BlockSpec(memory_space=pl.ANY)
    dma = pltpu.SemaphoreType.DMA
    bf16 = jnp.bfloat16
    return pl.pallas_call(
        intake_kernel,
        out_shape=(
            jax.ShapeDtypeStruct((2, 4, 2, OFF, part), bf16),
            jax.ShapeDtypeStruct((2, PAIRS, 4, HALF, HS), bf16),
            jax.ShapeDtypeStruct((PAIRS, 4, OFF, HS), bf16),
        ),
        in_specs=[vm] * 9 + [anywhere] * 4,
        out_specs=(vm, vm, vm),
        scratch_shapes=[
            pltpu.VMEM((N_TP, projector.shape[0], 4 * HS), bf16),
            pltpu.VMEM((N_TP, N_CTX, 2 * CAP, 2 * HS), bf16),
            pltpu.VMEM((devices, 2 * CAP, 2 * HS), bf16),
            pltpu.VMEM((2, 4, HS, part), bf16),
            pltpu.VMEM((N_TP, 2, HS, part), bf16),
            pltpu.VMEM((N_TP, 16, part), bf16),
            pltpu.VMEM((N_TP, 2 * HS, part), bf16),
            pltpu.VMEM((2, 4, depth, HS), bf16),
            pltpu.VMEM((2, depth, 2 * HS), bf16),
            pltpu.VMEM((4, 2, 2, HS, HS), bf16),
            pltpu.VMEM((2, 2, 2, HS, HS), bf16),
            dma((N_TP,)),
            dma,
            dma((2,)),
            dma,
            dma,
            dma((14,)),
            dma((14,)),
            dma((4,)),
            dma((4,)),
            dma((4, 2)),
            dma((N_TP,)),
            dma((N_TP,)),
            dma((N_TP,)),
            dma((4,)),
            dma((4,)),
            dma((4,)),
            dma((2, 2, 4)),
            dma((PAIRS, 2)),
            dma((2, 2, 4)),
            dma((PAIRS, 2)),
        ],
        compiler_params=pltpu.CompilerParams(
            collective_id=1, has_side_effects=True, vmem_limit_bytes=48 * 2**20
        ),
        name="intake",
    )(
        text_embed.reshape(2, 4, HS, part),
        jnp.broadcast_to(norm_gain[None, :], (16, part)),
        frame_features,
        frame_positions.reshape(1, -1),
        frame_positions.reshape(-1, 1),
        span_order.reshape(1, -1),
        span_order.reshape(-1, 1),
        *tables,
        projector,
        query_weight,
        key_weight,
        value_weight,
    )


def attention_kernel(
    slot_of, query, kv_own, out_weight, out, gathered,
    kv, q, summed, largest, total, limit, send, recv, pass_send, wsend, wrecv, own_sem,
):
    scale = LOG2E / math.sqrt(HS)
    c = lax.axis_index("ctx")
    t = lax.axis_index("tp")
    pair = c // 2
    core = c % 2
    sibling = c + 1 - 2 * core
    base = pair // 4 * 4
    other = 4 - base
    z = pair % 4
    up = lax.rem(z + 1, 4)
    down = lax.rem(z + 3, 4)
    far = lax.rem(z + 2, 4)
    z_up, z_down, z_far = base + up, base + down, base + far
    x_own, x_up, x_down, x_far = other + z, other + up, other + down, other + far

    y = lax.rem(t, 4)
    side = t - y
    across = 4 - side
    t_up, t_down, t_far = (side + add4(y, n) for n in (1, 3, 2))
    a_own, a_up, a_down, a_far = (across + add4(y, n) for n in (0, 1, 3, 2))
    x_next = 2 * x_own + core

    barrier = pltpu.get_barrier_semaphore()
    signal(barrier, sibling, t)
    for e in (z_up, z_down, z_far, x_own):
        signal(barrier, 2 * e + core, t)
    signal(barrier, x_next, a_own)
    for j in (t_up, t_down, t_far):
        signal(barrier, c, j)
    for j in range(32):
        kv[pair, core, j * OFF : (j + 1) * OFF] = kv_own[slot_of[j]]
    pl.semaphore_wait(barrier, 9)

    cols = gathered.shape[-1]
    quarter_rows = gathered.shape[1] // 4
    own_weight = out_weight.at[:, pl.ds(pl.multiple_of(cols * core, HS), cols)]

    def quarter(ref, n):
        return ref.at[pl.ds(quarter_rows * n, quarter_rows)]

    def wmove(m):
        whole = lambda g: (gathered.at[g], gathered.at[g])
        part = lambda g: (quarter(gathered.at[g], z), quarter(gathered.at[g], z))
        src, dst, ctx, tp = (
            (own_weight, gathered.at[t], x_next, a_own),
            (own_weight, gathered.at[t], c, t_up),
            (own_weight, gathered.at[t], c, t_down),
            (quarter(own_weight, z), quarter(gathered.at[t], z), c, t_far),
            (*whole(a_own), c, t_up),
            (*whole(a_own), c, t_down),
            (*part(a_own), c, t_far),
            (*part(t_far), 2 * z_up + core, t),
            (*part(t_far), 2 * z_down + core, t),
            (*part(t_far), 2 * z_far + core, t),
            (*part(a_far), 2 * z_up + core, t),
            (*part(a_far), 2 * z_down + core, t),
            (*part(a_far), 2 * z_far + core, t),
        )[m]
        return push(src, dst, wsend.at[m], wrecv.at[m], ctx, tp)

    def warrive(m):
        ref = (
            gathered.at[a_own], gathered.at[t_down], gathered.at[t_up],
            quarter(gathered.at[t_far], z),
            gathered.at[a_down], gathered.at[a_up], quarter(gathered.at[a_far], z),
            quarter(gathered.at[t_far], down), quarter(gathered.at[t_far], up),
            quarter(gathered.at[t_far], far),
            quarter(gathered.at[a_far], down), quarter(gathered.at[a_far], up),
            quarter(gathered.at[a_far], far),
        )[m]
        push(ref, ref, wsend.at[m], wrecv.at[m], sibling, t).wait_recv()

    def transfer(e, to, index):
        block = kv.at[e, core]
        return push(block, block, send.at[index], recv.at[e, core], 2 * to + core, t)

    def share(e):
        block = kv.at[e, core]
        return push(block, block, pass_send.at[e], recv.at[e, core], sibling, t)

    def arrive(e, which):
        block = kv.at[e, which]
        push(block, block, send.at[0], recv.at[e, which], sibling, t).wait_recv()

    share(pair).start()
    moves = (
        (pair, x_own), (pair, z_up), (pair, z_down), (pair, z_far),
        (x_own, z_up), (x_own, z_down), (z_far, x_own),
    )
    for index in range(3):
        transfer(*moves[index], index).start()
    for m in (0, 3, 1, 2):
        wmove(m).start()
    own_copy = pltpu.make_async_copy(own_weight, gathered.at[t], own_sem)
    own_copy.start()
    for j in range(32):
        q[j * OFF : (j + 1) * OFF] = query[:, slot_of[j]].reshape(2 * HALF, HS)

    rows = 8 * HALF
    row = lax.broadcasted_iota(jnp.int32, (rows, 1), 0)
    col = lax.broadcasted_iota(jnp.int32, (1, 4 * OFF), 1)

    def starts(index, i, e):
        value = jnp.zeros(index.shape, jnp.int32)
        for a in range(4):
            kind = class_of(slot_of[4 * i + a] // 4, e)
            start = a * CH + HS * lax.rem(kind, 4) + OFF * (kind // 4)
            value = jnp.where(index // OFF == a, start, value)
        return value

    for i in range(8):
        limit[i * rows : (i + 1) * rows] = (
            starts(row, i, pair) + HALF * core + row % HALF
        )

    def update(e, first):
        for i in range(8):
            at = starts(col, i, e) + col % OFF
            here = slice(i * rows, (i + 1) * rows)
            width = 4 * OFF * (i + 1)
            s = lax.dot_general(
                q[here], kv[e, 0, :width], (((1,), (1,)), ((), ())),
                preferred_element_type=jnp.float32,
            )
            edge = jnp.where(at <= limit[here], s[:, width - 4 * OFF :], -1e30)
            s = edge if i == 0 else jnp.concatenate([s[:, : width - 4 * OFF], edge], axis=1)
            top = jnp.max(s, axis=1, keepdims=True)
            if not first:
                top = jnp.maximum(top, largest[here])
            weights = jnp.exp2((s - top) * scale)
            added = jnp.sum(weights, axis=1, keepdims=True)
            product = jnp.dot(
                weights.astype(jnp.bfloat16), kv[e, 1, :width], preferred_element_type=jnp.float32
            )
            if not first:
                factor = jnp.exp2((largest[here] - top) * scale)
                added = added + total[here] * factor
                product = product + summed[here] * factor
            largest[here] = top
            total[here] = added
            summed[here] = product

    arrive(pair, 1 - core)
    update(pair, True)
    transfer(*moves[3], 3).start()
    arrive(x_own, core)
    transfer(*moves[4], 4).start()
    transfer(*moves[5], 5).start()
    share(x_own).start()
    arrive(z_up, core)
    share(z_up).start()
    arrive(z_down, core)
    share(z_down).start()

    order = (x_own, z_up, z_down, x_up, x_down, z_far, x_far)

    def step(n, unused):
        e = order[6]
        for index in range(6):
            e = jnp.where(n == index, order[index], e)

        @pl.when(n == 2)
        def _():
            warrive(3)
            for m in (7, 8, 9):
                wmove(m).start()
            arrive(x_up, core)
            share(x_up).start()

        @pl.when(n == 3)
        def _():
            arrive(x_down, core)
            share(x_down).start()
            arrive(z_far, core)
            transfer(*moves[6], 6).start()
            share(z_far).start()

        @pl.when(n == 4)
        def _():
            warrive(0)
            for m in (6, 4, 5):
                wmove(m).start()

        @pl.when(n == 6)
        def _():
            arrive(x_far, core)
            share(x_far).start()

        arrive(e, 1 - core)
        update(e, False)
        return unused

    lax.fori_loop(0, 7, step, 0)
    for i in range(8):
        here = slice(i * rows, (i + 1) * rows)
        attended = (summed[here] / total[here]).astype(jnp.bfloat16).reshape(4, 2, HALF, HS)
        for a in range(4):
            out[4 * i + a] = jnp.concatenate([attended[a, 0], attended[a, 1]], axis=1)
    warrive(6)
    for m in (10, 11, 12):
        wmove(m).start()
    for m in (1, 2, 4, 5, 7, 8, 9, 10, 11, 12):
        warrive(m)
    own_copy.wait()
    for index in range(7):
        transfer(*moves[index], index).wait_send()
    for e in range(PAIRS):
        share(e).wait_send()
    for m in range(13):
        wmove(m).wait_send()


def attention(slot_of, query, kv, out_weight):
    anywhere = pl.BlockSpec(memory_space=pl.ANY)
    depth, width = out_weight.shape
    vm = pl.BlockSpec(memory_space=pltpu.VMEM)
    sm = pl.BlockSpec(memory_space=pltpu.SMEM)
    keys = 32 * OFF
    return pl.pallas_call(
        attention_kernel,
        out_shape=(
            jax.ShapeDtypeStruct((32, HALF, 2 * HS), jnp.bfloat16),
            jax.ShapeDtypeStruct((N_TP, depth, width // 2), jnp.bfloat16),
        ),
        in_specs=[sm, vm, vm, anywhere],
        out_specs=(vm, anywhere),
        scratch_shapes=[
            pltpu.VMEM((PAIRS, 2, keys, HS), jnp.bfloat16),
            pltpu.VMEM((keys, HS), jnp.bfloat16),
            pltpu.VMEM((keys, HS), jnp.float32),
            pltpu.VMEM((keys, 1), jnp.float32),
            pltpu.VMEM((keys, 1), jnp.float32),
            pltpu.VMEM((keys, 1), jnp.int32),
            pltpu.SemaphoreType.DMA((7,)),
            pltpu.SemaphoreType.DMA((PAIRS, 2)),
            pltpu.SemaphoreType.DMA((PAIRS,)),
            pltpu.SemaphoreType.DMA((13,)),
            pltpu.SemaphoreType.DMA((13,)),
            pltpu.SemaphoreType.DMA,
        ],
        compiler_params=pltpu.CompilerParams(
            collective_id=4, has_side_effects=True, vmem_limit_bytes=48 * 2**20
        ),
        name="attention",
    )(slot_of, query, kv, out_weight)


def out_kernel(
    span_order, attended, out_weight, rows, out, sorted_heads, heads, weight, product, result,
    wsem, hsend, hrecv, fsend, frecv, rsend, rrecv,
):
    c = lax.axis_index("ctx")
    t = lax.axis_index("tp")
    pair = c // 2
    core = c % 2
    sibling = c + 1 - 2 * core
    side = t // 4
    parts = N_TP // 2

    def load(g):
        return pltpu.make_async_copy(out_weight.at[g], weight.at[g], wsem.at[g])

    for g in range(N_TP):
        load(g).start()

    own = t == 0
    home = side == core
    origin = pair_of(pair, t)
    barrier = pltpu.get_barrier_semaphore()
    signal(barrier, sibling, t)
    for d in range(N_TP):
        j = lax.rem(t + d, N_TP)
        if d == 0:

            @pl.when(jnp.logical_not(own))
            def _():
                signal(barrier, 2 * origin + core, j)

            @pl.when(jnp.logical_not(home))
            def _():
                signal(barrier, 2 * pair + side, j)

        else:
            signal(barrier, 2 * origin + core, j)
            signal(barrier, 2 * pair + side, j)
    for j in range(32):
        sorted_heads[j] = attended[span_order[j]]
    pl.semaphore_wait(
        barrier, 1 + PAIRS - jnp.where(own, 1, 0) + 2 * parts - jnp.where(home, 1, 0)
    )

    mine = pl.ds(core * HALF, HALF)
    theirs = pl.ds((1 - core) * HALF, HALF)

    def gather(d):
        e = lax.rem(pair + d, PAIRS)
        return push(
            sorted_heads.at[pl.ds(4 * e, 4)], heads.at[t, :, mine, :], hsend.at[d], hrecv.at[t],
            2 * e + core, class_of(e, pair),
        )

    @pl.when(own)
    def _():
        pltpu.make_async_copy(
            sorted_heads.at[pl.ds(4 * pair, 4)], heads.at[t, :, mine, :], hrecv.at[t]
        ).start()

    @pl.when(jnp.logical_not(own))
    def _():
        gather(0).start()

    for d in range(1, PAIRS):
        gather(d).start()

    def forward(j):
        return push(
            heads.at[j, :, mine, :], heads.at[j, :, mine, :], fsend.at[j], frecv.at[j], sibling, t
        )

    for d in range(N_TP):
        j = lax.rem(t + d, N_TP)
        push(
            heads.at[j, :, mine, :], heads.at[j, :, mine, :], hsend.at[0], hrecv.at[j], sibling, t
        ).wait_recv()
        forward(j).start()
    for j in range(N_TP):
        push(
            heads.at[j, :, theirs, :], heads.at[j, :, theirs, :], fsend.at[j], frecv.at[j],
            sibling, t,
        ).wait_recv()
    for g in range(N_TP):
        load(g).wait()

    part = out.shape[-1]

    place = HS * lax.rem(t, 4) + OFF * side

    def send_home(j, a):
        return push(
            result.at[j, a], out.at[:, pl.ds(place, OFF), :], rsend.at[j, a], rrecv.at[t],
            2 * pair + a, parts * core + j,
        )

    def is_home(j, a):
        return jnp.logical_and(home, jnp.logical_and(a == core, parts * core + j == t))

    block = 2 * HS

    def project(n):
        total = jnp.zeros((4 * OFF, block), jnp.float32)
        for g in range(N_TP):
            x = heads[g].reshape(4 * OFF, 2 * HS)
            total = total + jnp.dot(
                x, weight[g, :, n * block : (n + 1) * block], preferred_element_type=jnp.float32
            ).astype(jnp.bfloat16).astype(jnp.float32)
        product[:, n * block : (n + 1) * block] = total

    ready = 0
    for j in range(parts):
        while ready * block < (j + 1) * part:
            project(ready)
            ready += 1
        start = j * part // HS * HS
        shift = j * part - start
        window = -(-(part + shift) // HS) * HS
        total = product[:, start : start + window]
        if shift:
            total = pltpu.roll(total, window - shift, 1)
        total = total[:, :part]
        for a in range(2):
            placed = rows[a, j].reshape(2 * OFF, part).astype(jnp.float32)
            result[j, a] = (placed + total[a * 2 * OFF : (a + 1) * 2 * OFF]).astype(
                jnp.bfloat16
            ).reshape(2, OFF, part)

            @pl.when(is_home(j, a))
            def _():
                pltpu.make_async_copy(
                    result.at[j, a], out.at[:, pl.ds(place, OFF), :], rrecv.at[t]
                ).start()

            @pl.when(jnp.logical_not(is_home(j, a)))
            def _():
                send_home(j, a).start()

    for e in range(PAIRS):
        push(
            result.at[0, 0], out.at[:, pl.ds(OFF * e, OFF), :], rsend.at[0, 0], rrecv.at[e],
            sibling, t,
        ).wait_recv()

    @pl.when(jnp.logical_not(own))
    def _():
        gather(0).wait_send()

    for d in range(1, PAIRS):
        gather(d).wait_send()
    for j in range(N_TP):
        forward(j).wait_send()
    for j in range(parts):
        for a in range(2):

            @pl.when(jnp.logical_not(is_home(j, a)))
            def _():
                send_home(j, a).wait_send()


def out_exchange(span_order, attended, out_weight, rows):
    part = rows.shape[-1]
    parts = N_TP // 2
    vm = pl.BlockSpec(memory_space=pltpu.VMEM)
    anywhere = pl.BlockSpec(memory_space=pl.ANY)
    return pl.pallas_call(
        out_kernel,
        out_shape=jax.ShapeDtypeStruct((2, CH, part), jnp.bfloat16),
        in_specs=[pl.BlockSpec(memory_space=pltpu.SMEM), vm, anywhere, vm],
        out_specs=vm,
        scratch_shapes=[
            pltpu.VMEM((32, HALF, 2 * HS), jnp.bfloat16),
            pltpu.VMEM((N_TP, 4, OFF, 2 * HS), jnp.bfloat16),
            pltpu.VMEM(out_weight.shape, jnp.bfloat16),
            pltpu.VMEM((4 * OFF, parts * part), jnp.float32),
            pltpu.VMEM((parts, 2, 2, OFF, part), jnp.bfloat16),
            pltpu.SemaphoreType.DMA((N_TP,)),
            pltpu.SemaphoreType.DMA((N_TP,)),
            pltpu.SemaphoreType.DMA((N_TP,)),
            pltpu.SemaphoreType.DMA((N_TP,)),
            pltpu.SemaphoreType.DMA((N_TP,)),
            pltpu.SemaphoreType.DMA((parts, 2)),
            pltpu.SemaphoreType.DMA((PAIRS,)),
        ],
        compiler_params=pltpu.CompilerParams(
            collective_id=3, has_side_effects=True, vmem_limit_bytes=40 * 2**20
        ),
        name="out",
    )(span_order, attended, out_weight, rows)


def per_device(
    text_embed,
    frame_features,
    frame_positions,
    span_order,
    projector,
    norm_gain,
    query_weight,
    key_weight,
    value_weight,
    out_weight,
):
    tok_rows, part = text_embed.shape
    c = lax.axis_index("ctx")
    t = lax.axis_index("tp")
    slots = span_order.shape[0]
    index = jnp.arange(slots, dtype=jnp.int32)
    slot_of = jnp.sum(
        jnp.where(span_order[None, :] == index[:, None], index[None, :], 0), axis=1
    )
    spans = lax.dynamic_slice_in_dim(span_order, 2 * c, 2, 0)
    positions = (
        spans[:, None] * CH + HS * (t % 4) + jnp.arange(HS, dtype=jnp.int32)[None, :]
    ).reshape(-1)
    half = HS // 2
    freqs = 1000000.0 ** (-(jnp.arange(half, dtype=jnp.float32) * 2.0 / HS))
    angles = positions.astype(jnp.float32)[:, None] * freqs[None, :]
    cos = jnp.cos(angles)
    sin = jnp.sin(angles)
    cosine = jnp.concatenate([cos, cos], axis=1)
    sine = jnp.concatenate([-sin, sin], axis=1)
    rows, query, kv = intake(
        text_embed, norm_gain, frame_features, frame_positions, span_order, (cosine, sine),
        projector, query_weight, key_weight, value_weight,
    )
    attended, gathered = attention(
        slot_of, query.reshape(2, 32, HALF, HS), kv.reshape(32, OFF, HS), out_weight
    )
    mixed = out_exchange(span_order, attended, gathered, rows)
    return mixed.reshape(tok_rows, part)


def solution(mesh):
    in_specs = (
        P("ctx", "tp"),
        P(("ctx", "tp"), None),
        P(("ctx", "tp")),
        P(),
        P(),
        P("tp"),
        P(None, "tp"),
        P(),
        P(),
        P("tp", None),
    )
    out_specs = P("ctx", "tp")
    return jax.shard_map(
        per_device, mesh=mesh, in_specs=in_specs, out_specs=out_specs, check_vma=False
    )
```

```python
import functools
import math

import jax
import jax.numpy as jnp
from jax import lax
from jax.experimental import pallas as pl
from jax.experimental.pallas import tpu as pltpu
from jax.sharding import PartitionSpec as P

HS = 128
KVH = 4
CAP = 8
CH = 512
N_CTX = 16
N_TP = 8
PAIRS = 8
OFF = 64
HALF = 32
MESH = pl.DeviceIdType.MESH
LOG2E = math.log2(math.e)


def signal(sem, ctx, tp):
    pl.semaphore_signal(sem, inc=1, device_id=(ctx, tp), device_id_type=MESH)


def push(src, dst, send_sem, recv_sem, ctx, tp):
    return pltpu.make_async_remote_copy(
        src_ref=src, dst_ref=dst, send_sem=send_sem, recv_sem=recv_sem,
        device_id=(ctx, tp), device_id_type=MESH,
    )


def add4(a, b):
    return lax.rem(a + b + 4, 4)


def pair_of(e, t):
    return lax.rem(e // 4 + t // 4, 2) * 4 + add4(lax.rem(e, 4), lax.rem(t, 4))


def class_of(e, pair):
    return lax.rem(e // 4 + pair // 4, 2) * 4 + add4(lax.rem(pair, 4), -lax.rem(e, 4))


def intake_kernel(
    text, gain, features, pos_row, pos_col, order_row, order_col, cosine, sine,
    projector, query_weight, key_weight, value_weight,
    rows_out, query_out, kv_out,
    pweight, outgoing, incoming, placed, rows, gains, normed, weight, kv_weight, query, kv,
    psem, own_sem, kv_sem, fr_send, fr_recv, wsend, wrecv, csend, crecv,
    send, recv, gsend, grecv, osem, qsend, qrecv, ksend, krecv,
):
    c = lax.axis_index("ctx")
    t = lax.axis_index("tp")
    pair = c // 2
    core = c % 2
    sibling = c + 1 - 2 * core
    devices = N_CTX * N_TP
    me = c * N_TP + t
    part = text.shape[-1]
    width = N_TP * part
    base = pair // 4 * 4
    z = pair % 4
    z_up, z_down, z_far = (base + add4(z, n) for n in (1, 3, 2))
    y = lax.rem(t, 4)
    side = t - y
    half = t // 4
    y_up, y_down, y_far = (add4(y, n) for n in (1, 3, 2))

    own_copy = pltpu.make_async_copy(
        query_weight.at[:, pl.ds(pl.multiple_of(HS * core, HS), HS)], weight.at[core, y], own_sem
    )
    own_copy.start()
    block = 4 * HS

    def load(d):
        j = lax.rem(t + d, N_TP)
        start = pl.multiple_of((j * part) // HS * HS, HS)
        return pltpu.make_async_copy(
            projector.at[:, pl.ds(start, block)], pweight.at[d], psem.at[d]
        )

    for d in range(N_TP):
        load(d).start()
    kv_cols = pl.ds(pl.multiple_of(2 * HS * half, HS), 2 * HS)
    kv_loads = [
        pltpu.make_async_copy(ref.at[:, kv_cols], kv_weight.at[n], kv_sem.at[n])
        for n, ref in enumerate((key_weight, value_weight))
    ]
    for one in kv_loads:
        one.start()

    barrier = pltpu.get_barrier_semaphore()

    def greet(d, unused):
        other = lax.rem(me + d, devices)
        signal(barrier, other // N_TP, lax.rem(other, N_TP))
        return unused

    lax.fori_loop(1, devices, greet, 0)

    f32 = jnp.float32
    spans = order_row.shape[1]
    tokens = pos_row.shape[1]
    entries = N_CTX * CAP
    slot_row = jnp.sum(
        jnp.where(
            order_col[...] == pos_row[...] // CH,
            lax.broadcasted_iota(jnp.int32, (spans, tokens), 0).astype(f32), 0.0,
        ),
        axis=0, keepdims=True,
    ).astype(jnp.int32)
    slot_col = jnp.sum(
        jnp.where(
            order_row[...] == pos_col[...] // CH,
            lax.broadcasted_iota(jnp.int32, (tokens, spans), 1).astype(f32), 0.0,
        ),
        axis=1, keepdims=True,
    ).astype(jnp.int32)
    first = lax.broadcasted_iota(jnp.int32, (tokens, tokens), 0)
    second = lax.broadcasted_iota(jnp.int32, (tokens, tokens), 1)
    earlier = jnp.logical_and(slot_col // 2 == slot_row // 2, first < second)
    place = jnp.sum(jnp.where(earlier, 1.0, 0.0), axis=0, keepdims=True).astype(jnp.int32)
    entry = slot_row // 2 * CAP + place
    chosen = lax.broadcasted_iota(jnp.int32, (entries, tokens), 0) == entry
    ordered = jnp.dot(
        jnp.where(chosen, 1.0, 0.0).astype(jnp.bfloat16), features[...],
        preferred_element_type=f32,
    ).astype(jnp.bfloat16)
    token_row = (slot_row % 2 * CH + pos_row[...] % CH + 1).astype(f32)
    row_at = jnp.sum(jnp.where(chosen, token_row, 0.0), axis=1, keepdims=True) - 1.0
    row_at = row_at.astype(jnp.int32)
    high = (row_at >> 5).astype(f32)
    low = (row_at & 31).astype(f32)
    lane = lax.broadcasted_iota(jnp.int32, (entries, block), 1)
    tail = jnp.where(lane < part + 32, high, jnp.where(lane < part + 48, low, 1.0))

    pl.semaphore_wait(barrier, devices - 1)

    depth = weight.shape[2]
    direct = pl.ds(0, depth // 2)

    def eighth(n):
        return pl.ds(depth // 2 + depth // 8 * n, depth // 8)

    def quarter(n):
        return pl.ds(depth // 4 * n, depth // 4)

    def wmove(m):
        if m < 5:
            cut, tp = (
                (direct, y_up), (direct, y_down), (eighth(z), y_up), (eighth(z), y_down),
                (quarter(z), y_far),
            )[m]
            ref, ctx, tp = weight.at[core, y, cut], c, side + tp
        else:
            n = m - 5
            cut = quarter(z) if n // 3 == 2 else eighth(z)
            ref, tp = weight.at[core, (y_up, y_down, y_far)[n // 3], cut], t
            ctx = 2 * (z_up, z_down, z_far)[n % 3] + core
        return push(ref, ref, wsend.at[m], wrecv.at[m], ctx, tp)

    def warrive(m):
        if m < 5:
            shard = (y_down, y_up, y_down, y_up, y_far)[m]
            cut = (direct, direct, eighth(z), eighth(z), quarter(z))[m]
        else:
            n = m - 5
            shard = (y_up, y_down, y_far)[n // 3]
            origin = (add4(z, 3), add4(z, 1), add4(z, 2))[n % 3]
            cut = quarter(origin) if n // 3 == 2 else eighth(origin)
        ref = weight.at[core, shard, cut]
        push(ref, ref, wsend.at[m], wrecv.at[m], sibling, t).wait_recv()

    def share(n):
        ref = weight.at[core, add4(y, n)]
        return push(ref, ref, csend.at[n], crecv.at[n], sibling, t)

    def shared(n):
        ref = weight.at[1 - core, add4(y, n)]
        push(ref, ref, csend.at[n], crecv.at[n], sibling, t).wait_recv()

    own_copy.wait()
    for m in (4, 2, 3, 0, 1):
        wmove(m).start()
    share(0).start()

    for d in range(N_TP):
        j = lax.rem(t + d, N_TP)
        load(d).wait()
        x = jnp.dot(ordered, pweight[d], preferred_element_type=f32)
        x = 0.5 * x * (1.0 + lax.erf(x * math.sqrt(0.5)))
        shift = j * part - (j * part) // HS * HS
        x = jnp.where(shift > 0, pltpu.roll(x, block - HS // 2, 1), x)
        x = jnp.where(lane < part, x, tail)
        halves = [
            x[:, n * 2 * HS : (n + 1) * 2 * HS].reshape(N_CTX, CAP, 2 * HS) for n in range(2)
        ]
        outgoing[d] = jnp.concatenate(halves, axis=1).astype(jnp.bfloat16)

        def deliver(n, unused):
            oc = lax.rem(c + n, N_CTX)
            push(outgoing.at[d, oc], incoming.at[me], fr_send, fr_recv, oc, j).start()
            return unused

        if d == 0:
            pltpu.make_async_copy(outgoing.at[0, c], incoming.at[me], fr_recv).start()
        else:
            push(outgoing.at[d, c], incoming.at[me], fr_send, fr_recv, c, j).start()
        lax.fori_loop(1, N_CTX, deliver, 0)

    for m in (2, 3, 4):
        warrive(m)
    for m in range(5, 14):
        wmove(m).start()
    pltpu.make_async_copy(incoming, incoming, fr_recv).wait()

    def row_block(n, across):
        j = add4(y, n)
        tp = j + (4 - side if across else side)
        return push(
            placed.at[:, j], rows.at[t], send.at[n, across], recv.at[t], c, tp
        )

    def gain_block(d):
        return push(gain, gains.at[t], gsend.at[d], grecv.at[t], c, lax.rem(t + d, N_TP))

    pltpu.make_async_copy(gain, gains.at[t], grecv.at[t]).start()
    for d in range(1, N_TP):
        gain_block(d).start()
    arrived = incoming[...].astype(f32)
    slots = devices * CAP
    left = arrived[:, :CAP].reshape(slots, 2 * HS)
    right = arrived[:, CAP:].reshape(slots, 2 * HS)
    edge = part - 2 * HS
    at = right[:, edge : edge + 1] * 32.0 + right[:, edge + 32 : edge + 33]
    at = jnp.transpose(jnp.broadcast_to(at, (slots, HS)))[0:1, :]
    left = left.astype(jnp.bfloat16)
    right = right.astype(jnp.bfloat16)
    group = 2 * HS
    offset = lax.broadcasted_iota(jnp.int32, (group, 1), 0)
    offset = offset // HS * CH + offset % HS
    for n in range(4):
        j = add4(y, n)
        row = offset + j * HS
        hit = jnp.where(row.astype(f32) == at, 1.0, 0.0).astype(jnp.bfloat16)
        new_left = jnp.dot(hit, left, preferred_element_type=f32)
        new_right = jnp.dot(hit, right, preferred_element_type=f32)
        framed = new_right[:, 2 * HS - 1 :] > 0.5
        old = text[:, j].reshape(group, part).astype(f32)
        placed[:, j, :, : 2 * HS] = (
            jnp.where(framed, new_left, old[:, : 2 * HS]).astype(jnp.bfloat16)
        ).reshape(2, HS, 2 * HS)
        placed[:, j, :, 2 * HS :] = (
            jnp.where(framed, new_right[:, :edge], old[:, 2 * HS :]).astype(jnp.bfloat16)
        ).reshape(2, HS, edge)
        row_block(n, 1).start()
        if n == 0:
            pltpu.make_async_copy(placed.at[:, y], rows.at[t], recv.at[t]).start()
        else:
            row_block(n, 0).start()

    for m in (0, 1, *range(5, 14)):
        warrive(m)
    for n in range(1, 4):
        share(n).start()
    for one in kv_loads:
        one.wait()

    total = jnp.zeros((group, 1), f32)
    for d in range(N_TP):
        j = lax.rem(t + d, N_TP)
        push(gain, gains.at[j], gsend.at[0], grecv.at[j], sibling, t).wait_recv()
        push(rows.at[j], rows.at[j], send.at[0, 0], recv.at[j], sibling, t).wait_recv()
        x = rows[j].reshape(group, part).astype(f32)
        total = total + jnp.sum(x * x, axis=1, keepdims=True)

    keep = pltpu.make_async_copy(rows.at[pl.ds(side, 4)], rows_out, osem)
    keep.start()

    inverse = lax.rsqrt(total / width + 1e-06)
    for j in range(N_TP):
        x = rows[j].reshape(group, part).astype(f32)
        normed[j] = (x * inverse * gains[j, 0:1, :].astype(f32)).astype(jnp.bfloat16)

    def product(piece):
        total = None
        for j in range(N_TP):
            term = jnp.dot(
                normed[j], piece(slice(j * part, (j + 1) * part)), preferred_element_type=f32
            )
            total = term if total is None else total + term
        return total

    def rotated(x, cos, sin):
        return (x * cos + pltpu.roll(x, HS // 2, 1) * sin).astype(jnp.bfloat16).reshape(2, HS, HS)

    goal = [pair_of(pair, 4 * n + y) for n in range(2)]
    mine = pl.ds(2 * core, 2)

    def kv_push(n, which, m):
        return push(
            kv.at[which, m // 2, :, pl.ds(OFF * n, OFF), :], kv_out.at[pair, mine],
            ksend.at[n, which, m], krecv.at[pair, core], 2 * goal[n] + which, side + m,
        )

    def q_push(n, k, m):
        return push(
            query.at[m, :, :, pl.ds(OFF * n + HALF * k, HALF), :], query_out.at[:, pair, mine],
            qsend.at[n, k, m], qrecv.at[pair, core], 2 * goal[n] + k, side + m,
        )

    def is_here(n, k, m):
        return jnp.logical_and(goal[n] == pair, jnp.logical_and(core == k, y == m))

    cos = cosine[...]
    sin = sine[...]
    for which in range(2):
        out = product(lambda cut: kv_weight[which, cut, :])
        for h in range(2):
            x = out[:, h * HS : (h + 1) * HS]
            kv[which, h] = rotated(x, cos, sin) if which == 0 else x.astype(
                jnp.bfloat16
            ).reshape(2, HS, HS)
        for m in range(4):
            for n in range(2):

                @pl.when(is_here(n, which, m))
                def _():
                    pltpu.make_async_copy(
                        kv.at[which, m // 2, :, pl.ds(OFF * n, OFF), :], kv_out.at[pair, mine],
                        krecv.at[pair, core],
                    ).start()

                @pl.when(jnp.logical_not(is_here(n, which, m)))
                def _():
                    kv_push(n, which, m).start()

    for m0 in range(4):
        m = add4(y, m0)
        shared(m0)
        out = product(
            lambda cut: jnp.concatenate([weight[0, m, cut], weight[1, m, cut]], axis=1)
        )
        for h in range(2):
            query[m, h] = rotated(out[:, h * HS : (h + 1) * HS], cos, sin)
        for n in range(2):
            for k in range(2):
                if m0 == 0:
                    here = jnp.logical_and(goal[n] == pair, core == k)

                    @pl.when(here)
                    def _():
                        pltpu.make_async_copy(
                            query.at[m, :, :, pl.ds(OFF * n + HALF * k, HALF), :],
                            query_out.at[:, pair, mine], qrecv.at[pair, core],
                        ).start()

                    @pl.when(jnp.logical_not(here))
                    def _():
                        q_push(n, k, m).start()

                else:
                    q_push(n, k, m).start()

    for e in range(PAIRS):
        for a in range(2):
            two = pl.ds(2 * a, 2)
            ref = kv_out.at[e, two]
            push(ref, ref, ksend.at[0, 0, 0], krecv.at[e, a], sibling, t).wait_recv()
            ref = query_out.at[:, e, two]
            push(ref, ref, qsend.at[0, 0, 0], qrecv.at[e, a], sibling, t).wait_recv()
    keep.wait()
    pltpu.make_async_copy(
        incoming.at[pl.ds(0, devices - 1)], incoming.at[pl.ds(0, devices - 1)], fr_send
    ).wait()
    for m in range(14):
        wmove(m).wait_send()
    for n in range(4):
        share(n).wait_send()
        row_block(n, 1).wait_send()
        if n:
            row_block(n, 0).wait_send()
    for d in range(1, N_TP):
        gain_block(d).wait_send()
    for n in range(2):
        for k in range(2):
            for m in range(4):

                @pl.when(jnp.logical_not(is_here(n, k, m)))
                def _():
                    kv_push(n, k, m).wait_send()
                    q_push(n, k, m).wait_send()


def intake(
    text_embed, norm_gain, frame_features, frame_positions, span_order, tables,
    projector, query_weight, key_weight, value_weight,
):
    tok_rows, part = text_embed.shape
    depth = query_weight.shape[0]
    devices = N_CTX * N_TP
    vm = pl.BlockSpec(memory_space=pltpu.VMEM)
    anywhere = pl.BlockSpec(memory_space=pl.ANY)
    dma = pltpu.SemaphoreType.DMA
    bf16 = jnp.bfloat16
    return pl.pallas_call(
        intake_kernel,
        out_shape=(
            jax.ShapeDtypeStruct((4, 2, HS, part), bf16),
            jax.ShapeDtypeStruct((2, PAIRS, 4, HALF, HS), bf16),
            jax.ShapeDtypeStruct((PAIRS, 4, OFF, HS), bf16),
        ),
        in_specs=[vm] * 9 + [anywhere] * 4,
        out_specs=(vm, vm, vm),
        scratch_shapes=[
            pltpu.VMEM((N_TP, projector.shape[0], 4 * HS), bf16),
            pltpu.VMEM((N_TP, N_CTX, 2 * CAP, 2 * HS), bf16),
            pltpu.VMEM((devices, 2 * CAP, 2 * HS), bf16),
            pltpu.VMEM((2, 4, HS, part), bf16),
            pltpu.VMEM((N_TP, 2, HS, part), bf16),
            pltpu.VMEM((N_TP, 16, part), bf16),
            pltpu.VMEM((N_TP, 2 * HS, part), bf16),
            pltpu.VMEM((2, 4, depth, HS), bf16),
            pltpu.VMEM((2, depth, 2 * HS), bf16),
            pltpu.VMEM((4, 2, 2, HS, HS), bf16),
            pltpu.VMEM((2, 2, 2, HS, HS), bf16),
            dma((N_TP,)),
            dma,
            dma((2,)),
            dma,
            dma,
            dma((14,)),
            dma((14,)),
            dma((4,)),
            dma((4,)),
            dma((4, 2)),
            dma((N_TP,)),
            dma((N_TP,)),
            dma((N_TP,)),
            dma,
            dma((2, 2, 4)),
            dma((PAIRS, 2)),
            dma((2, 2, 4)),
            dma((PAIRS, 2)),
        ],
        compiler_params=pltpu.CompilerParams(
            collective_id=1, has_side_effects=True, vmem_limit_bytes=48 * 2**20
        ),
        name="intake",
    )(
        text_embed.reshape(2, 4, HS, part),
        jnp.broadcast_to(norm_gain[None, :], (16, part)),
        frame_features,
        frame_positions.reshape(1, -1),
        frame_positions.reshape(-1, 1),
        span_order.reshape(1, -1),
        span_order.reshape(-1, 1),
        *tables,
        projector,
        query_weight,
        key_weight,
        value_weight,
    )


def attention_kernel(
    slot_of, span_order, query, kv_own, out_weight, rows, out,
    kv, q, summed, largest, limit, attended, heads, weight, product, result,
    send, recv, pass_send, wsend, wrecv, csend, crecv, own_sem,
    hsend, hrecv, rsend, rrecv,
):
    f32 = jnp.float32
    scale = LOG2E / math.sqrt(HS)
    c = lax.axis_index("ctx")
    t = lax.axis_index("tp")
    pair = c // 2
    core = c % 2
    sibling = c + 1 - 2 * core
    base = pair // 4 * 4
    other = 4 - base
    z = pair % 4
    up, down, far = (add4(z, n) for n in (1, 3, 2))
    z_up, z_down, z_far = base + up, base + down, base + far
    x_own, x_up, x_down, x_far = other + z, other + up, other + down, other + far
    y = lax.rem(t, 4)
    side = t - y
    half = t // 4
    across = 4 - side
    t_up, t_down, t_far = (side + add4(y, n) for n in (1, 3, 2))
    a_own, a_up, a_down, a_far = (across + add4(y, n) for n in (0, 1, 3, 2))
    x_next = 2 * x_own + core
    depth, cols = weight.shape[2:]

    def columns(of_half):
        return out_weight.at[:, pl.ds(pl.multiple_of(cols * (2 * of_half + core), HS), cols)]

    own_copy = pltpu.make_async_copy(columns(half), weight.at[core, t], own_sem)
    own_copy.start()
    barrier = pltpu.get_barrier_semaphore()
    signal(barrier, sibling, t)
    for e in (z_up, z_down, z_far, x_own):
        signal(barrier, 2 * e + core, t)
    signal(barrier, x_next, a_own)
    for j in (t_up, t_down, t_far):
        signal(barrier, c, j)
    first = y == 0
    for n in range(2):
        origin = pair_of(pair, 4 * n + y)
        for k in range(2):
            for d in range(N_TP):
                j = lax.rem(t + d, N_TP)
                if n == 0 and d == 0:

                    @pl.when(jnp.logical_not(jnp.logical_and(first, core == k)))
                    def _():
                        signal(barrier, 2 * origin + k, j)

                else:
                    signal(barrier, 2 * origin + k, j)
    for j in range(32):
        kv[pair, core, j * OFF : (j + 1) * OFF] = kv_own[slot_of[j]]
    pl.semaphore_wait(barrier, 9 + 32 - jnp.where(first, 1, 0))

    def quarter(ref, n):
        return ref.at[pl.ds(depth // 4 * n, depth // 4)]

    def wmove(m):
        own = weight.at[core, t]
        passed = weight.at[core, a_own]
        if m == 0:
            src, dst, ctx, tp = columns(1 - half), own, x_next, a_own
        elif m < 7:
            dst, tp = (
                (own, t_up), (own, t_down), (quarter(own, z), t_far),
                (passed, t_up), (passed, t_down), (quarter(passed, z), t_far),
            )[m - 1]
            src, ctx = dst, c
        else:
            n = m - 7
            dst = quarter(weight.at[core, (t_far, a_far)[n // 3]], z)
            src, tp, ctx = dst, t, 2 * (z_up, z_down, z_far)[n % 3] + core
        return push(src, dst, wsend.at[m], wrecv.at[m], ctx, tp)

    def warrive(m):
        if m < 7:
            ref = weight.at[core, (a_own, t_down, t_up, t_far, a_down, a_up, a_far)[m]]
            if m % 3 == 0 and m:
                ref = quarter(ref, z)
        else:
            n = m - 7
            ref = quarter(weight.at[core, (t_far, a_far)[n // 3]], (down, up, far)[n % 3])
        push(ref, ref, wsend.at[m], wrecv.at[m], sibling, t).wait_recv()

    def give(g):
        ref = weight.at[core, g]
        return push(ref, ref, csend.at[g], crecv.at[g], sibling, t)

    def transfer(e, to, index):
        block = kv.at[e, core]
        return push(block, block, send.at[index], recv.at[e, core], 2 * to + core, t)

    def share(e):
        block = kv.at[e, core]
        return push(block, block, pass_send.at[e], recv.at[e, core], sibling, t)

    def arrive(e, which):
        block = kv.at[e, which]
        push(block, block, send.at[0], recv.at[e, which], sibling, t).wait_recv()

    share(pair).start()
    moves = (
        (pair, x_own), (pair, z_up), (pair, z_down), (pair, z_far),
        (x_own, z_up), (x_own, z_down), (z_far, x_own),
    )
    for index in range(4):
        transfer(*moves[index], index).start()
    own_copy.wait()
    for m in (3, 1, 2):
        wmove(m).start()
    for j in range(32):
        q[j * OFF : (j + 1) * OFF] = query[:, slot_of[j]].reshape(2 * HALF, HS)

    group = 8 * HALF
    row = lax.broadcasted_iota(jnp.int32, (group, 1), 0)
    col = lax.broadcasted_iota(jnp.int32, (1, 4 * OFF), 1)

    def starts(index, i, e):
        value = jnp.zeros(index.shape, jnp.int32)
        for a in range(4):
            kind = class_of(slot_of[4 * i + a] // 4, e)
            start = a * CH + HS * lax.rem(kind, 4) + OFF * (kind // 4)
            value = jnp.where(index // OFF == a, start, value)
        return value

    for i in range(8):
        limit[i * group : (i + 1) * group] = starts(row, i, pair) + HALF * core + row % HALF

    def update(e, first_set):
        def chunk(i):
            return slice(i * group, (i + 1) * group), 4 * OFF * (i + 1)

        def scores(i):
            here, width = chunk(i)
            return lax.dot_general(
                q[here], kv[e, 0, :width], (((1,), (1,)), ((), ())), preferred_element_type=f32
            )

        def soft(i, s):
            here, width = chunk(i)
            at = starts(col, i, e) + col % OFF
            edge = jnp.where(at <= limit[here], s[:, width - 4 * OFF :], -1e30)
            s = edge if i == 0 else jnp.concatenate([s[:, : width - 4 * OFF], edge], axis=1)
            top = jnp.max(s, axis=1, keepdims=True)
            if not first_set:
                top = jnp.maximum(top, largest[here])
                summed[here] = summed[here] * jnp.exp2((largest[here] - top) * scale)
            largest[here] = top
            return jnp.exp2((s - top) * scale).astype(jnp.bfloat16)

        def gather(i, weights):
            here, width = chunk(i)
            beside = jnp.concatenate(
                [kv[e, 1, :width], jnp.ones((width, HS), jnp.bfloat16)], axis=1
            )
            new = jnp.dot(weights, beside, preferred_element_type=f32)
            summed[here] = new if first_set else summed[here] + new

        s = scores(0)
        held = None
        for i in range(8):
            ahead = scores(i + 1) if i < 7 else None
            weights = soft(i, s)
            if held is not None:
                gather(*held)
            held = (i, weights)
            s = ahead
        gather(*held)

    arrive(pair, 1 - core)
    update(pair, True)
    arrive(x_own, core)
    transfer(*moves[4], 4).start()
    transfer(*moves[5], 5).start()
    share(x_own).start()
    wmove(0).start()
    give(t).start()
    order = (x_own, z_up, z_down, z_far, x_up, x_down, x_far)

    def step(n, unused):
        e = order[6]
        for index in range(6):
            e = jnp.where(n == index, order[index], e)

        @pl.when(n == 1)
        def _():
            arrive(z_up, core)
            share(z_up).start()
            arrive(z_down, core)
            share(z_down).start()

        @pl.when(n == 2)
        def _():
            arrive(z_far, core)
            transfer(*moves[6], 6).start()
            share(z_far).start()
            warrive(3)
            for m in (7, 8, 9):
                wmove(m).start()

        @pl.when(n == 4)
        def _():
            warrive(0)
            for m in (6, 4, 5):
                wmove(m).start()
            give(a_own).start()
            arrive(x_up, core)
            share(x_up).start()
            arrive(x_down, core)
            share(x_down).start()

        @pl.when(n == 6)
        def _():
            arrive(x_far, core)
            share(x_far).start()
            warrive(6)
            for m in (10, 11, 12):
                wmove(m).start()

        arrive(e, 1 - core)
        update(e, False)
        return unused

    lax.fori_loop(0, 7, step, 0)

    for i in range(8):
        here = slice(i * group, (i + 1) * group)
        done = (summed[here, :HS] / summed[here, HS : HS + 1]).astype(jnp.bfloat16)
        done = done.reshape(4, 2, HALF, HS)
        for a in range(4):
            attended[0, 4 * i + a] = jnp.concatenate([done[a, 0], done[a, 1]], axis=1)

    def head_push(d, a, n):
        e = lax.rem(pair + d, PAIRS)
        kind = class_of(e, pair)
        at = pl.ds(OFF * (kind // 4) + HALF * core, HALF)
        return push(
            attended.at[1, pl.ds(4 * e + 2 * a, 2)], heads.at[t, :, at, :], hsend.at[d, a, n],
            hrecv.at[t, kind // 4, core], 2 * e + a, lax.rem(4 * n + lax.rem(kind, 4) + side, N_TP),
        )

    def is_here(d, a, n):
        if d or n:
            return jnp.bool_(False)
        return jnp.logical_and(first, core == a)

    for j in range(32):
        attended[1, j] = attended[0, span_order[j]]
    for d in range(PAIRS):
        for n in range(2):
            for a in range(2):
                if d or n:
                    head_push(d, a, n).start()
                else:

                    @pl.when(is_here(d, a, n))
                    def _():
                        pltpu.make_async_copy(
                            attended.at[1, pl.ds(4 * pair + 2 * a, 2)],
                            heads.at[t, :, pl.ds(HALF * core, HALF), :], hrecv.at[t, 0, core],
                        ).start()

                    @pl.when(jnp.logical_not(is_here(d, a, n)))
                    def _():
                        head_push(d, a, n).start()

    for m in (1, 2, 4, 5, 7, 8, 9, 10, 11, 12):
        warrive(m)
    for g in (t_up, t_down, t_far, a_up, a_down, a_far):
        give(g).start()
    for g in range(N_TP):
        ref = weight.at[1 - core, g]
        push(ref, ref, csend.at[g], crecv.at[g], sibling, t).wait_recv()
    for g in range(N_TP):
        for n in range(2):
            for k in range(2):
                ref = heads.at[g, :, pl.ds(OFF * n + HALF * k, HALF), :]
                push(ref, ref, hsend.at[0, 0, 0], hrecv.at[g, n, k], sibling, t).wait_recv()

    part = out.shape[-1]
    place = pl.ds(HS * y, HS)

    def send_home(n):
        return push(
            result.at[n], out.at[:, place, :], rsend.at[n], rrecv.at[y], c, side + n
        )

    for n in range(4):
        if n % 2 == 0:
            for begin, end in ((0, 4 * HS), (4 * HS, cols)):
                total = jnp.zeros((2 * HS, end - begin), f32)
                for g in range(N_TP):
                    x = heads[g].reshape(2 * HS, 2 * HS)
                    total = total + jnp.dot(
                        x, weight[n // 2, g, :, begin:end], preferred_element_type=f32
                    ).astype(jnp.bfloat16).astype(f32)
                product[:, begin:end] = total
            total = product[:, : 4 * HS][:, :part]
        else:
            start = part // HS * HS
            total = product[:, start : start + 4 * HS]
            total = pltpu.roll(total, 4 * HS - (part - start), 1)[:, :part]
        placed = rows[n].reshape(2 * HS, part).astype(f32)
        result[n] = (placed + total).astype(jnp.bfloat16).reshape(2, HS, part)

        @pl.when(y == n)
        def _():
            pltpu.make_async_copy(result.at[n], out.at[:, place, :], rrecv.at[y]).start()

        @pl.when(y != n)
        def _():
            send_home(n).start()

    for n in range(4):
        ref = out.at[:, pl.ds(HS * n, HS), :]
        push(ref, ref, rsend.at[0], rrecv.at[n], sibling, t).wait_recv()
    for index in range(7):
        transfer(*moves[index], index).wait_send()
    for e in range(PAIRS):
        share(e).wait_send()
    for m in range(13):
        wmove(m).wait_send()
    for g in range(N_TP):
        give(g).wait_send()
    for d in range(PAIRS):
        for n in range(2):
            for a in range(2):
                if d or n:
                    head_push(d, a, n).wait_send()
                else:

                    @pl.when(jnp.logical_not(is_here(d, a, n)))
                    def _():
                        head_push(d, a, n).wait_send()

    for n in range(4):

        @pl.when(y != n)
        def _():
            send_home(n).wait_send()


def attention(slot_of, span_order, query, kv, out_weight, rows):
    vm = pl.BlockSpec(memory_space=pltpu.VMEM)
    sm = pl.BlockSpec(memory_space=pltpu.SMEM)
    anywhere = pl.BlockSpec(memory_space=pl.ANY)
    dma = pltpu.SemaphoreType.DMA
    bf16 = jnp.bfloat16
    keys = 32 * OFF
    depth, width = out_weight.shape
    part = rows.shape[-1]
    return pl.pallas_call(
        attention_kernel,
        out_shape=jax.ShapeDtypeStruct((2, CH, part), bf16),
        in_specs=[sm, sm, vm, vm, anywhere, vm],
        out_specs=vm,
        scratch_shapes=[
            pltpu.VMEM((PAIRS, 2, keys, HS), bf16),
            pltpu.VMEM((keys, HS), bf16),
            pltpu.VMEM((keys, 2 * HS), jnp.float32),
            pltpu.VMEM((keys, 1), jnp.float32),
            pltpu.VMEM((keys, 1), jnp.int32),
            pltpu.VMEM((2, 32, HALF, 2 * HS), bf16),
            pltpu.VMEM((N_TP, 2, HS, 2 * HS), bf16),
            pltpu.VMEM((2, N_TP, depth, width // 4), bf16),
            pltpu.VMEM((2 * HS, width // 4), jnp.float32),
            pltpu.VMEM((4, 2, HS, part), bf16),
            dma((7,)),
            dma((PAIRS, 2)),
            dma((PAIRS,)),
            dma((13,)),
            dma((13,)),
            dma((N_TP,)),
            dma((N_TP,)),
            dma,
            dma((PAIRS, 2, 2)),
            dma((N_TP, 2, 2)),
            dma((4,)),
            dma((4,)),
        ],
        compiler_params=pltpu.CompilerParams(
            collective_id=2, has_side_effects=True, vmem_limit_bytes=52 * 2**20
        ),
        name="attention",
    )(slot_of, span_order, query, kv, out_weight, rows)


def per_device(
    text_embed,
    frame_features,
    frame_positions,
    span_order,
    projector,
    norm_gain,
    query_weight,
    key_weight,
    value_weight,
    out_weight,
):
    tok_rows, part = text_embed.shape
    c = lax.axis_index("ctx")
    t = lax.axis_index("tp")
    slots = span_order.shape[0]
    index = jnp.arange(slots, dtype=jnp.int32)
    slot_of = jnp.sum(
        jnp.where(span_order[None, :] == index[:, None], index[None, :], 0), axis=1
    )
    spans = lax.dynamic_slice_in_dim(span_order, 2 * c, 2, 0)
    positions = (
        spans[:, None] * CH + HS * (t % 4) + jnp.arange(HS, dtype=jnp.int32)[None, :]
    ).reshape(-1)
    half = HS // 2
    freqs = 1000000.0 ** (-(jnp.arange(half, dtype=jnp.float32) * 2.0 / HS))
    angles = positions.astype(jnp.float32)[:, None] * freqs[None, :]
    cos = jnp.cos(angles)
    sin = jnp.sin(angles)
    cosine = jnp.concatenate([cos, cos], axis=1)
    sine = jnp.concatenate([-sin, sin], axis=1)
    rows, query, kv = intake(
        text_embed, norm_gain, frame_features, frame_positions, span_order, (cosine, sine),
        projector, query_weight, key_weight, value_weight,
    )
    mixed = attention(
        slot_of, span_order, query.reshape(2, 32, HALF, HS), kv.reshape(32, OFF, HS),
        out_weight, rows,
    )
    return mixed.reshape(tok_rows, part)


def solution(mesh):
    in_specs = (
        P("ctx", "tp"),
        P(("ctx", "tp"), None),
        P(("ctx", "tp")),
        P(),
        P(),
        P("tp"),
        P(None, "tp"),
        P(),
        P(),
        P("tp", None),
    )
    out_specs = P("ctx", "tp")
    return jax.shard_map(
        per_device, mesh=mesh, in_specs=in_specs, out_specs=out_specs, check_vma=False
    )
```

```python
import functools
import math

import jax
import jax.numpy as jnp
from jax import lax
from jax.experimental import pallas as pl
from jax.experimental.pallas import tpu as pltpu
from jax.sharding import PartitionSpec as P

HS = 128
KVH = 4
CAP = 8
CH = 512
N_CTX = 16
N_TP = 8
PAIRS = 8
OFF = 64
HALF = 32
MESH = pl.DeviceIdType.MESH
LOG2E = math.log2(math.e)


def signal(sem, ctx, tp):
    pl.semaphore_signal(sem, inc=1, device_id=(ctx, tp), device_id_type=MESH)


def push(src, dst, send_sem, recv_sem, ctx, tp):
    return pltpu.make_async_remote_copy(
        src_ref=src, dst_ref=dst, send_sem=send_sem, recv_sem=recv_sem,
        device_id=(ctx, tp), device_id_type=MESH,
    )


def add4(a, b):
    return lax.rem(a + b + 4, 4)


def pair_of(e, t):
    x = lax.rem(e // 4 + t // 4, 2)
    return x * 4 + lax.rem(lax.rem(e, 4) + lax.rem(t, 4) + 2 * x, 4)


def class_of(e, pair):
    x = pair // 4
    return lax.rem(e // 4 + x, 2) * 4 + lax.rem(lax.rem(pair, 4) - lax.rem(e, 4) + 2 * x + 4, 4)


def intake_kernel(
    norm_gain, pos_row, order_row, cosine, sine,
    text, frame_features, projector, query_weight, key_weight, value_weight,
    rows_out, query_out, kv_out,
    features, gain, pweight, outgoing, incoming, placed, rows, gains, normed, weight, kv_weight, query, kv,
    tsem, psem, own_sem, kv_sem, fr_send, fr_recv, wsend, wrecv, csend, crecv,
    send, recv, gsend, grecv, osem, qsend, qrecv, ksend, krecv,
):
    c = lax.axis_index("ctx")
    t = lax.axis_index("tp")
    pair = c // 2
    core = c % 2
    sibling = c + 1 - 2 * core
    devices = N_CTX * N_TP
    me = c * N_TP + t
    part = text.shape[-1]
    width = N_TP * part
    base = pair // 4 * 4
    z = pair % 4
    z_up, z_down, z_far = (base + add4(z, n) for n in (1, 3, 2))
    y = lax.rem(t, 4)
    side = t - y
    half = t // 4
    y_up, y_down, y_far = (add4(y, n) for n in (1, 3, 2))

    own_copy = pltpu.make_async_copy(
        query_weight.at[:, pl.ds(pl.multiple_of(HS * core, HS), HS)], weight.at[core, y], own_sem
    )
    own_copy.start()
    block = 4 * HS
    take_features = pltpu.make_async_copy(frame_features, features, tsem.at[0])
    take_features.start()
    take_text = pltpu.make_async_copy(text, placed, tsem.at[1])

    def load(d):
        j = lax.rem(t + d, N_TP)
        start = pl.multiple_of((j * part) // HS * HS, HS)
        return pltpu.make_async_copy(
            projector.at[:, pl.ds(start, block)], pweight.at[d], psem.at[d]
        )

    for d in range(N_TP):
        load(d).start()
    kv_cols = pl.ds(pl.multiple_of(2 * HS * half, HS), 2 * HS)
    kv_loads = [
        pltpu.make_async_copy(ref.at[:, kv_cols], kv_weight.at[n], kv_sem.at[n])
        for n, ref in enumerate((key_weight, value_weight))
    ]
    take_text.start()
    for one in kv_loads:
        one.start()

    barrier = pltpu.get_barrier_semaphore()

    def greet(d, unused):
        other = lax.rem(me + d, devices)
        signal(barrier, other // N_TP, lax.rem(other, N_TP))
        return unused

    lax.fori_loop(1, devices, greet, 0)

    f32 = jnp.float32
    gain[...] = jnp.broadcast_to(norm_gain[...], gain.shape)
    spans = order_row.shape[1]
    tokens = pos_row.shape[1]
    entries = N_CTX * CAP

    def turned(x):
        size = x.shape[1]
        same = lax.broadcasted_iota(jnp.int32, (size, size), 0) == lax.broadcasted_iota(
            jnp.int32, (size, size), 1
        )
        return jnp.sum(jnp.where(same, x, 0.0), axis=1, keepdims=True)

    order_col = turned(order_row[...].astype(f32))
    slot_row = jnp.sum(
        jnp.where(
            order_col == (pos_row[...] // CH).astype(f32),
            lax.broadcasted_iota(jnp.int32, (spans, tokens), 0).astype(f32), 0.0,
        ),
        axis=0, keepdims=True,
    )
    slot_col = turned(slot_row).astype(jnp.int32)
    slot_row = slot_row.astype(jnp.int32)
    first = lax.broadcasted_iota(jnp.int32, (tokens, tokens), 0)
    second = lax.broadcasted_iota(jnp.int32, (tokens, tokens), 1)
    earlier = jnp.logical_and(slot_col // 2 == slot_row // 2, first < second)
    place = jnp.sum(jnp.where(earlier, 1.0, 0.0), axis=0, keepdims=True).astype(jnp.int32)
    entry = slot_row // 2 * CAP + place
    chosen = lax.broadcasted_iota(jnp.int32, (entries, tokens), 0) == entry
    take_features.wait()
    ordered = jnp.dot(
        jnp.where(chosen, 1.0, 0.0).astype(jnp.bfloat16), features[...],
        preferred_element_type=f32,
    ).astype(jnp.bfloat16)
    token_row = (slot_row % 2 * CH + pos_row[...] % CH + 1).astype(f32)
    row_at = jnp.sum(jnp.where(chosen, token_row, 0.0), axis=1, keepdims=True) - 1.0
    row_at = row_at.astype(jnp.int32)
    high = (row_at >> 5).astype(f32)
    low = (row_at & 31).astype(f32)
    lane = lax.broadcasted_iota(jnp.int32, (entries, block), 1)
    tail = jnp.where(lane < part + 32, high, jnp.where(lane < part + 48, low, 1.0))

    pl.semaphore_wait(barrier, devices - 1)

    depth = weight.shape[2]

    def quarter(n):
        return pl.ds(depth // 4 * n, depth // 4)

    def wmove(m):
        n = m - 3
        shard = y if m < 3 else (y_up, y_down, y_far)[n // 3]
        ref = weight.at[core, shard, quarter(z)]
        if m < 3:
            ctx, tp = c, side + (y_up, y_down, y_far)[m]
        else:
            ctx, tp = 2 * (z_up, z_down, z_far)[n % 3] + core, t
        return push(ref, ref, wsend.at[m], wrecv.at[m], ctx, tp)

    def warrive(m):
        n = m - 3
        shard = (y_down, y_up, y_far)[m] if m < 3 else (y_up, y_down, y_far)[n // 3]
        origin = z if m < 3 else add4(z, (3, 1, 2)[n % 3])
        ref = weight.at[core, shard, quarter(origin)]
        push(ref, ref, wsend.at[m], wrecv.at[m], sibling, t).wait_recv()

    def share(n):
        ref = weight.at[core, add4(y, n)]
        return push(ref, ref, csend.at[n], crecv.at[n], sibling, t)

    def shared(n):
        ref = weight.at[1 - core, add4(y, n)]
        push(ref, ref, csend.at[n], crecv.at[n], sibling, t).wait_recv()

    own_copy.wait()
    for m in (2, 0, 1):
        wmove(m).start()
    share(0).start()

    for d in range(N_TP):
        j = lax.rem(t + d, N_TP)
        load(d).wait()
        x = jnp.dot(ordered, pweight[d], preferred_element_type=f32)
        x = 0.5 * x * (1.0 + lax.erf(x * math.sqrt(0.5)))
        shift = j * part - (j * part) // HS * HS
        x = jnp.where(shift > 0, pltpu.roll(x, block - HS // 2, 1), x)
        x = jnp.where(lane < part, x, tail)
        halves = [
            x[:, n * 2 * HS : (n + 1) * 2 * HS].reshape(N_CTX, CAP, 2 * HS) for n in range(2)
        ]
        outgoing[d] = jnp.concatenate(halves, axis=1).astype(jnp.bfloat16)

        def deliver(n, unused):
            oc = lax.rem(c + n, N_CTX)
            push(outgoing.at[d, oc], incoming.at[me], fr_send, fr_recv, oc, j).start()
            return unused

        if d == 0:
            pltpu.make_async_copy(outgoing.at[0, c], incoming.at[me], fr_recv).start()
        else:
            push(outgoing.at[d, c], incoming.at[me], fr_send, fr_recv, c, j).start()
        lax.fori_loop(1, N_CTX, deliver, 0)
        if d == 4:
            for m in range(3):
                warrive(m)
            for m in range(3, 12):
                wmove(m).start()

    pltpu.make_async_copy(incoming, incoming, fr_recv).wait()

    def row_block(n, across):
        j = add4(y, n)
        tp = j + (4 - side if across else side)
        return push(
            placed.at[:, j], rows.at[t], send.at[n, across], recv.at[t], c, tp
        )

    def gain_block(d):
        return push(gain, gains.at[t], gsend.at[d], grecv.at[t], c, lax.rem(t + d, N_TP))

    pltpu.make_async_copy(gain, gains.at[t], grecv.at[t]).start()
    for d in range(1, N_TP):
        gain_block(d).start()
    arrived = incoming[...].astype(f32)
    slots = devices * CAP
    left = arrived[:, :CAP].reshape(slots, 2 * HS)
    right = arrived[:, CAP:].reshape(slots, 2 * HS)
    edge = part - 2 * HS
    at = right[:, edge : edge + 1] * 32.0 + right[:, edge + 32 : edge + 33]
    at = jnp.transpose(jnp.broadcast_to(at, (slots, HS)))[0:1, :]
    left = left.astype(jnp.bfloat16)
    right = right.astype(jnp.bfloat16)
    group = 2 * HS
    take_text.wait()
    offset = lax.broadcasted_iota(jnp.int32, (group, 1), 0)
    offset = offset // HS * CH + offset % HS
    for n in range(4):
        j = add4(y, n)
        row = offset + j * HS
        hit = jnp.where(row.astype(f32) == at, 1.0, 0.0).astype(jnp.bfloat16)
        new_left = jnp.dot(hit, left, preferred_element_type=f32)
        new_right = jnp.dot(hit, right, preferred_element_type=f32)
        framed = new_right[:, 2 * HS - 1 :] > 0.5
        old = placed[:, j].reshape(group, part).astype(f32)
        placed[:, j, :, : 2 * HS] = (
            jnp.where(framed, new_left, old[:, : 2 * HS]).astype(jnp.bfloat16)
        ).reshape(2, HS, 2 * HS)
        placed[:, j, :, 2 * HS :] = (
            jnp.where(framed, new_right[:, :edge], old[:, 2 * HS :]).astype(jnp.bfloat16)
        ).reshape(2, HS, edge)
        row_block(n, 1).start()
        if n == 0:
            pltpu.make_async_copy(placed.at[:, y], rows.at[t], recv.at[t]).start()
        else:
            row_block(n, 0).start()

    for m in range(3, 12):
        warrive(m)
    for n in range(1, 4):
        share(n).start()
    for one in kv_loads:
        one.wait()

    total = jnp.zeros((group, 1), f32)
    for d in range(N_TP):
        j = lax.rem(t + d, N_TP)
        push(gain, gains.at[j], gsend.at[0], grecv.at[j], sibling, t).wait_recv()
        push(rows.at[j], rows.at[j], send.at[0, 0], recv.at[j], sibling, t).wait_recv()
        x = rows[j].reshape(group, part).astype(f32)
        total = total + jnp.sum(x * x, axis=1, keepdims=True)

    keep = pltpu.make_async_copy(rows.at[pl.ds(side, 4)], rows_out, osem)
    keep.start()

    inverse = lax.rsqrt(total / width + 1e-06)
    for j in range(N_TP):
        x = rows[j].reshape(group, part).astype(f32)
        normed[j] = (x * inverse * gains[j, 0:1, :].astype(f32)).astype(jnp.bfloat16)

    def product(piece):
        total = None
        for j in range(N_TP):
            term = jnp.dot(
                normed[j], piece(slice(j * part, (j + 1) * part)), preferred_element_type=f32
            )
            total = term if total is None else total + term
        return total

    def rotated(x, cos, sin):
        return (x * cos + pltpu.roll(x, HS // 2, 1) * sin).astype(jnp.bfloat16).reshape(2, HS, HS)

    goal = [pair_of(pair, 4 * n + y) for n in range(2)]
    mine = pl.ds(2 * core, 2)

    def kv_push(n, which, m):
        return push(
            kv.at[which, m // 2, :, pl.ds(OFF * n, OFF), :], kv_out.at[pair, mine],
            ksend.at[n, which, m], krecv.at[pair, core], 2 * goal[n] + which, side + m,
        )

    def q_push(n, k, m):
        return push(
            query.at[m, :, :, pl.ds(OFF * n + HALF * k, HALF), :], query_out.at[:, pair, mine],
            qsend.at[n, k, m], qrecv.at[pair, core], 2 * goal[n] + k, side + m,
        )

    def is_here(n, k, m):
        return jnp.logical_and(goal[n] == pair, jnp.logical_and(core == k, y == m))

    cos = cosine[...]
    sin = sine[...]
    for which in range(2):
        out = product(lambda cut: kv_weight[which, cut, :])
        for h in range(2):
            x = out[:, h * HS : (h + 1) * HS]
            kv[which, h] = rotated(x, cos, sin) if which == 0 else x.astype(
                jnp.bfloat16
            ).reshape(2, HS, HS)
        for m in range(4):
            for n in range(2):

                @pl.when(is_here(n, which, m))
                def _():
                    pltpu.make_async_copy(
                        kv.at[which, m // 2, :, pl.ds(OFF * n, OFF), :], kv_out.at[pair, mine],
                        krecv.at[pair, core],
                    ).start()

                @pl.when(jnp.logical_not(is_here(n, which, m)))
                def _():
                    kv_push(n, which, m).start()

    for m0 in range(4):
        m = add4(y, m0)
        shared(m0)
        out = product(
            lambda cut: jnp.concatenate([weight[0, m, cut], weight[1, m, cut]], axis=1)
        )
        for h in range(2):
            query[m, h] = rotated(out[:, h * HS : (h + 1) * HS], cos, sin)
        for n in range(2):
            for k in range(2):
                if m0 == 0:
                    here = jnp.logical_and(goal[n] == pair, core == k)

                    @pl.when(here)
                    def _():
                        pltpu.make_async_copy(
                            query.at[m, :, :, pl.ds(OFF * n + HALF * k, HALF), :],
                            query_out.at[:, pair, mine], qrecv.at[pair, core],
                        ).start()

                    @pl.when(jnp.logical_not(here))
                    def _():
                        q_push(n, k, m).start()

                else:
                    q_push(n, k, m).start()

    for e in range(PAIRS):
        for a in range(2):
            two = pl.ds(2 * a, 2)
            ref = kv_out.at[e, two]
            push(ref, ref, ksend.at[0, 0, 0], krecv.at[e, a], sibling, t).wait_recv()
            ref = query_out.at[:, e, two]
            push(ref, ref, qsend.at[0, 0, 0], qrecv.at[e, a], sibling, t).wait_recv()
    keep.wait()
    pltpu.make_async_copy(
        incoming.at[pl.ds(0, devices - 1)], incoming.at[pl.ds(0, devices - 1)], fr_send
    ).wait()
    for m in range(12):
        wmove(m).wait_send()
    for n in range(4):
        share(n).wait_send()
        row_block(n, 1).wait_send()
        if n:
            row_block(n, 0).wait_send()
    for d in range(1, N_TP):
        gain_block(d).wait_send()
    for n in range(2):
        for k in range(2):
            for m in range(4):

                @pl.when(jnp.logical_not(is_here(n, k, m)))
                def _():
                    kv_push(n, k, m).wait_send()
                    q_push(n, k, m).wait_send()


def intake(
    text_embed, norm_gain, frame_features, frame_positions, span_order, tables,
    projector, query_weight, key_weight, value_weight,
):
    tok_rows, part = text_embed.shape
    depth = query_weight.shape[0]
    devices = N_CTX * N_TP
    vm = pl.BlockSpec(memory_space=pltpu.VMEM)
    anywhere = pl.BlockSpec(memory_space=pl.ANY)
    dma = pltpu.SemaphoreType.DMA
    bf16 = jnp.bfloat16
    return pl.pallas_call(
        intake_kernel,
        out_shape=(
            jax.ShapeDtypeStruct((4, 2, HS, part), bf16),
            jax.ShapeDtypeStruct((2, PAIRS, 4, HALF, HS), bf16),
            jax.ShapeDtypeStruct((PAIRS, 4, OFF, HS), bf16),
        ),
        in_specs=[vm] * 5 + [anywhere] * 6,
        out_specs=(vm, vm, vm),
        scratch_shapes=[
            pltpu.VMEM(frame_features.shape, bf16),
            pltpu.VMEM((16, part), bf16),
            pltpu.VMEM((N_TP, projector.shape[0], 4 * HS), bf16),
            pltpu.VMEM((N_TP, N_CTX, 2 * CAP, 2 * HS), bf16),
            pltpu.VMEM((devices, 2 * CAP, 2 * HS), bf16),
            pltpu.VMEM((2, 4, HS, part), bf16),
            pltpu.VMEM((N_TP, 2, HS, part), bf16),
            pltpu.VMEM((N_TP, 16, part), bf16),
            pltpu.VMEM((N_TP, 2 * HS, part), bf16),
            pltpu.VMEM((2, 4, depth, HS), bf16),
            pltpu.VMEM((2, depth, 2 * HS), bf16),
            pltpu.VMEM((4, 2, 2, HS, HS), bf16),
            pltpu.VMEM((2, 2, 2, HS, HS), bf16),
            dma((2,)),
            dma((N_TP,)),
            dma,
            dma((2,)),
            dma,
            dma,
            dma((12,)),
            dma((12,)),
            dma((4,)),
            dma((4,)),
            dma((4, 2)),
            dma((N_TP,)),
            dma((N_TP,)),
            dma((N_TP,)),
            dma,
            dma((2, 2, 4)),
            dma((PAIRS, 2)),
            dma((2, 2, 4)),
            dma((PAIRS, 2)),
        ],
        compiler_params=pltpu.CompilerParams(
            collective_id=1, has_side_effects=True, vmem_limit_bytes=56 * 2**20
        ),
        name="intake",
    )(
        norm_gain.reshape(1, part),
        frame_positions.reshape(1, -1),
        span_order.reshape(1, -1),
        *tables,
        text_embed.reshape(2, 4, HS, part),
        frame_features,
        projector,
        query_weight,
        key_weight,
        value_weight,
    )


def attention_kernel(
    slot_of, span_order, query, kv_own, out_weight, rows, out,
    kv, q, summed, largest, limit, attended, heads, weight, product, result,
    send, recv, pass_send, wsend, wrecv, csend, crecv, own_sem,
    hsend, hrecv, rsend, rrecv,
):
    f32 = jnp.float32
    scale = LOG2E / math.sqrt(HS)
    c = lax.axis_index("ctx")
    t = lax.axis_index("tp")
    pair = c // 2
    core = c % 2
    sibling = c + 1 - 2 * core
    base = pair // 4 * 4
    other = 4 - base
    z = pair % 4
    up, down, far = (add4(z, n) for n in (1, 3, 2))
    z_up, z_down, z_far = base + up, base + down, base + far
    x_own, x_up, x_down, x_far = other + z, other + up, other + down, other + far
    y = lax.rem(t, 4)
    side = t - y
    half = t // 4
    across = 4 - side
    t_up, t_down, t_far = (side + add4(y, n) for n in (1, 3, 2))
    a_own, a_up, a_down, a_far = (across + add4(y, n) for n in (0, 1, 3, 2))
    x_next = 2 * x_own + core
    depth, cols = weight.shape[2:]

    def columns(of_half):
        return out_weight.at[:, pl.ds(pl.multiple_of(cols * (2 * of_half + core), HS), cols)]

    own_copy = pltpu.make_async_copy(columns(half), weight.at[core, t], own_sem)
    own_copy.start()
    barrier = pltpu.get_barrier_semaphore()
    signal(barrier, sibling, t)
    for e in (z_up, z_down, z_far, x_own):
        signal(barrier, 2 * e + core, t)
    signal(barrier, x_next, a_own)
    for j in (t_up, t_down, t_far):
        signal(barrier, c, j)
    first = y == 2 * (pair // 4)
    for n in range(2):
        origin = pair_of(pair, 4 * n + y)
        for k in range(2):
            for d in range(N_TP):
                j = lax.rem(t + d, N_TP)
                if n == 0 and d == 0:

                    @pl.when(jnp.logical_not(jnp.logical_and(first, core == k)))
                    def _():
                        signal(barrier, 2 * origin + k, j)

                else:
                    signal(barrier, 2 * origin + k, j)
    for j in range(32):
        kv[pair, core, j * OFF : (j + 1) * OFF] = kv_own[slot_of[j]]
    pl.semaphore_wait(barrier, 9 + 32 - jnp.where(first, 1, 0))

    def quarter(ref, n):
        return ref.at[pl.ds(depth // 4 * n, depth // 4)]

    def wmove(m):
        own = weight.at[core, t]
        passed = weight.at[core, a_own]
        if m == 0:
            src, dst, ctx, tp = columns(1 - half), own, x_next, a_own
        elif m < 7:
            dst, tp = (
                (own, t_up), (own, t_down), (quarter(own, z), t_far),
                (passed, t_up), (passed, t_down), (quarter(passed, z), t_far),
            )[m - 1]
            src, ctx = dst, c
        else:
            n = m - 7
            dst = quarter(weight.at[core, (t_far, a_far)[n // 3]], z)
            src, tp, ctx = dst, t, 2 * (z_up, z_down, z_far)[n % 3] + core
        return push(src, dst, wsend.at[m], wrecv.at[m], ctx, tp)

    def warrive(m):
        if m < 7:
            ref = weight.at[core, (a_own, t_down, t_up, t_far, a_down, a_up, a_far)[m]]
            if m % 3 == 0 and m:
                ref = quarter(ref, z)
        else:
            n = m - 7
            ref = quarter(weight.at[core, (t_far, a_far)[n // 3]], (down, up, far)[n % 3])
        push(ref, ref, wsend.at[m], wrecv.at[m], sibling, t).wait_recv()

    def give(g):
        ref = weight.at[core, g]
        return push(ref, ref, csend.at[g], crecv.at[g], sibling, t)

    def transfer(e, to, index):
        block = kv.at[e, core]
        return push(block, block, send.at[index], recv.at[e, core], 2 * to + core, t)

    def share(e):
        block = kv.at[e, core]
        return push(block, block, pass_send.at[e], recv.at[e, core], sibling, t)

    def arrive(e, which):
        block = kv.at[e, which]
        push(block, block, send.at[0], recv.at[e, which], sibling, t).wait_recv()

    share(pair).start()
    moves = (
        (pair, x_own), (pair, z_up), (pair, z_down), (pair, z_far),
        (x_own, z_up), (x_own, z_down), (z_far, x_own),
    )
    for index in range(3):
        transfer(*moves[index], index).start()
    own_copy.wait()
    for m in (3, 1, 2):
        wmove(m).start()
    for j in range(32):
        q[j * OFF : (j + 1) * OFF] = query[:, slot_of[j]].reshape(2 * HALF, HS)

    group = 8 * HALF
    row = lax.broadcasted_iota(jnp.int32, (group, 1), 0)
    col = lax.broadcasted_iota(jnp.int32, (1, 4 * OFF), 1)

    def starts(index, i, e):
        value = jnp.zeros(index.shape, jnp.int32)
        for a in range(4):
            kind = class_of(slot_of[4 * i + a] // 4, e)
            start = a * CH + HS * lax.rem(kind, 4) + OFF * (kind // 4)
            value = jnp.where(index // OFF == a, start, value)
        return value

    for i in range(8):
        limit[i * group : (i + 1) * group] = starts(row, i, pair) + HALF * core + row % HALF

    def update(e, first_set):
        def chunk(i):
            return slice(i * group, (i + 1) * group), 4 * OFF * (i + 1)

        def scores(i):
            here, width = chunk(i)
            return lax.dot_general(
                q[here], kv[e, 0, :width], (((1,), (1,)), ((), ())), preferred_element_type=f32
            )

        def soft(i, s):
            here, width = chunk(i)
            at = starts(col, i, e) + col % OFF
            edge = jnp.where(at <= limit[here], s[:, width - 4 * OFF :], -1e30)
            s = edge if i == 0 else jnp.concatenate([s[:, : width - 4 * OFF], edge], axis=1)
            top = jnp.max(s, axis=1, keepdims=True)
            if not first_set:
                top = jnp.maximum(top, largest[here])
                summed[here] = summed[here] * jnp.exp2((largest[here] - top) * scale)
            largest[here] = top
            return jnp.exp2((s - top) * scale).astype(jnp.bfloat16)

        def gather(i, weights):
            here, width = chunk(i)
            beside = jnp.concatenate(
                [kv[e, 1, :width], jnp.ones((width, HS), jnp.bfloat16)], axis=1
            )
            new = jnp.dot(weights, beside, preferred_element_type=f32)
            summed[here] = new if first_set else summed[here] + new

        s = scores(0)
        held = None
        for i in range(8):
            ahead = scores(i + 1) if i < 7 else None
            weights = soft(i, s)
            if held is not None:
                gather(*held)
            held = (i, weights)
            s = ahead
        gather(*held)

    arrive(pair, 1 - core)
    update(pair, True)
    arrive(x_own, core)
    share(x_own).start()
    transfer(*moves[1], 1).wait_send()
    transfer(*moves[2], 2).wait_send()
    transfer(*moves[3], 3).start()
    wmove(0).start()
    give(t).start()
    order = (x_own, z_up, z_down, z_far, x_up, x_down, x_far)

    def step(n, unused):
        e = order[6]
        for index in range(6):
            e = jnp.where(n == index, order[index], e)

        @pl.when(n == 1)
        def _():
            arrive(z_up, core)
            share(z_up).start()
            arrive(z_down, core)
            share(z_down).start()

        @pl.when(n == 2)
        def _():
            transfer(*moves[3], 3).wait_send()
            transfer(*moves[4], 4).start()
            transfer(*moves[5], 5).start()
            arrive(z_far, core)
            transfer(*moves[6], 6).start()
            share(z_far).start()
            warrive(3)
            for m in (7, 8, 9):
                wmove(m).start()

        @pl.when(n == 4)
        def _():
            warrive(0)
            for m in (6, 4, 5):
                wmove(m).start()
            give(a_own).start()
            arrive(x_up, core)
            share(x_up).start()
            arrive(x_down, core)
            share(x_down).start()

        @pl.when(n == 6)
        def _():
            arrive(x_far, core)
            share(x_far).start()
            warrive(6)
            for m in (10, 11, 12):
                wmove(m).start()

        arrive(e, 1 - core)
        update(e, False)
        return unused

    lax.fori_loop(0, 7, step, 0)

    for i in range(8):
        here = slice(i * group, (i + 1) * group)
        done = (summed[here, :HS] / summed[here, HS : HS + 1]).astype(jnp.bfloat16)
        done = done.reshape(4, 2, HALF, HS)
        for a in range(4):
            attended[0, 4 * i + a] = jnp.concatenate([done[a, 0], done[a, 1]], axis=1)

    def head_push(d, a, n):
        e = lax.rem(pair + d, PAIRS)
        kind = class_of(e, pair)
        at = pl.ds(OFF * (kind // 4) + HALF * core, HALF)
        return push(
            attended.at[1, pl.ds(4 * e + 2 * a, 2)], heads.at[t, :, at, :], hsend.at[d, a, n],
            hrecv.at[t, kind // 4, core], 2 * e + a, lax.rem(4 * n + lax.rem(kind, 4) + side, N_TP),
        )

    def is_here(d, a, n):
        if d or n:
            return jnp.bool_(False)
        return jnp.logical_and(first, core == a)

    for j in range(32):
        attended[1, j] = attended[0, span_order[j]]
    for d in range(PAIRS):
        for n in range(2):
            for a in range(2):
                if d or n:
                    head_push(d, a, n).start()
                else:

                    @pl.when(is_here(d, a, n))
                    def _():
                        pltpu.make_async_copy(
                            attended.at[1, pl.ds(4 * pair + 2 * a, 2)],
                            heads.at[t, :, pl.ds(HALF * core, HALF), :], hrecv.at[t, 0, core],
                        ).start()

                    @pl.when(jnp.logical_not(is_here(d, a, n)))
                    def _():
                        head_push(d, a, n).start()

    for m in (1, 2, 4, 5, 7, 8, 9, 10, 11, 12):
        warrive(m)
    for g in (t_up, t_down, t_far, a_up, a_down, a_far):
        give(g).start()
    for g in range(N_TP):
        ref = weight.at[1 - core, g]
        push(ref, ref, csend.at[g], crecv.at[g], sibling, t).wait_recv()
    for g in range(N_TP):
        for n in range(2):
            for k in range(2):
                ref = heads.at[g, :, pl.ds(OFF * n + HALF * k, HALF), :]
                push(ref, ref, hsend.at[0, 0, 0], hrecv.at[g, n, k], sibling, t).wait_recv()

    part = out.shape[-1]
    place = pl.ds(HS * y, HS)

    def send_home(n):
        return push(
            result.at[n], out.at[:, place, :], rsend.at[n], rrecv.at[y], c, side + n
        )

    for n in range(4):
        if n % 2 == 0:
            for begin, end in ((0, 4 * HS), (4 * HS, cols)):
                total = jnp.zeros((2 * HS, end - begin), f32)
                for g in range(N_TP):
                    x = heads[g].reshape(2 * HS, 2 * HS)
                    total = total + jnp.dot(
                        x, weight[n // 2, g, :, begin:end], preferred_element_type=f32
                    ).astype(jnp.bfloat16).astype(f32)
                product[:, begin:end] = total
            total = product[:, : 4 * HS][:, :part]
        else:
            start = part // HS * HS
            total = product[:, start : start + 4 * HS]
            total = pltpu.roll(total, 4 * HS - (part - start), 1)[:, :part]
        placed = rows[n].reshape(2 * HS, part).astype(f32)
        result[n] = (placed + total).astype(jnp.bfloat16).reshape(2, HS, part)

        @pl.when(y == n)
        def _():
            pltpu.make_async_copy(result.at[n], out.at[:, place, :], rrecv.at[y]).start()

        @pl.when(y != n)
        def _():
            send_home(n).start()

    for n in range(4):
        ref = out.at[:, pl.ds(HS * n, HS), :]
        push(ref, ref, rsend.at[0], rrecv.at[n], sibling, t).wait_recv()
    for index in (0, 4, 5, 6):
        transfer(*moves[index], index).wait_send()
    for e in range(PAIRS):
        share(e).wait_send()
    for m in range(13):
        wmove(m).wait_send()
    for g in range(N_TP):
        give(g).wait_send()
    for d in range(PAIRS):
        for n in range(2):
            for a in range(2):
                if d or n:
                    head_push(d, a, n).wait_send()
                else:

                    @pl.when(jnp.logical_not(is_here(d, a, n)))
                    def _():
                        head_push(d, a, n).wait_send()

    for n in range(4):

        @pl.when(y != n)
        def _():
            send_home(n).wait_send()


def attention(slot_of, span_order, query, kv, out_weight, rows):
    vm = pl.BlockSpec(memory_space=pltpu.VMEM)
    sm = pl.BlockSpec(memory_space=pltpu.SMEM)
    anywhere = pl.BlockSpec(memory_space=pl.ANY)
    dma = pltpu.SemaphoreType.DMA
    bf16 = jnp.bfloat16
    keys = 32 * OFF
    depth, width = out_weight.shape
    part = rows.shape[-1]
    return pl.pallas_call(
        attention_kernel,
        out_shape=jax.ShapeDtypeStruct((2, CH, part), bf16),
        in_specs=[sm, sm, vm, vm, anywhere, vm],
        out_specs=vm,
        scratch_shapes=[
            pltpu.VMEM((PAIRS, 2, keys, HS), bf16),
            pltpu.VMEM((keys, HS), bf16),
            pltpu.VMEM((keys, 2 * HS), jnp.float32),
            pltpu.VMEM((keys, 1), jnp.float32),
            pltpu.VMEM((keys, 1), jnp.int32),
            pltpu.VMEM((2, 32, HALF, 2 * HS), bf16),
            pltpu.VMEM((N_TP, 2, HS, 2 * HS), bf16),
            pltpu.VMEM((2, N_TP, depth, width // 4), bf16),
            pltpu.VMEM((2 * HS, width // 4), jnp.float32),
            pltpu.VMEM((4, 2, HS, part), bf16),
            dma((7,)),
            dma((PAIRS, 2)),
            dma((PAIRS,)),
            dma((13,)),
            dma((13,)),
            dma((N_TP,)),
            dma((N_TP,)),
            dma,
            dma((PAIRS, 2, 2)),
            dma((N_TP, 2, 2)),
            dma((4,)),
            dma((4,)),
        ],
        compiler_params=pltpu.CompilerParams(
            collective_id=2, has_side_effects=True, vmem_limit_bytes=52 * 2**20
        ),
        name="attention",
    )(slot_of, span_order, query, kv, out_weight, rows)


def per_device(
    text_embed,
    frame_features,
    frame_positions,
    span_order,
    projector,
    norm_gain,
    query_weight,
    key_weight,
    value_weight,
    out_weight,
):
    tok_rows, part = text_embed.shape
    c = lax.axis_index("ctx")
    t = lax.axis_index("tp")
    slots = span_order.shape[0]
    index = jnp.arange(slots, dtype=jnp.int32)
    slot_of = jnp.sum(
        jnp.where(span_order[None, :] == index[:, None], index[None, :], 0), axis=1
    )
    spans = lax.dynamic_slice_in_dim(span_order, 2 * c, 2, 0)
    positions = (
        spans[:, None] * CH + HS * (t % 4) + jnp.arange(HS, dtype=jnp.int32)[None, :]
    ).reshape(-1)
    half = HS // 2
    freqs = 1000000.0 ** (-(jnp.arange(half, dtype=jnp.float32) * 2.0 / HS))
    angles = positions.astype(jnp.float32)[:, None] * freqs[None, :]
    cos = jnp.cos(angles)
    sin = jnp.sin(angles)
    cosine = jnp.concatenate([cos, cos], axis=1)
    sine = jnp.concatenate([-sin, sin], axis=1)
    rows, query, kv = intake(
        text_embed, norm_gain, frame_features, frame_positions, span_order, (cosine, sine),
        projector, query_weight, key_weight, value_weight,
    )
    mixed = attention(
        slot_of, span_order, query.reshape(2, 32, HALF, HS), kv.reshape(32, OFF, HS),
        out_weight, rows,
    )
    return mixed.reshape(tok_rows, part)


def solution(mesh):
    in_specs = (
        P("ctx", "tp"),
        P(("ctx", "tp"), None),
        P(("ctx", "tp")),
        P(),
        P(),
        P("tp"),
        P(None, "tp"),
        P(),
        P(),
        P("tp", None),
    )
    out_specs = P("ctx", "tp")
    return jax.shard_map(
        per_device, mesh=mesh, in_specs=in_specs, out_specs=out_specs, check_vma=False
    )
```

```python
import functools
import math

import jax
import jax.numpy as jnp
from jax import lax
from jax.experimental import pallas as pl
from jax.experimental.pallas import tpu as pltpu
from jax.sharding import PartitionSpec as P

HS = 128
KVH = 4
CAP = 8
CH = 512
N_CTX = 16
N_TP = 8
PAIRS = 8
OFF = 64
HALF = 32
MESH = pl.DeviceIdType.MESH
LOG2E = math.log2(math.e)


def signal(sem, ctx, tp):
    pl.semaphore_signal(sem, inc=1, device_id=(ctx, tp), device_id_type=MESH)


def push(src, dst, send_sem, recv_sem, ctx, tp):
    return pltpu.make_async_remote_copy(
        src_ref=src, dst_ref=dst, send_sem=send_sem, recv_sem=recv_sem,
        device_id=(ctx, tp), device_id_type=MESH,
    )


def add4(a, b):
    return lax.rem(a + b + 4, 4)


def pair_of(e, t):
    x = lax.rem(e // 4 + t // 4, 2)
    return x * 4 + lax.rem(lax.rem(e, 4) + lax.rem(t, 4) + 2 * x, 4)


def class_of(e, pair):
    x = pair // 4
    return lax.rem(e // 4 + x, 2) * 4 + lax.rem(lax.rem(pair, 4) - lax.rem(e, 4) + 2 * x + 4, 4)


def intake_kernel(
    gain, pos_row, order_row, cosine, sine,
    text, frame_features, projector, query_weight, key_weight, value_weight,
    rows_out, query_out, kv_out,
    features, turned_text, pweight, outgoing, incoming, placed, rows, gains, normed, weight, kv_weight, query, kv,
    tsem, psem, own_sem, kv_sem, fr_send, fr_recv, wsend, wrecv, csend, crecv,
    send, recv, gsend, grecv, osem, qsend, qrecv, ksend, krecv,
):
    c = lax.axis_index("ctx")
    t = lax.axis_index("tp")
    pair = c // 2
    core = c % 2
    sibling = c + 1 - 2 * core
    devices = N_CTX * N_TP
    me = c * N_TP + t
    part = text.shape[0]
    width = N_TP * part
    base = pair // 4 * 4
    z = pair % 4
    z_up, z_down, z_far = (base + add4(z, n) for n in (1, 3, 2))
    y = lax.rem(t, 4)
    side = t - y
    half = t // 4
    y_up, y_down, y_far = (add4(y, n) for n in (1, 3, 2))

    own_copy = pltpu.make_async_copy(
        query_weight.at[:, pl.ds(pl.multiple_of(HS * core, HS), HS)], weight.at[core, y], own_sem
    )
    own_copy.start()
    block = 4 * HS
    take_features = pltpu.make_async_copy(frame_features, features, tsem.at[0])
    take_features.start()
    take_text = pltpu.make_async_copy(text, turned_text, tsem.at[1])

    def load(d):
        j = lax.rem(t + d, N_TP)
        start = pl.multiple_of((j * part) // HS * HS, HS)
        return pltpu.make_async_copy(
            projector.at[:, pl.ds(start, block)], pweight.at[d], psem.at[d]
        )

    for d in range(N_TP):
        load(d).start()
    kv_cols = pl.ds(pl.multiple_of(2 * HS * half, HS), 2 * HS)
    kv_loads = [
        pltpu.make_async_copy(ref.at[:, kv_cols], kv_weight.at[n], kv_sem.at[n])
        for n, ref in enumerate((key_weight, value_weight))
    ]
    take_text.start()
    for one in kv_loads:
        one.start()

    barrier = pltpu.get_barrier_semaphore()

    def greet(d, unused):
        other = lax.rem(me + d, devices)
        signal(barrier, other // N_TP, lax.rem(other, N_TP))
        return unused

    lax.fori_loop(1, devices, greet, 0)

    f32 = jnp.float32
    spans = order_row.shape[1]
    tokens = pos_row.shape[1]
    entries = N_CTX * CAP

    def turned(x):
        size = x.shape[1]
        same = lax.broadcasted_iota(jnp.int32, (size, size), 0) == lax.broadcasted_iota(
            jnp.int32, (size, size), 1
        )
        return jnp.sum(jnp.where(same, x, 0.0), axis=1, keepdims=True)

    order_col = turned(order_row[...].astype(f32))
    slot_row = jnp.sum(
        jnp.where(
            order_col == (pos_row[...] // CH).astype(f32),
            lax.broadcasted_iota(jnp.int32, (spans, tokens), 0).astype(f32), 0.0,
        ),
        axis=0, keepdims=True,
    )
    slot_col = turned(slot_row).astype(jnp.int32)
    slot_row = slot_row.astype(jnp.int32)
    first = lax.broadcasted_iota(jnp.int32, (tokens, tokens), 0)
    second = lax.broadcasted_iota(jnp.int32, (tokens, tokens), 1)
    earlier = jnp.logical_and(slot_col // 2 == slot_row // 2, first < second)
    place = jnp.sum(jnp.where(earlier, 1.0, 0.0), axis=0, keepdims=True).astype(jnp.int32)
    entry = slot_row // 2 * CAP + place
    chosen = lax.broadcasted_iota(jnp.int32, (entries, tokens), 0) == entry
    take_features.wait()
    ordered = jnp.dot(
        jnp.where(chosen, 1.0, 0.0).astype(jnp.bfloat16), features[...],
        preferred_element_type=f32,
    ).astype(jnp.bfloat16)
    token_row = (slot_row % 2 * CH + pos_row[...] % CH + 1).astype(f32)
    row_at = jnp.sum(jnp.where(chosen, token_row, 0.0), axis=1, keepdims=True) - 1.0
    row_at = row_at.astype(jnp.int32)
    high = (row_at >> 5).astype(f32)
    low = (row_at & 31).astype(f32)
    lane = lax.broadcasted_iota(jnp.int32, (entries, block), 1)
    tail = jnp.where(lane < part + 32, high, jnp.where(lane < part + 48, low, 1.0))

    pl.semaphore_wait(barrier, devices - 1)

    depth = weight.shape[2]

    def quarter(n):
        return pl.ds(depth // 4 * n, depth // 4)

    def wmove(m):
        n = m - 3
        shard = y if m < 3 else (y_up, y_down, y_far)[n // 3]
        ref = weight.at[core, shard, quarter(z)]
        if m < 3:
            ctx, tp = c, side + (y_up, y_down, y_far)[m]
        else:
            ctx, tp = 2 * (z_up, z_down, z_far)[n % 3] + core, t
        return push(ref, ref, wsend.at[m], wrecv.at[m], ctx, tp)

    def warrive(m):
        n = m - 3
        shard = (y_down, y_up, y_far)[m] if m < 3 else (y_up, y_down, y_far)[n // 3]
        origin = z if m < 3 else add4(z, (3, 1, 2)[n % 3])
        ref = weight.at[core, shard, quarter(origin)]
        push(ref, ref, wsend.at[m], wrecv.at[m], sibling, t).wait_recv()

    def share(n):
        ref = weight.at[core, add4(y, n)]
        return push(ref, ref, csend.at[n], crecv.at[n], sibling, t)

    def shared(n):
        ref = weight.at[1 - core, add4(y, n)]
        push(ref, ref, csend.at[n], crecv.at[n], sibling, t).wait_recv()

    own_copy.wait()
    for m in (2, 0, 1):
        wmove(m).start()
    share(0).start()

    for d in range(N_TP):
        j = lax.rem(t + d, N_TP)
        load(d).wait()
        x = jnp.dot(ordered, pweight[d], preferred_element_type=f32)
        x = 0.5 * x * (1.0 + lax.erf(x * math.sqrt(0.5)))
        shift = j * part - (j * part) // HS * HS
        x = jnp.where(shift > 0, pltpu.roll(x, block - HS // 2, 1), x)
        x = jnp.where(lane < part, x, tail)
        halves = [
            x[:, n * 2 * HS : (n + 1) * 2 * HS].reshape(N_CTX, CAP, 2 * HS) for n in range(2)
        ]
        outgoing[d] = jnp.concatenate(halves, axis=1).astype(jnp.bfloat16)

        def deliver(n, unused):
            oc = lax.rem(c + n, N_CTX)
            push(outgoing.at[d, oc], incoming.at[me], fr_send, fr_recv, oc, j).start()
            return unused

        if d == 0:
            pltpu.make_async_copy(outgoing.at[0, c], incoming.at[me], fr_recv).start()
        else:
            push(outgoing.at[d, c], incoming.at[me], fr_send, fr_recv, c, j).start()
        lax.fori_loop(1, N_CTX, deliver, 0)
        if d == 4:
            for m in range(3):
                warrive(m)
            for m in range(3, 12):
                wmove(m).start()

    take_text.wait()
    for a in range(2):
        for n in range(4):
            block_cols = slice((4 * a + n) * HS, (4 * a + n + 1) * HS)
            placed[a, n] = jnp.transpose(turned_text[:, block_cols].astype(f32)).astype(
                jnp.bfloat16
            )
    pltpu.make_async_copy(incoming, incoming, fr_recv).wait()

    def row_block(n, across):
        j = add4(y, n)
        tp = j + (4 - side if across else side)
        return push(
            placed.at[:, j], rows.at[t], send.at[n, across], recv.at[t], c, tp
        )

    def gain_block(d):
        return push(gain, gains.at[t], gsend.at[d], grecv.at[t], c, lax.rem(t + d, N_TP))

    pltpu.make_async_copy(gain, gains.at[t], grecv.at[t]).start()
    for d in range(1, N_TP):
        gain_block(d).start()
    arrived = incoming[...].astype(f32)
    slots = devices * CAP
    left = arrived[:, :CAP].reshape(slots, 2 * HS)
    right = arrived[:, CAP:].reshape(slots, 2 * HS)
    edge = part - 2 * HS
    at = right[:, edge : edge + 1] * 32.0 + right[:, edge + 32 : edge + 33]
    at = jnp.transpose(jnp.broadcast_to(at, (slots, HS)))[0:1, :]
    left = left.astype(jnp.bfloat16)
    right = right.astype(jnp.bfloat16)
    group = 2 * HS
    offset = lax.broadcasted_iota(jnp.int32, (group, 1), 0)
    offset = offset // HS * CH + offset % HS
    for n in range(4):
        j = add4(y, n)
        row = offset + j * HS
        hit = jnp.where(row.astype(f32) == at, 1.0, 0.0).astype(jnp.bfloat16)
        new_left = jnp.dot(hit, left, preferred_element_type=f32)
        new_right = jnp.dot(hit, right, preferred_element_type=f32)
        framed = new_right[:, 2 * HS - 1 :] > 0.5
        old = placed[:, j].reshape(group, part).astype(f32)
        placed[:, j, :, : 2 * HS] = (
            jnp.where(framed, new_left, old[:, : 2 * HS]).astype(jnp.bfloat16)
        ).reshape(2, HS, 2 * HS)
        placed[:, j, :, 2 * HS :] = (
            jnp.where(framed, new_right[:, :edge], old[:, 2 * HS :]).astype(jnp.bfloat16)
        ).reshape(2, HS, edge)
        row_block(n, 1).start()
        if n == 0:
            pltpu.make_async_copy(placed.at[:, y], rows.at[t], recv.at[t]).start()
        else:
            row_block(n, 0).start()

    for one in kv_loads:
        one.wait()

    total = jnp.zeros((group, 1), f32)
    for d in range(N_TP):
        j = lax.rem(t + d, N_TP)
        push(gain, gains.at[j], gsend.at[0], grecv.at[j], sibling, t).wait_recv()
        push(rows.at[j], rows.at[j], send.at[0, 0], recv.at[j], sibling, t).wait_recv()
        x = rows[j].reshape(group, part).astype(f32)
        total = total + jnp.sum(x * x, axis=1, keepdims=True)

    keep = pltpu.make_async_copy(rows.at[pl.ds(side, 4)], rows_out, osem)
    keep.start()

    for m in range(3, 12):
        warrive(m)
    for n in range(1, 4):
        share(n).start()
    inverse = lax.rsqrt(total / width + 1e-06)
    for j in range(N_TP):
        x = rows[j].reshape(group, part).astype(f32)
        normed[j] = (x * inverse * gains[j, 0:1, :].astype(f32)).astype(jnp.bfloat16)

    def product(piece):
        total = None
        for j in range(N_TP):
            term = jnp.dot(
                normed[j], piece(slice(j * part, (j + 1) * part)), preferred_element_type=f32
            )
            total = term if total is None else total + term
        return total

    def rotated(x, cos, sin):
        return (x * cos + pltpu.roll(x, HS // 2, 1) * sin).astype(jnp.bfloat16).reshape(2, HS, HS)

    goal = [pair_of(pair, 4 * n + y) for n in range(2)]
    mine = pl.ds(2 * core, 2)

    def kv_push(n, which, m):
        return push(
            kv.at[which, m // 2, :, pl.ds(OFF * n, OFF), :], kv_out.at[pair, mine],
            ksend.at[n, which, m], krecv.at[pair, core], 2 * goal[n] + which, side + m,
        )

    def q_push(n, k, m):
        return push(
            query.at[m, :, :, pl.ds(OFF * n + HALF * k, HALF), :], query_out.at[:, pair, mine],
            qsend.at[n, k, m], qrecv.at[pair, core], 2 * goal[n] + k, side + m,
        )

    def is_here(n, k, m):
        return jnp.logical_and(goal[n] == pair, jnp.logical_and(core == k, y == m))

    cos = cosine[...]
    sin = sine[...]
    for which in range(2):
        out = product(lambda cut: kv_weight[which, cut, :])
        for h in range(2):
            x = out[:, h * HS : (h + 1) * HS]
            kv[which, h] = rotated(x, cos, sin) if which == 0 else x.astype(
                jnp.bfloat16
            ).reshape(2, HS, HS)
        for m in range(4):
            for n in range(2):

                @pl.when(is_here(n, which, m))
                def _():
                    pltpu.make_async_copy(
                        kv.at[which, m // 2, :, pl.ds(OFF * n, OFF), :], kv_out.at[pair, mine],
                        krecv.at[pair, core],
                    ).start()

                @pl.when(jnp.logical_not(is_here(n, which, m)))
                def _():
                    kv_push(n, which, m).start()

    for m0 in range(4):
        m = add4(y, m0)
        shared(m0)
        out = product(
            lambda cut: jnp.concatenate([weight[0, m, cut], weight[1, m, cut]], axis=1)
        )
        for h in range(2):
            query[m, h] = rotated(out[:, h * HS : (h + 1) * HS], cos, sin)
        for n in range(2):
            for k in range(2):
                if m0 == 0:
                    here = jnp.logical_and(goal[n] == pair, core == k)

                    @pl.when(here)
                    def _():
                        pltpu.make_async_copy(
                            query.at[m, :, :, pl.ds(OFF * n + HALF * k, HALF), :],
                            query_out.at[:, pair, mine], qrecv.at[pair, core],
                        ).start()

                    @pl.when(jnp.logical_not(here))
                    def _():
                        q_push(n, k, m).start()

                else:
                    q_push(n, k, m).start()

    for e in range(PAIRS):
        for a in range(2):
            two = pl.ds(2 * a, 2)
            ref = kv_out.at[e, two]
            push(ref, ref, ksend.at[0, 0, 0], krecv.at[e, a], sibling, t).wait_recv()
            ref = query_out.at[:, e, two]
            push(ref, ref, qsend.at[0, 0, 0], qrecv.at[e, a], sibling, t).wait_recv()
    keep.wait()
    pltpu.make_async_copy(
        incoming.at[pl.ds(0, devices - 1)], incoming.at[pl.ds(0, devices - 1)], fr_send
    ).wait()
    for m in range(12):
        wmove(m).wait_send()
    for n in range(4):
        share(n).wait_send()
        row_block(n, 1).wait_send()
        if n:
            row_block(n, 0).wait_send()
    for d in range(1, N_TP):
        gain_block(d).wait_send()
    for n in range(2):
        for k in range(2):
            for m in range(4):

                @pl.when(jnp.logical_not(is_here(n, k, m)))
                def _():
                    kv_push(n, k, m).wait_send()
                    q_push(n, k, m).wait_send()


def intake(
    text_embed, norm_gain, frame_features, frame_positions, span_order, tables,
    projector, query_weight, key_weight, value_weight,
):
    tok_rows, part = text_embed.shape
    depth = query_weight.shape[0]
    devices = N_CTX * N_TP
    vm = pl.BlockSpec(memory_space=pltpu.VMEM)
    anywhere = pl.BlockSpec(memory_space=pl.ANY)
    dma = pltpu.SemaphoreType.DMA
    bf16 = jnp.bfloat16
    return pl.pallas_call(
        intake_kernel,
        out_shape=(
            jax.ShapeDtypeStruct((4, 2, HS, part), bf16),
            jax.ShapeDtypeStruct((2, PAIRS, 4, HALF, HS), bf16),
            jax.ShapeDtypeStruct((PAIRS, 4, OFF, HS), bf16),
        ),
        in_specs=[vm] * 5 + [anywhere] * 6,
        out_specs=(vm, vm, vm),
        scratch_shapes=[
            pltpu.VMEM(frame_features.shape, bf16),
            pltpu.VMEM((part, tok_rows), bf16),
            pltpu.VMEM((N_TP, projector.shape[0], 4 * HS), bf16),
            pltpu.VMEM((N_TP, N_CTX, 2 * CAP, 2 * HS), bf16),
            pltpu.VMEM((devices, 2 * CAP, 2 * HS), bf16),
            pltpu.VMEM((2, 4, HS, part), bf16),
            pltpu.VMEM((N_TP, 2, HS, part), bf16),
            pltpu.VMEM((N_TP, 16, part), bf16),
            pltpu.VMEM((N_TP, 2 * HS, part), bf16),
            pltpu.VMEM((2, 4, depth, HS), bf16),
            pltpu.VMEM((2, depth, 2 * HS), bf16),
            pltpu.VMEM((4, 2, 2, HS, HS), bf16),
            pltpu.VMEM((2, 2, 2, HS, HS), bf16),
            dma((2,)),
            dma((N_TP,)),
            dma,
            dma((2,)),
            dma,
            dma,
            dma((12,)),
            dma((12,)),
            dma((4,)),
            dma((4,)),
            dma((4, 2)),
            dma((N_TP,)),
            dma((N_TP,)),
            dma((N_TP,)),
            dma,
            dma((2, 2, 4)),
            dma((PAIRS, 2)),
            dma((2, 2, 4)),
            dma((PAIRS, 2)),
        ],
        compiler_params=pltpu.CompilerParams(
            collective_id=1, has_side_effects=True, vmem_limit_bytes=56 * 2**20
        ),
        name="intake",
    )(
        jnp.broadcast_to(norm_gain[None, :], (16, part)),
        frame_positions.reshape(1, -1),
        span_order.reshape(1, -1),
        *tables,
        text_embed.T,
        frame_features,
        projector,
        query_weight,
        key_weight,
        value_weight,
    )


def attention_kernel(
    slot_of, span_order, query_in, kv_in, out_weight, rows_in, out,
    query, kv_own, rows, kv, q, summed, largest, limit, attended, heads, weight, product, result,
    isem, send, recv, pass_send, wsend, wrecv, csend, crecv, own_sem,
    hsend, hrecv, rsend, rrecv,
):
    f32 = jnp.float32
    scale = LOG2E / math.sqrt(HS)
    c = lax.axis_index("ctx")
    t = lax.axis_index("tp")
    pair = c // 2
    core = c % 2
    sibling = c + 1 - 2 * core
    base = pair // 4 * 4
    other = 4 - base
    z = pair % 4
    up, down, far = (add4(z, n) for n in (1, 3, 2))
    z_up, z_down, z_far = base + up, base + down, base + far
    x_own, x_up, x_down, x_far = other + z, other + up, other + down, other + far
    y = lax.rem(t, 4)
    side = t - y
    half = t // 4
    across = 4 - side
    t_up, t_down, t_far = (side + add4(y, n) for n in (1, 3, 2))
    a_own, a_up, a_down, a_far = (across + add4(y, n) for n in (0, 1, 3, 2))
    x_next = 2 * x_own + core
    depth, cols = weight.shape[2:]

    def columns(of_half):
        return out_weight.at[:, pl.ds(pl.multiple_of(cols * (2 * of_half + core), HS), cols)]

    take_kv, take_query, take_rows = (
        pltpu.make_async_copy(src, dst, isem.at[n])
        for n, (src, dst) in enumerate(((kv_in, kv_own), (query_in, query), (rows_in, rows)))
    )
    take_kv.start()
    take_query.start()
    own_copy = pltpu.make_async_copy(columns(half), weight.at[core, t], own_sem)
    own_copy.start()
    take_rows.start()
    barrier = pltpu.get_barrier_semaphore()
    signal(barrier, sibling, t)
    for e in (z_up, z_down, z_far, x_own):
        signal(barrier, 2 * e + core, t)
    signal(barrier, x_next, a_own)
    for j in (t_up, t_down, t_far):
        signal(barrier, c, j)
    first = y == 2 * (pair // 4)
    for n in range(2):
        origin = pair_of(pair, 4 * n + y)
        for k in range(2):
            for d in range(N_TP):
                j = lax.rem(t + d, N_TP)
                if n == 0 and d == 0:

                    @pl.when(jnp.logical_not(jnp.logical_and(first, core == k)))
                    def _():
                        signal(barrier, 2 * origin + k, j)

                else:
                    signal(barrier, 2 * origin + k, j)
    take_kv.wait()
    for j in range(32):
        kv[pair, core, j * OFF : (j + 1) * OFF] = kv_own[slot_of[j]]
    pl.semaphore_wait(barrier, 9 + 32 - jnp.where(first, 1, 0))

    def wmove(m):
        own = weight.at[core, t]
        passed = weight.at[core, a_own]
        if m == 0:
            src, dst, ctx, tp = columns(1 - half), own, x_next, a_own
        else:
            src = dst = own if m < 4 else passed
            ctx, tp = c, (t_up, t_down, t_far)[(m - 1) % 3]
        return push(src, dst, wsend.at[m], wrecv.at[m], ctx, tp)

    def warrive(m):
        ref = weight.at[core, (a_own, t_down, t_up, t_far, a_down, a_up, a_far)[m]]
        push(ref, ref, wsend.at[m], wrecv.at[m], sibling, t).wait_recv()

    def give(g):
        ref = weight.at[core, g]
        return push(ref, ref, csend.at[g], crecv.at[g], sibling, t)

    def transfer(e, to, index):
        block = kv.at[e, core]
        return push(block, block, send.at[index], recv.at[e, core], 2 * to + core, t)

    def share(e):
        block = kv.at[e, core]
        return push(block, block, pass_send.at[e], recv.at[e, core], sibling, t)

    def arrive(e, which):
        block = kv.at[e, which]
        push(block, block, send.at[0], recv.at[e, which], sibling, t).wait_recv()

    share(pair).start()
    moves = (
        (pair, x_own), (pair, z_up), (pair, z_down), (pair, z_far),
        (x_own, z_up), (x_own, z_down), (z_far, x_own),
    )
    for index in range(3):
        transfer(*moves[index], index).start()
    own_copy.wait()
    for m in (1, 2, 3):
        wmove(m).start()
    take_query.wait()
    for j in range(32):
        q[j * OFF : (j + 1) * OFF] = query[:, slot_of[j]].reshape(2 * HALF, HS)

    group = 8 * HALF
    row = lax.broadcasted_iota(jnp.int32, (group, 1), 0)
    col = lax.broadcasted_iota(jnp.int32, (1, 4 * OFF), 1)

    def starts(index, i, e):
        value = jnp.zeros(index.shape, jnp.int32)
        for a in range(4):
            kind = class_of(slot_of[4 * i + a] // 4, e)
            start = a * CH + HS * lax.rem(kind, 4) + OFF * (kind // 4)
            value = jnp.where(index // OFF == a, start, value)
        return value

    for i in range(8):
        limit[i * group : (i + 1) * group] = starts(row, i, pair) + HALF * core + row % HALF

    def update(e, first_set):
        def chunk(i):
            return slice(i * group, (i + 1) * group), 4 * OFF * (i + 1)

        def scores(i):
            here, width = chunk(i)
            return lax.dot_general(
                q[here], kv[e, 0, :width], (((1,), (1,)), ((), ())), preferred_element_type=f32
            )

        def soft(i, s):
            here, width = chunk(i)
            at = starts(col, i, e) + col % OFF
            edge = jnp.where(at <= limit[here], s[:, width - 4 * OFF :], -1e30)
            s = edge if i == 0 else jnp.concatenate([s[:, : width - 4 * OFF], edge], axis=1)
            top = jnp.max(s, axis=1, keepdims=True)
            if not first_set:
                top = jnp.maximum(top, largest[here])
                summed[here] = summed[here] * jnp.exp2((largest[here] - top) * scale)
            largest[here] = top
            return jnp.exp2((s - top) * scale).astype(jnp.bfloat16)

        def gather(i, weights):
            here, width = chunk(i)
            beside = jnp.concatenate(
                [kv[e, 1, :width], jnp.ones((width, HS), jnp.bfloat16)], axis=1
            )
            new = jnp.dot(weights, beside, preferred_element_type=f32)
            summed[here] = new if first_set else summed[here] + new

        s = scores(0)
        held = None
        for i in range(8):
            ahead = scores(i + 1) if i < 7 else None
            weights = soft(i, s)
            if held is not None:
                gather(*held)
            held = (i, weights)
            s = ahead
        gather(*held)

    arrive(pair, 1 - core)
    update(pair, True)
    arrive(x_own, core)
    share(x_own).start()
    transfer(*moves[1], 1).wait_send()
    transfer(*moves[2], 2).wait_send()
    transfer(*moves[3], 3).start()
    wmove(0).start()
    give(t).start()
    order = (x_own, z_up, z_down, z_far, x_up, x_down, x_far)

    def step(n, unused):
        e = order[6]
        for index in range(6):
            e = jnp.where(n == index, order[index], e)

        @pl.when(n == 1)
        def _():
            arrive(z_up, core)
            share(z_up).start()
            arrive(z_down, core)
            share(z_down).start()

        @pl.when(n == 2)
        def _():
            transfer(*moves[3], 3).wait_send()
            transfer(*moves[4], 4).start()
            transfer(*moves[5], 5).start()
            arrive(z_far, core)
            transfer(*moves[6], 6).start()
            share(z_far).start()

        @pl.when(n == 4)
        def _():
            warrive(0)
            for m in (4, 5, 6):
                wmove(m).start()
            give(a_own).start()
            arrive(x_up, core)
            share(x_up).start()
            arrive(x_down, core)
            share(x_down).start()

        @pl.when(n == 6)
        def _():
            arrive(x_far, core)
            share(x_far).start()

        arrive(e, 1 - core)
        update(e, False)
        return unused

    lax.fori_loop(0, 7, step, 0)

    for i in range(8):
        here = slice(i * group, (i + 1) * group)
        done = (summed[here, :HS] / summed[here, HS : HS + 1]).astype(jnp.bfloat16)
        done = done.reshape(4, 2, HALF, HS)
        for a in range(4):
            attended[0, 4 * i + a] = jnp.concatenate([done[a, 0], done[a, 1]], axis=1)

    def head_push(d, a, n):
        e = lax.rem(pair + d, PAIRS)
        kind = class_of(e, pair)
        at = pl.ds(OFF * (kind // 4) + HALF * core, HALF)
        return push(
            attended.at[1, pl.ds(4 * e + 2 * a, 2)], heads.at[t, :, at, :], hsend.at[d, a, n],
            hrecv.at[t, kind // 4, core], 2 * e + a, lax.rem(4 * n + lax.rem(kind, 4) + side, N_TP),
        )

    def is_here(d, a, n):
        if d or n:
            return jnp.bool_(False)
        return jnp.logical_and(first, core == a)

    for j in range(32):
        attended[1, j] = attended[0, span_order[j]]
    for d in range(PAIRS):
        for n in range(2):
            for a in range(2):
                if d or n:
                    head_push(d, a, n).start()
                else:

                    @pl.when(is_here(d, a, n))
                    def _():
                        pltpu.make_async_copy(
                            attended.at[1, pl.ds(4 * pair + 2 * a, 2)],
                            heads.at[t, :, pl.ds(HALF * core, HALF), :], hrecv.at[t, 0, core],
                        ).start()

                    @pl.when(jnp.logical_not(is_here(d, a, n)))
                    def _():
                        head_push(d, a, n).start()

    for m in range(1, 7):
        warrive(m)
    for g in (t_up, t_down, t_far, a_up, a_down, a_far):
        give(g).start()
    for g in range(N_TP):
        ref = weight.at[1 - core, g]
        push(ref, ref, csend.at[g], crecv.at[g], sibling, t).wait_recv()
    for g in range(N_TP):
        for n in range(2):
            for k in range(2):
                ref = heads.at[g, :, pl.ds(OFF * n + HALF * k, HALF), :]
                push(ref, ref, hsend.at[0, 0, 0], hrecv.at[g, n, k], sibling, t).wait_recv()

    take_rows.wait()

    part = out.shape[-1]
    place = pl.ds(HS * y, HS)

    def send_home(n):
        return push(
            result.at[n], out.at[:, place, :], rsend.at[n], rrecv.at[y], c, side + n
        )

    for n in range(4):
        if n % 2 == 0:
            for begin, end in ((0, 4 * HS), (4 * HS, cols)):
                total = jnp.zeros((2 * HS, end - begin), f32)
                for g in range(N_TP):
                    x = heads[g].reshape(2 * HS, 2 * HS)
                    total = total + jnp.dot(
                        x, weight[n // 2, g, :, begin:end], preferred_element_type=f32
                    ).astype(jnp.bfloat16).astype(f32)
                product[:, begin:end] = total
            total = product[:, : 4 * HS][:, :part]
        else:
            start = part // HS * HS
            total = product[:, start : start + 4 * HS]
            total = pltpu.roll(total, 4 * HS - (part - start), 1)[:, :part]
        placed = rows[n].reshape(2 * HS, part).astype(f32)
        result[n] = (placed + total).astype(jnp.bfloat16).reshape(2, HS, part)

        @pl.when(y == n)
        def _():
            pltpu.make_async_copy(result.at[n], out.at[:, place, :], rrecv.at[y]).start()

        @pl.when(y != n)
        def _():
            send_home(n).start()

    for n in range(4):
        ref = out.at[:, pl.ds(HS * n, HS), :]
        push(ref, ref, rsend.at[0], rrecv.at[n], sibling, t).wait_recv()
    for index in (0, 4, 5, 6):
        transfer(*moves[index], index).wait_send()
    for e in range(PAIRS):
        share(e).wait_send()
    for m in range(7):
        wmove(m).wait_send()
    for g in range(N_TP):
        give(g).wait_send()
    for d in range(PAIRS):
        for n in range(2):
            for a in range(2):
                if d or n:
                    head_push(d, a, n).wait_send()
                else:

                    @pl.when(jnp.logical_not(is_here(d, a, n)))
                    def _():
                        head_push(d, a, n).wait_send()

    for n in range(4):

        @pl.when(y != n)
        def _():
            send_home(n).wait_send()


def attention(slot_of, span_order, query, kv, out_weight, rows):
    vm = pl.BlockSpec(memory_space=pltpu.VMEM)
    sm = pl.BlockSpec(memory_space=pltpu.SMEM)
    anywhere = pl.BlockSpec(memory_space=pl.ANY)
    dma = pltpu.SemaphoreType.DMA
    bf16 = jnp.bfloat16
    keys = 32 * OFF
    depth, width = out_weight.shape
    part = rows.shape[-1]
    return pl.pallas_call(
        attention_kernel,
        out_shape=jax.ShapeDtypeStruct((2, CH, part), bf16),
        in_specs=[sm, sm, anywhere, anywhere, anywhere, anywhere],
        out_specs=vm,
        scratch_shapes=[
            pltpu.VMEM(query.shape, bf16),
            pltpu.VMEM(kv.shape, bf16),
            pltpu.VMEM(rows.shape, bf16),
            pltpu.VMEM((PAIRS, 2, keys, HS), bf16),
            pltpu.VMEM((keys, HS), bf16),
            pltpu.VMEM((keys, 2 * HS), jnp.float32),
            pltpu.VMEM((keys, 1), jnp.float32),
            pltpu.VMEM((keys, 1), jnp.int32),
            pltpu.VMEM((2, 32, HALF, 2 * HS), bf16),
            pltpu.VMEM((N_TP, 2, HS, 2 * HS), bf16),
            pltpu.VMEM((2, N_TP, depth, width // 4), bf16),
            pltpu.VMEM((2 * HS, width // 4), jnp.float32),
            pltpu.VMEM((4, 2, HS, part), bf16),
            dma((3,)),
            dma((7,)),
            dma((PAIRS, 2)),
            dma((PAIRS,)),
            dma((7,)),
            dma((7,)),
            dma((N_TP,)),
            dma((N_TP,)),
            dma,
            dma((PAIRS, 2, 2)),
            dma((N_TP, 2, 2)),
            dma((4,)),
            dma((4,)),
        ],
        compiler_params=pltpu.CompilerParams(
            collective_id=2, has_side_effects=True, vmem_limit_bytes=60 * 2**20
        ),
        name="attention",
    )(slot_of, span_order, query, kv, out_weight, rows)


def per_device(
    text_embed,
    frame_features,
    frame_positions,
    span_order,
    projector,
    norm_gain,
    query_weight,
    key_weight,
    value_weight,
    out_weight,
):
    tok_rows, part = text_embed.shape
    c = lax.axis_index("ctx")
    t = lax.axis_index("tp")
    slots = span_order.shape[0]
    index = jnp.arange(slots, dtype=jnp.int32)
    slot_of = jnp.sum(
        jnp.where(span_order[None, :] == index[:, None], index[None, :], 0), axis=1
    )
    spans = lax.dynamic_slice_in_dim(span_order, 2 * c, 2, 0)
    positions = (
        spans[:, None] * CH + HS * (t % 4) + jnp.arange(HS, dtype=jnp.int32)[None, :]
    ).reshape(-1)
    half = HS // 2
    lane = jnp.arange(HS, dtype=jnp.int32)
    freqs = 1000000.0 ** (-((lane % half).astype(jnp.float32) * 2.0 / HS))
    angles = positions.astype(jnp.float32)[:, None] * freqs[None, :]
    cosine = jnp.cos(angles)
    sine = jnp.where(lane[None, :] < half, -1.0, 1.0) * jnp.sin(angles)
    rows, query, kv = intake(
        text_embed, norm_gain, frame_features, frame_positions, span_order, (cosine, sine),
        projector, query_weight, key_weight, value_weight,
    )
    mixed = attention(
        slot_of, span_order, query.reshape(2, 32, HALF, HS), kv.reshape(32, OFF, HS),
        out_weight, rows,
    )
    return mixed.reshape(tok_rows, part)


def solution(mesh):
    in_specs = (
        P("ctx", "tp"),
        P(("ctx", "tp"), None),
        P(("ctx", "tp")),
        P(),
        P(),
        P("tp"),
        P(None, "tp"),
        P(),
        P(),
        P("tp", None),
    )
    out_specs = P("ctx", "tp")
    return jax.shard_map(
        per_device, mesh=mesh, in_specs=in_specs, out_specs=out_specs, check_vma=False
    )
```

```python
import functools
import math

import jax
import jax.numpy as jnp
from jax import lax
from jax.experimental import pallas as pl
from jax.experimental.pallas import tpu as pltpu
from jax.sharding import PartitionSpec as P

HS = 128
KVH = 4
CAP = 8
CH = 512
N_CTX = 16
N_TP = 8
PAIRS = 8
OFF = 64
HALF = 32
MESH = pl.DeviceIdType.MESH
LOG2E = math.log2(math.e)


def signal(sem, ctx, tp):
    pl.semaphore_signal(sem, inc=1, device_id=(ctx, tp), device_id_type=MESH)


def push(src, dst, send_sem, recv_sem, ctx, tp):
    return pltpu.make_async_remote_copy(
        src_ref=src, dst_ref=dst, send_sem=send_sem, recv_sem=recv_sem,
        device_id=(ctx, tp), device_id_type=MESH,
    )


def add4(a, b):
    return lax.rem(a + b + 4, 4)


def pair_of(e, t):
    x = lax.rem(e // 4 + t // 4, 2)
    return x * 4 + lax.rem(lax.rem(e, 4) + lax.rem(t, 4) + 2 * x, 4)


def class_of(e, pair):
    x = pair // 4
    return lax.rem(e // 4 + x, 2) * 4 + lax.rem(lax.rem(pair, 4) - lax.rem(e, 4) + 2 * x + 4, 4)


def intake_kernel(
    gain, pos_row, order_row, cosine, sine,
    text, frame_features, projector, query_weight, key_weight, value_weight,
    rows_out, query_out, kv_out,
    features, turned_text, pweight, outgoing, incoming, placed, rows, gains, normed, weight, kv_weight, query, kv,
    tsem, psem, own_sem, kv_sem, fr_send, fr_recv, wsend, wrecv, csend, crecv,
    send, recv, gsend, grecv, osem, qsend, qrecv, ksend, krecv,
):
    c = lax.axis_index("ctx")
    t = lax.axis_index("tp")
    pair = c // 2
    core = c % 2
    sibling = c + 1 - 2 * core
    devices = N_CTX * N_TP
    me = c * N_TP + t
    part = text.shape[0]
    width = N_TP * part
    base = pair // 4 * 4
    z = pair % 4
    z_up, z_down, z_far = (base + add4(z, n) for n in (1, 3, 2))
    y = lax.rem(t, 4)
    side = t - y
    half = t // 4
    y_up, y_down, y_far = (add4(y, n) for n in (1, 3, 2))

    own_copy = pltpu.make_async_copy(
        query_weight.at[:, pl.ds(pl.multiple_of(HS * core, HS), HS)], weight.at[core, y], own_sem
    )
    own_copy.start()
    block = 4 * HS
    take_features = pltpu.make_async_copy(frame_features, features, tsem.at[0])
    take_features.start()
    take_text = pltpu.make_async_copy(text, turned_text, tsem.at[1])

    def load(d):
        j = lax.rem(t + d, N_TP)
        start = pl.multiple_of((j * part) // HS * HS, HS)
        return pltpu.make_async_copy(
            projector.at[:, pl.ds(start, block)], pweight.at[d], psem.at[d]
        )

    for d in range(N_TP):
        load(d).start()
    kv_cols = pl.ds(pl.multiple_of(2 * HS * half, HS), 2 * HS)
    kv_loads = [
        pltpu.make_async_copy(ref.at[:, kv_cols], kv_weight.at[n], kv_sem.at[n])
        for n, ref in enumerate((key_weight, value_weight))
    ]
    take_text.start()
    for one in kv_loads:
        one.start()

    barrier = pltpu.get_barrier_semaphore()

    def greet(d, unused):
        other = lax.rem(me + d, devices)
        signal(barrier, other // N_TP, lax.rem(other, N_TP))
        return unused

    lax.fori_loop(1, devices, greet, 0)

    f32 = jnp.float32
    spans = order_row.shape[1]
    tokens = pos_row.shape[1]
    entries = N_CTX * CAP

    def turned(x):
        size = x.shape[1]
        same = lax.broadcasted_iota(jnp.int32, (size, size), 0) == lax.broadcasted_iota(
            jnp.int32, (size, size), 1
        )
        return jnp.sum(jnp.where(same, x, 0.0), axis=1, keepdims=True)

    order_col = turned(order_row[...].astype(f32))
    slot_row = jnp.sum(
        jnp.where(
            order_col == (pos_row[...] // CH).astype(f32),
            lax.broadcasted_iota(jnp.int32, (spans, tokens), 0).astype(f32), 0.0,
        ),
        axis=0, keepdims=True,
    )
    slot_col = turned(slot_row).astype(jnp.int32)
    slot_row = slot_row.astype(jnp.int32)
    first = lax.broadcasted_iota(jnp.int32, (tokens, tokens), 0)
    second = lax.broadcasted_iota(jnp.int32, (tokens, tokens), 1)
    earlier = jnp.logical_and(slot_col // 2 == slot_row // 2, first < second)
    place = jnp.sum(jnp.where(earlier, 1.0, 0.0), axis=0, keepdims=True).astype(jnp.int32)
    entry = slot_row // 2 * CAP + place
    chosen = lax.broadcasted_iota(jnp.int32, (entries, tokens), 0) == entry
    take_features.wait()
    ordered = jnp.dot(
        jnp.where(chosen, 1.0, 0.0).astype(jnp.bfloat16), features[...],
        preferred_element_type=f32,
    ).astype(jnp.bfloat16)
    token_row = (slot_row % 2 * CH + pos_row[...] % CH + 1).astype(f32)
    row_at = jnp.sum(jnp.where(chosen, token_row, 0.0), axis=1, keepdims=True) - 1.0
    row_at = row_at.astype(jnp.int32)
    high = (row_at >> 5).astype(f32)
    low = (row_at & 31).astype(f32)
    lane = lax.broadcasted_iota(jnp.int32, (entries, block), 1)
    tail = jnp.where(lane < part + 32, high, jnp.where(lane < part + 48, low, 1.0))

    pl.semaphore_wait(barrier, devices - 1)

    depth = weight.shape[2]

    def quarter(n):
        return pl.ds(depth // 4 * n, depth // 4)

    def half_quarter(n, second):
        return pl.ds(depth // 4 * n + depth // 8 * second, depth // 8)

    z_next = (add4(z, 1), add4(z, 3))
    y_others = (y_up, y_down, y_far)

    def wmove(m):
        if m < 3:
            ref, ctx, tp = weight.at[core, y, quarter(z)], c, side + y_others[m]
        else:
            n, up = (m - 3) % 6 // 2, (m - 3) % 2
            cut = quarter(z) if m < 9 else half_quarter(z_next[1 - up], up)
            ref, tp = weight.at[core, y_others[n], cut], t
            ctx = 2 * (z_up, z_down)[up] + core
        return push(ref, ref, wsend.at[m], wrecv.at[m], ctx, tp)

    def warrive(m):
        if m < 3:
            ref = weight.at[core, (y_down, y_up, y_far)[m], quarter(z)]
        else:
            n, up = (m - 3) % 6 // 2, (m - 3) % 2
            cut = quarter(z_next[1 - up]) if m < 9 else half_quarter(add4(z, 2), up)
            ref = weight.at[core, y_others[n], cut]
        push(ref, ref, wsend.at[m], wrecv.at[m], sibling, t).wait_recv()

    def share(n):
        ref = weight.at[core, add4(y, n)]
        return push(ref, ref, csend.at[n], crecv.at[n], sibling, t)

    def shared(n):
        ref = weight.at[1 - core, add4(y, n)]
        push(ref, ref, csend.at[n], crecv.at[n], sibling, t).wait_recv()

    own_copy.wait()
    for m in (2, 0, 1):
        wmove(m).start()
    share(0).start()

    for d in range(N_TP):
        j = lax.rem(t + d, N_TP)
        load(d).wait()
        x = jnp.dot(ordered, pweight[d], preferred_element_type=f32)
        x = 0.5 * x * (1.0 + lax.erf(x * math.sqrt(0.5)))
        shift = j * part - (j * part) // HS * HS
        x = jnp.where(shift > 0, pltpu.roll(x, block - HS // 2, 1), x)
        x = jnp.where(lane < part, x, tail)
        halves = [
            x[:, n * 2 * HS : (n + 1) * 2 * HS].reshape(N_CTX, CAP, 2 * HS) for n in range(2)
        ]
        outgoing[d] = jnp.concatenate(halves, axis=1).astype(jnp.bfloat16)

        def deliver(n, unused):
            oc = lax.rem(c + n, N_CTX)
            push(outgoing.at[d, oc], incoming.at[me], fr_send, fr_recv, oc, j).start()
            return unused

        if d == 0:
            pltpu.make_async_copy(outgoing.at[0, c], incoming.at[me], fr_recv).start()
        else:
            push(outgoing.at[d, c], incoming.at[me], fr_send, fr_recv, c, j).start()
        lax.fori_loop(1, N_CTX, deliver, 0)
        if d == 4:
            for m in range(3):
                warrive(m)
            for m in range(3, 9):
                wmove(m).start()

    take_text.wait()
    for a in range(2):
        for n in range(4):
            block_cols = slice((4 * a + n) * HS, (4 * a + n + 1) * HS)
            placed[a, n] = jnp.transpose(turned_text[:, block_cols].astype(f32)).astype(
                jnp.bfloat16
            )
    pltpu.make_async_copy(incoming, incoming, fr_recv).wait()

    def row_block(n, across):
        j = add4(y, n)
        tp = j + (4 - side if across else side)
        return push(
            placed.at[:, j], rows.at[t], send.at[n, across], recv.at[t], c, tp
        )

    def gain_block(d):
        return push(gain, gains.at[t], gsend.at[d], grecv.at[t], c, lax.rem(t + d, N_TP))

    pltpu.make_async_copy(gain, gains.at[t], grecv.at[t]).start()
    for d in range(1, N_TP):
        gain_block(d).start()
    arrived = incoming[...].astype(f32)
    slots = devices * CAP
    left = arrived[:, :CAP].reshape(slots, 2 * HS)
    right = arrived[:, CAP:].reshape(slots, 2 * HS)
    edge = part - 2 * HS
    at = right[:, edge : edge + 1] * 32.0 + right[:, edge + 32 : edge + 33]
    at = jnp.transpose(jnp.broadcast_to(at, (slots, HS)))[0:1, :]
    left = left.astype(jnp.bfloat16)
    right = right.astype(jnp.bfloat16)
    group = 2 * HS
    offset = lax.broadcasted_iota(jnp.int32, (group, 1), 0)
    offset = offset // HS * CH + offset % HS
    for n in range(4):
        j = add4(y, n)
        row = offset + j * HS
        hit = jnp.where(row.astype(f32) == at, 1.0, 0.0).astype(jnp.bfloat16)
        new_left = jnp.dot(hit, left, preferred_element_type=f32)
        new_right = jnp.dot(hit, right, preferred_element_type=f32)
        framed = new_right[:, 2 * HS - 1 :] > 0.5
        old = placed[:, j].reshape(group, part).astype(f32)
        placed[:, j, :, : 2 * HS] = (
            jnp.where(framed, new_left, old[:, : 2 * HS]).astype(jnp.bfloat16)
        ).reshape(2, HS, 2 * HS)
        placed[:, j, :, 2 * HS :] = (
            jnp.where(framed, new_right[:, :edge], old[:, 2 * HS :]).astype(jnp.bfloat16)
        ).reshape(2, HS, edge)
        row_block(n, 1).start()
        if n == 0:
            pltpu.make_async_copy(placed.at[:, y], rows.at[t], recv.at[t]).start()
        else:
            row_block(n, 0).start()

    for one in kv_loads:
        one.wait()

    for m in range(3, 9):
        warrive(m)
    for m in range(9, 15):
        wmove(m).start()
    total = jnp.zeros((group, 1), f32)
    for d in range(N_TP):
        j = lax.rem(t + d, N_TP)
        push(gain, gains.at[j], gsend.at[0], grecv.at[j], sibling, t).wait_recv()
        push(rows.at[j], rows.at[j], send.at[0, 0], recv.at[j], sibling, t).wait_recv()
        x = rows[j].reshape(group, part).astype(f32)
        total = total + jnp.sum(x * x, axis=1, keepdims=True)

    keep = pltpu.make_async_copy(rows.at[pl.ds(side, 4)], rows_out, osem)
    keep.start()

    for m in range(9, 15):
        warrive(m)
    for n in range(1, 4):
        share(n).start()
    inverse = lax.rsqrt(total / width + 1e-06)
    for j in range(N_TP):
        x = rows[j].reshape(group, part).astype(f32)
        normed[j] = (x * inverse * gains[j, 0:1, :].astype(f32)).astype(jnp.bfloat16)

    def product(piece):
        total = None
        for j in range(N_TP):
            term = jnp.dot(
                normed[j], piece(slice(j * part, (j + 1) * part)), preferred_element_type=f32
            )
            total = term if total is None else total + term
        return total

    def rotated(x, cos, sin):
        return (x * cos + pltpu.roll(x, HS // 2, 1) * sin).astype(jnp.bfloat16).reshape(2, HS, HS)

    goal = [pair_of(pair, 4 * n + y) for n in range(2)]
    mine = pl.ds(2 * core, 2)

    def kv_push(n, which, m):
        return push(
            kv.at[which, m // 2, :, pl.ds(OFF * n, OFF), :], kv_out.at[pair, mine],
            ksend.at[n, which, m], krecv.at[pair, core], 2 * goal[n] + which, side + m,
        )

    def q_push(n, k, m):
        return push(
            query.at[m, :, :, pl.ds(OFF * n + HALF * k, HALF), :], query_out.at[:, pair, mine],
            qsend.at[n, k, m], qrecv.at[pair, core], 2 * goal[n] + k, side + m,
        )

    def is_here(n, k, m):
        return jnp.logical_and(goal[n] == pair, jnp.logical_and(core == k, y == m))

    cos = cosine[...]
    sin = sine[...]
    for which in range(2):
        out = product(lambda cut: kv_weight[which, cut, :])
        for h in range(2):
            x = out[:, h * HS : (h + 1) * HS]
            kv[which, h] = rotated(x, cos, sin) if which == 0 else x.astype(
                jnp.bfloat16
            ).reshape(2, HS, HS)
        for m in range(4):
            for n in range(2):

                @pl.when(is_here(n, which, m))
                def _():
                    pltpu.make_async_copy(
                        kv.at[which, m // 2, :, pl.ds(OFF * n, OFF), :], kv_out.at[pair, mine],
                        krecv.at[pair, core],
                    ).start()

                @pl.when(jnp.logical_not(is_here(n, which, m)))
                def _():
                    kv_push(n, which, m).start()

    for m0 in range(4):
        m = add4(y, m0)
        shared(m0)
        out = product(
            lambda cut: jnp.concatenate([weight[0, m, cut], weight[1, m, cut]], axis=1)
        )
        for h in range(2):
            query[m, h] = rotated(out[:, h * HS : (h + 1) * HS], cos, sin)
        for n in range(2):
            for k in range(2):
                if m0 == 0:
                    here = jnp.logical_and(goal[n] == pair, core == k)

                    @pl.when(here)
                    def _():
                        pltpu.make_async_copy(
                            query.at[m, :, :, pl.ds(OFF * n + HALF * k, HALF), :],
                            query_out.at[:, pair, mine], qrecv.at[pair, core],
                        ).start()

                    @pl.when(jnp.logical_not(here))
                    def _():
                        q_push(n, k, m).start()

                else:
                    q_push(n, k, m).start()

    for e in range(PAIRS):
        for a in range(2):
            two = pl.ds(2 * a, 2)
            ref = kv_out.at[e, two]
            push(ref, ref, ksend.at[0, 0, 0], krecv.at[e, a], sibling, t).wait_recv()
            ref = query_out.at[:, e, two]
            push(ref, ref, qsend.at[0, 0, 0], qrecv.at[e, a], sibling, t).wait_recv()
    keep.wait()
    pltpu.make_async_copy(
        incoming.at[pl.ds(0, devices - 1)], incoming.at[pl.ds(0, devices - 1)], fr_send
    ).wait()
    for m in range(15):
        wmove(m).wait_send()
    for n in range(4):
        share(n).wait_send()
        row_block(n, 1).wait_send()
        if n:
            row_block(n, 0).wait_send()
    for d in range(1, N_TP):
        gain_block(d).wait_send()
    for n in range(2):
        for k in range(2):
            for m in range(4):

                @pl.when(jnp.logical_not(is_here(n, k, m)))
                def _():
                    kv_push(n, k, m).wait_send()
                    q_push(n, k, m).wait_send()


def intake(
    text_embed, norm_gain, frame_features, frame_positions, span_order, tables,
    projector, query_weight, key_weight, value_weight,
):
    tok_rows, part = text_embed.shape
    depth = query_weight.shape[0]
    devices = N_CTX * N_TP
    vm = pl.BlockSpec(memory_space=pltpu.VMEM)
    anywhere = pl.BlockSpec(memory_space=pl.ANY)
    dma = pltpu.SemaphoreType.DMA
    bf16 = jnp.bfloat16
    return pl.pallas_call(
        intake_kernel,
        out_shape=(
            jax.ShapeDtypeStruct((4, 2, HS, part), bf16),
            jax.ShapeDtypeStruct((2, PAIRS, 4, HALF, HS), bf16),
            jax.ShapeDtypeStruct((PAIRS, 4, OFF, HS), bf16),
        ),
        in_specs=[vm] * 5 + [anywhere] * 6,
        out_specs=(vm, vm, vm),
        scratch_shapes=[
            pltpu.VMEM(frame_features.shape, bf16),
            pltpu.VMEM((part, tok_rows), bf16),
            pltpu.VMEM((N_TP, projector.shape[0], 4 * HS), bf16),
            pltpu.VMEM((N_TP, N_CTX, 2 * CAP, 2 * HS), bf16),
            pltpu.VMEM((devices, 2 * CAP, 2 * HS), bf16),
            pltpu.VMEM((2, 4, HS, part), bf16),
            pltpu.VMEM((N_TP, 2, HS, part), bf16),
            pltpu.VMEM((N_TP, 16, part), bf16),
            pltpu.VMEM((N_TP, 2 * HS, part), bf16),
            pltpu.VMEM((2, 4, depth, HS), bf16),
            pltpu.VMEM((2, depth, 2 * HS), bf16),
            pltpu.VMEM((4, 2, 2, HS, HS), bf16),
            pltpu.VMEM((2, 2, 2, HS, HS), bf16),
            dma((2,)),
            dma((N_TP,)),
            dma,
            dma((2,)),
            dma,
            dma,
            dma((15,)),
            dma((15,)),
            dma((4,)),
            dma((4,)),
            dma((4, 2)),
            dma((N_TP,)),
            dma((N_TP,)),
            dma((N_TP,)),
            dma,
            dma((2, 2, 4)),
            dma((PAIRS, 2)),
            dma((2, 2, 4)),
            dma((PAIRS, 2)),
        ],
        compiler_params=pltpu.CompilerParams(
            collective_id=1, has_side_effects=True, vmem_limit_bytes=56 * 2**20
        ),
        name="intake",
    )(
        jnp.broadcast_to(norm_gain[None, :], (16, part)),
        frame_positions.reshape(1, -1),
        span_order.reshape(1, -1),
        *tables,
        text_embed.T,
        frame_features,
        projector,
        query_weight,
        key_weight,
        value_weight,
    )


def attention_kernel(
    slot_of, span_order, query_in, kv_in, out_weight, rows_in, out,
    query, kv_own, rows, kv, q, summed, largest, limit, attended, heads, weight, product, result,
    isem, send, recv, pass_send, half_send, half_recv, wsend, wrecv, csend, crecv, own_sem,
    hsend, hrecv, rsend, rrecv,
):
    f32 = jnp.float32
    scale = LOG2E / math.sqrt(HS)
    c = lax.axis_index("ctx")
    t = lax.axis_index("tp")
    pair = c // 2
    core = c % 2
    sibling = c + 1 - 2 * core
    base = pair // 4 * 4
    other = 4 - base
    z = pair % 4
    up, down, far = (add4(z, n) for n in (1, 3, 2))
    z_up, z_down, z_far = base + up, base + down, base + far
    keys = kv.shape[2]
    x_own, x_up, x_down, x_far = other + z, other + up, other + down, other + far
    y = lax.rem(t, 4)
    side = t - y
    half = t // 4
    across = 4 - side
    t_up, t_down, t_far = (side + add4(y, n) for n in (1, 3, 2))
    a_own, a_up, a_down, a_far = (across + add4(y, n) for n in (0, 1, 3, 2))
    x_next = 2 * x_own + core
    depth, cols = weight.shape[2:]

    def columns(of_half):
        return out_weight.at[:, pl.ds(pl.multiple_of(cols * (2 * of_half + core), HS), cols)]

    take_kv, take_query, take_rows = (
        pltpu.make_async_copy(src, dst, isem.at[n])
        for n, (src, dst) in enumerate(((kv_in, kv_own), (query_in, query), (rows_in, rows)))
    )
    take_kv.start()
    take_query.start()
    own_copy = pltpu.make_async_copy(columns(half), weight.at[core, t], own_sem)
    own_copy.start()
    take_rows.start()
    barrier = pltpu.get_barrier_semaphore()
    signal(barrier, sibling, t)
    for e in (z_up, z_down, z_far, x_own):
        signal(barrier, 2 * e + core, t)
    signal(barrier, x_next, a_own)
    for j in (t_up, t_down, t_far):
        signal(barrier, c, j)
    first = y == 2 * (pair // 4)
    for n in range(2):
        origin = pair_of(pair, 4 * n + y)
        for k in range(2):
            for d in range(N_TP):
                j = lax.rem(t + d, N_TP)
                if n == 0 and d == 0:

                    @pl.when(jnp.logical_not(jnp.logical_and(first, core == k)))
                    def _():
                        signal(barrier, 2 * origin + k, j)

                else:
                    signal(barrier, 2 * origin + k, j)
    take_kv.wait()
    for j in range(32):
        kv[pair, core, j * OFF : (j + 1) * OFF] = kv_own[slot_of[j]]
    pl.semaphore_wait(barrier, 9 + 32 - jnp.where(first, 1, 0))

    def wmove(m):
        own = weight.at[core, t]
        passed = weight.at[core, a_own]
        if m == 0:
            src, dst, ctx, tp = columns(1 - half), own, x_next, a_own
        else:
            src = dst = own if m < 4 else passed
            ctx, tp = c, (t_up, t_down, t_far)[(m - 1) % 3]
        return push(src, dst, wsend.at[m], wrecv.at[m], ctx, tp)

    def warrive(m):
        ref = weight.at[core, (a_own, t_down, t_up, t_far, a_down, a_up, a_far)[m]]
        push(ref, ref, wsend.at[m], wrecv.at[m], sibling, t).wait_recv()

    def give(g):
        ref = weight.at[core, g]
        return push(ref, ref, csend.at[g], crecv.at[g], sibling, t)

    def transfer(e, to, index):
        block = kv.at[e, core]
        return push(block, block, send.at[index], recv.at[e, core], 2 * to + core, t)

    def share(e):
        block = kv.at[e, core]
        return push(block, block, pass_send.at[e], recv.at[e, core], sibling, t)

    def arrive(e, which):
        block = kv.at[e, which]
        push(block, block, send.at[0], recv.at[e, which], sibling, t).wait_recv()

    share(pair).start()
    moves = (
        (pair, x_own), (pair, z_up), (pair, z_down), (x_own, z_up), (x_own, z_down), (z_far, x_own),
    )

    def pass_half(n):
        e, to = ((z_down, z_up), (z_up, z_down))[n]
        block = kv.at[e, core, pl.ds(keys // 2 * n, keys // 2)]
        return push(block, block, half_send.at[n], half_recv.at[n], 2 * to + core, t)

    def arrive_half(n):
        block = kv.at[z_far, core, pl.ds(keys // 2 * n, keys // 2)]
        push(block, block, half_send.at[n], half_recv.at[n], sibling, t).wait_recv()

    for index in range(3):
        transfer(*moves[index], index).start()
    own_copy.wait()
    for m in (1, 2, 3):
        wmove(m).start()
    take_query.wait()
    for j in range(32):
        q[j * OFF : (j + 1) * OFF] = query[:, slot_of[j]].reshape(2 * HALF, HS)

    group = 8 * HALF
    row = lax.broadcasted_iota(jnp.int32, (group, 1), 0)
    col = lax.broadcasted_iota(jnp.int32, (1, 4 * OFF), 1)

    def starts(index, i, e):
        value = jnp.zeros(index.shape, jnp.int32)
        for a in range(4):
            kind = class_of(slot_of[4 * i + a] // 4, e)
            start = a * CH + HS * lax.rem(kind, 4) + OFF * (kind // 4)
            value = jnp.where(index // OFF == a, start, value)
        return value

    for i in range(8):
        limit[i * group : (i + 1) * group] = starts(row, i, pair) + HALF * core + row % HALF

    def update(e, first_set):
        def chunk(i):
            return slice(i * group, (i + 1) * group), 4 * OFF * (i + 1)

        def scores(i):
            here, width = chunk(i)
            return lax.dot_general(
                q[here], kv[e, 0, :width], (((1,), (1,)), ((), ())), preferred_element_type=f32
            )

        def soft(i, s):
            here, width = chunk(i)
            at = starts(col, i, e) + col % OFF
            edge = jnp.where(at <= limit[here], s[:, width - 4 * OFF :], -1e30)
            s = edge if i == 0 else jnp.concatenate([s[:, : width - 4 * OFF], edge], axis=1)
            top = jnp.max(s, axis=1, keepdims=True)
            if not first_set:
                top = jnp.maximum(top, largest[here])
                summed[here] = summed[here] * jnp.exp2((largest[here] - top) * scale)
            largest[here] = top
            return jnp.exp2((s - top) * scale).astype(jnp.bfloat16)

        def gather(i, weights):
            here, width = chunk(i)
            beside = jnp.concatenate(
                [kv[e, 1, :width], jnp.ones((width, HS), jnp.bfloat16)], axis=1
            )
            new = jnp.dot(weights, beside, preferred_element_type=f32)
            summed[here] = new if first_set else summed[here] + new

        s = scores(0)
        held = None
        for i in range(8):
            ahead = scores(i + 1) if i < 7 else None
            weights = soft(i, s)
            if held is not None:
                gather(*held)
            held = (i, weights)
            s = ahead
        gather(*held)

    arrive(pair, 1 - core)
    update(pair, True)
    arrive(x_own, core)
    share(x_own).start()
    arrive(z_down, core)
    pass_half(0).start()
    share(z_down).start()
    arrive(z_up, core)
    pass_half(1).start()
    share(z_up).start()
    wmove(0).start()
    give(t).start()
    order = (x_own, z_up, z_down, z_far, x_up, x_down, x_far)

    def step(n, unused):
        e = order[6]
        for index in range(6):
            e = jnp.where(n == index, order[index], e)

        @pl.when(n == 1)
        def _():
            arrive_half(0)
            arrive_half(1)
            for index in (5, 3, 4):
                transfer(*moves[index], index).start()
            share(z_far).start()

        @pl.when(n == 4)
        def _():
            warrive(0)
            for m in (4, 5, 6):
                wmove(m).start()
            give(a_own).start()
            arrive(x_up, core)
            share(x_up).start()
            arrive(x_down, core)
            share(x_down).start()

        @pl.when(n == 6)
        def _():
            arrive(x_far, core)
            share(x_far).start()

        arrive(e, 1 - core)
        update(e, False)
        return unused

    lax.fori_loop(0, 7, step, 0)

    for i in range(8):
        here = slice(i * group, (i + 1) * group)
        done = (summed[here, :HS] / summed[here, HS : HS + 1]).astype(jnp.bfloat16)
        done = done.reshape(4, 2, HALF, HS)
        for a in range(4):
            attended[0, 4 * i + a] = jnp.concatenate([done[a, 0], done[a, 1]], axis=1)

    def head_push(d, a, n):
        e = lax.rem(pair + d, PAIRS)
        kind = class_of(e, pair)
        at = pl.ds(OFF * (kind // 4) + HALF * core, HALF)
        return push(
            attended.at[1, pl.ds(4 * e + 2 * a, 2)], heads.at[t, :, at, :], hsend.at[d, a, n],
            hrecv.at[t, kind // 4, core], 2 * e + a, lax.rem(4 * n + lax.rem(kind, 4) + side, N_TP),
        )

    def is_here(d, a, n):
        if d or n:
            return jnp.bool_(False)
        return jnp.logical_and(first, core == a)

    for j in range(32):
        attended[1, j] = attended[0, span_order[j]]
    for d in range(PAIRS):
        for n in range(2):
            for a in range(2):
                if d or n:
                    head_push(d, a, n).start()
                else:

                    @pl.when(is_here(d, a, n))
                    def _():
                        pltpu.make_async_copy(
                            attended.at[1, pl.ds(4 * pair + 2 * a, 2)],
                            heads.at[t, :, pl.ds(HALF * core, HALF), :], hrecv.at[t, 0, core],
                        ).start()

                    @pl.when(jnp.logical_not(is_here(d, a, n)))
                    def _():
                        head_push(d, a, n).start()

    for m in range(1, 7):
        warrive(m)
    for g in (t_up, t_down, t_far, a_up, a_down, a_far):
        give(g).start()
    for g in range(N_TP):
        ref = weight.at[1 - core, g]
        push(ref, ref, csend.at[g], crecv.at[g], sibling, t).wait_recv()
    for g in range(N_TP):
        for n in range(2):
            for k in range(2):
                ref = heads.at[g, :, pl.ds(OFF * n + HALF * k, HALF), :]
                push(ref, ref, hsend.at[0, 0, 0], hrecv.at[g, n, k], sibling, t).wait_recv()

    take_rows.wait()

    part = out.shape[-1]
    place = pl.ds(HS * y, HS)

    def send_home(n):
        return push(
            result.at[n], out.at[:, place, :], rsend.at[n], rrecv.at[y], c, side + n
        )

    for n in range(4):
        if n % 2 == 0:
            for begin, end in ((0, 4 * HS), (4 * HS, cols)):
                total = jnp.zeros((2 * HS, end - begin), f32)
                for g in range(N_TP):
                    x = heads[g].reshape(2 * HS, 2 * HS)
                    total = total + jnp.dot(
                        x, weight[n // 2, g, :, begin:end], preferred_element_type=f32
                    ).astype(jnp.bfloat16).astype(f32)
                product[:, begin:end] = total
            total = product[:, : 4 * HS][:, :part]
        else:
            start = part // HS * HS
            total = product[:, start : start + 4 * HS]
            total = pltpu.roll(total, 4 * HS - (part - start), 1)[:, :part]
        placed = rows[n].reshape(2 * HS, part).astype(f32)
        result[n] = (placed + total).astype(jnp.bfloat16).reshape(2, HS, part)

        @pl.when(y == n)
        def _():
            pltpu.make_async_copy(result.at[n], out.at[:, place, :], rrecv.at[y]).start()

        @pl.when(y != n)
        def _():
            send_home(n).start()

    for n in range(4):
        ref = out.at[:, pl.ds(HS * n, HS), :]
        push(ref, ref, rsend.at[0], rrecv.at[n], sibling, t).wait_recv()
    for n in range(2):
        pass_half(n).wait_send()
    for index in range(6):
        transfer(*moves[index], index).wait_send()
    for e in range(PAIRS):
        share(e).wait_send()
    for m in range(7):
        wmove(m).wait_send()
    for g in range(N_TP):
        give(g).wait_send()
    for d in range(PAIRS):
        for n in range(2):
            for a in range(2):
                if d or n:
                    head_push(d, a, n).wait_send()
                else:

                    @pl.when(jnp.logical_not(is_here(d, a, n)))
                    def _():
                        head_push(d, a, n).wait_send()

    for n in range(4):

        @pl.when(y != n)
        def _():
            send_home(n).wait_send()


def attention(slot_of, span_order, query, kv, out_weight, rows):
    vm = pl.BlockSpec(memory_space=pltpu.VMEM)
    sm = pl.BlockSpec(memory_space=pltpu.SMEM)
    anywhere = pl.BlockSpec(memory_space=pl.ANY)
    dma = pltpu.SemaphoreType.DMA
    bf16 = jnp.bfloat16
    keys = 32 * OFF
    depth, width = out_weight.shape
    part = rows.shape[-1]
    return pl.pallas_call(
        attention_kernel,
        out_shape=jax.ShapeDtypeStruct((2, CH, part), bf16),
        in_specs=[sm, sm, anywhere, anywhere, anywhere, anywhere],
        out_specs=vm,
        scratch_shapes=[
            pltpu.VMEM(query.shape, bf16),
            pltpu.VMEM(kv.shape, bf16),
            pltpu.VMEM(rows.shape, bf16),
            pltpu.VMEM((PAIRS, 2, keys, HS), bf16),
            pltpu.VMEM((keys, HS), bf16),
            pltpu.VMEM((keys, 2 * HS), jnp.float32),
            pltpu.VMEM((keys, 1), jnp.float32),
            pltpu.VMEM((keys, 1), jnp.int32),
            pltpu.VMEM((2, 32, HALF, 2 * HS), bf16),
            pltpu.VMEM((N_TP, 2, HS, 2 * HS), bf16),
            pltpu.VMEM((2, N_TP, depth, width // 4), bf16),
            pltpu.VMEM((2 * HS, width // 4), jnp.float32),
            pltpu.VMEM((4, 2, HS, part), bf16),
            dma((3,)),
            dma((6,)),
            dma((PAIRS, 2)),
            dma((PAIRS,)),
            dma((2,)),
            dma((2,)),
            dma((7,)),
            dma((7,)),
            dma((N_TP,)),
            dma((N_TP,)),
            dma,
            dma((PAIRS, 2, 2)),
            dma((N_TP, 2, 2)),
            dma((4,)),
            dma((4,)),
        ],
        compiler_params=pltpu.CompilerParams(
            collective_id=2, has_side_effects=True, vmem_limit_bytes=60 * 2**20
        ),
        name="attention",
    )(slot_of, span_order, query, kv, out_weight, rows)


def per_device(
    text_embed,
    frame_features,
    frame_positions,
    span_order,
    projector,
    norm_gain,
    query_weight,
    key_weight,
    value_weight,
    out_weight,
):
    tok_rows, part = text_embed.shape
    c = lax.axis_index("ctx")
    t = lax.axis_index("tp")
    slots = span_order.shape[0]
    index = jnp.arange(slots, dtype=jnp.int32)
    slot_of = jnp.sum(
        jnp.where(span_order[None, :] == index[:, None], index[None, :], 0), axis=1
    )
    spans = lax.dynamic_slice_in_dim(span_order, 2 * c, 2, 0)
    positions = (
        spans[:, None] * CH + HS * (t % 4) + jnp.arange(HS, dtype=jnp.int32)[None, :]
    ).reshape(-1)
    half = HS // 2
    lane = jnp.arange(HS, dtype=jnp.int32)
    freqs = 1000000.0 ** (-((lane % half).astype(jnp.float32) * 2.0 / HS))
    angles = positions.astype(jnp.float32)[:, None] * freqs[None, :]
    cosine = jnp.cos(angles)
    sine = jnp.where(lane[None, :] < half, -1.0, 1.0) * jnp.sin(angles)
    rows, query, kv = intake(
        text_embed, norm_gain, frame_features, frame_positions, span_order, (cosine, sine),
        projector, query_weight, key_weight, value_weight,
    )
    mixed = attention(
        slot_of, span_order, query.reshape(2, 32, HALF, HS), kv.reshape(32, OFF, HS),
        out_weight, rows,
    )
    return mixed.reshape(tok_rows, part)


def solution(mesh):
    in_specs = (
        P("ctx", "tp"),
        P(("ctx", "tp"), None),
        P(("ctx", "tp")),
        P(),
        P(),
        P("tp"),
        P(None, "tp"),
        P(),
        P(),
        P("tp", None),
    )
    out_specs = P("ctx", "tp")
    return jax.shard_map(
        per_device, mesh=mesh, in_specs=in_specs, out_specs=out_specs, check_vma=False
    )
```

```python
import functools
import math

import jax
import jax.numpy as jnp
from jax import lax
from jax.experimental import pallas as pl
from jax.experimental.pallas import tpu as pltpu
from jax.sharding import PartitionSpec as P

HS = 128
KVH = 4
CAP = 8
CH = 512
N_CTX = 16
N_TP = 8
PAIRS = 8
OFF = 64
HALF = 32
MESH = pl.DeviceIdType.MESH
LOG2E = math.log2(math.e)


def signal(sem, ctx, tp):
    pl.semaphore_signal(sem, inc=1, device_id=(ctx, tp), device_id_type=MESH)


def push(src, dst, send_sem, recv_sem, ctx, tp):
    return pltpu.make_async_remote_copy(
        src_ref=src, dst_ref=dst, send_sem=send_sem, recv_sem=recv_sem,
        device_id=(ctx, tp), device_id_type=MESH,
    )


def add4(a, b):
    return lax.rem(a + b + 4, 4)


def pair_of(e, t):
    x = lax.rem(e // 4 + t // 4, 2)
    return x * 4 + lax.rem(lax.rem(e, 4) + lax.rem(t, 4) + 2 * x, 4)


def class_of(e, pair):
    x = pair // 4
    return lax.rem(e // 4 + x, 2) * 4 + lax.rem(lax.rem(pair, 4) - lax.rem(e, 4) + 2 * x + 4, 4)


def intake_kernel(
    gain, pos_row, order_row, cosine, sine,
    text, frame_features, projector, query_weight, key_weight, value_weight,
    rows_out, query_out, kv_out,
    features, turned_text, pweight, outgoing, incoming, placed, rows, gains, normed, weight, kv_weight, query, kv,
    tsem, psem, own_sem, kv_sem, fr_send, fr_recv, wsend, wrecv, csend, crecv,
    send, recv, gsend, grecv, osem, qsend, qrecv, ksend, krecv,
):
    c = lax.axis_index("ctx")
    t = lax.axis_index("tp")
    pair = c // 2
    core = c % 2
    sibling = c + 1 - 2 * core
    devices = N_CTX * N_TP
    me = c * N_TP + t
    part = text.shape[0]
    width = N_TP * part
    base = pair // 4 * 4
    z = pair % 4
    z_up, z_down, z_far = (base + add4(z, n) for n in (1, 3, 2))
    y = lax.rem(t, 4)
    side = t - y
    half = t // 4
    y_up, y_down, y_far = (add4(y, n) for n in (1, 3, 2))

    own_copy = pltpu.make_async_copy(
        query_weight.at[:, pl.ds(pl.multiple_of(HS * core, HS), HS)], weight.at[core, y], own_sem
    )
    own_copy.start()
    block = 4 * HS
    take_features = pltpu.make_async_copy(frame_features, features, tsem.at[0])
    take_features.start()
    take_text = pltpu.make_async_copy(text, turned_text, tsem.at[1])

    def load(d):
        j = lax.rem(t + d, N_TP)
        start = pl.multiple_of((j * part) // HS * HS, HS)
        return pltpu.make_async_copy(
            projector.at[:, pl.ds(start, block)], pweight.at[d], psem.at[d]
        )

    for d in range(N_TP):
        load(d).start()
    kv_cols = pl.ds(pl.multiple_of(2 * HS * half, HS), 2 * HS)
    kv_loads = [
        pltpu.make_async_copy(ref.at[:, kv_cols], kv_weight.at[n], kv_sem.at[n])
        for n, ref in enumerate((key_weight, value_weight))
    ]
    take_text.start()
    for one in kv_loads:
        one.start()

    barrier = pltpu.get_barrier_semaphore()

    def greet(d, unused):
        other = lax.rem(me + d, devices)
        signal(barrier, other // N_TP, lax.rem(other, N_TP))
        return unused

    lax.fori_loop(1, devices, greet, 0)

    f32 = jnp.float32
    spans = order_row.shape[1]
    tokens = pos_row.shape[1]
    entries = N_CTX * CAP

    def turned(x):
        size = x.shape[1]
        same = lax.broadcasted_iota(jnp.int32, (size, size), 0) == lax.broadcasted_iota(
            jnp.int32, (size, size), 1
        )
        return jnp.sum(jnp.where(same, x, 0.0), axis=1, keepdims=True)

    order_col = turned(order_row[...].astype(f32))
    slot_row = jnp.sum(
        jnp.where(
            order_col == (pos_row[...] // CH).astype(f32),
            lax.broadcasted_iota(jnp.int32, (spans, tokens), 0).astype(f32), 0.0,
        ),
        axis=0, keepdims=True,
    )
    slot_col = turned(slot_row).astype(jnp.int32)
    slot_row = slot_row.astype(jnp.int32)
    first = lax.broadcasted_iota(jnp.int32, (tokens, tokens), 0)
    second = lax.broadcasted_iota(jnp.int32, (tokens, tokens), 1)
    earlier = jnp.logical_and(slot_col // 2 == slot_row // 2, first < second)
    place = jnp.sum(jnp.where(earlier, 1.0, 0.0), axis=0, keepdims=True).astype(jnp.int32)
    entry = slot_row // 2 * CAP + place
    chosen = lax.broadcasted_iota(jnp.int32, (entries, tokens), 0) == entry
    take_features.wait()
    ordered = jnp.dot(
        jnp.where(chosen, 1.0, 0.0).astype(jnp.bfloat16), features[...],
        preferred_element_type=f32,
    ).astype(jnp.bfloat16)
    token_row = (slot_row % 2 * CH + pos_row[...] % CH + 1).astype(f32)
    row_at = jnp.sum(jnp.where(chosen, token_row, 0.0), axis=1, keepdims=True) - 1.0
    row_at = row_at.astype(jnp.int32)
    high = (row_at >> 5).astype(f32)
    low = (row_at & 31).astype(f32)
    lane = lax.broadcasted_iota(jnp.int32, (entries, block), 1)
    tail = jnp.where(lane < part + 32, high, jnp.where(lane < part + 48, low, 1.0))

    pl.semaphore_wait(barrier, devices - 1)

    depth = weight.shape[2]

    def quarter(n):
        return pl.ds(depth // 4 * n, depth // 4)

    def half_quarter(n, second):
        return pl.ds(depth // 4 * n + depth // 8 * second, depth // 8)

    z_next = (add4(z, 1), add4(z, 3))
    y_others = (y_up, y_down, y_far)

    def wmove(m):
        if m < 3:
            ref, ctx, tp = weight.at[core, y, quarter(z)], c, side + y_others[m]
        else:
            n, up = (m - 3) % 6 // 2, (m - 3) % 2
            cut = quarter(z) if m < 9 else half_quarter(z_next[1 - up], up)
            ref, tp = weight.at[core, y_others[n], cut], t
            ctx = 2 * (z_up, z_down)[up] + core
        return push(ref, ref, wsend.at[m], wrecv.at[m], ctx, tp)

    def warrive(m):
        if m < 3:
            ref = weight.at[core, (y_down, y_up, y_far)[m], quarter(z)]
        else:
            n, up = (m - 3) % 6 // 2, (m - 3) % 2
            cut = quarter(z_next[1 - up]) if m < 9 else half_quarter(add4(z, 2), up)
            ref = weight.at[core, y_others[n], cut]
        push(ref, ref, wsend.at[m], wrecv.at[m], sibling, t).wait_recv()

    def share(n):
        ref = weight.at[core, add4(y, n)]
        return push(ref, ref, csend.at[n], crecv.at[n], sibling, t)

    def shared(n):
        ref = weight.at[1 - core, add4(y, n)]
        push(ref, ref, csend.at[n], crecv.at[n], sibling, t).wait_recv()

    own_copy.wait()
    for m in (2, 0, 1):
        wmove(m).start()
    share(0).start()

    for d in range(N_TP):
        j = lax.rem(t + d, N_TP)
        load(d).wait()
        x = jnp.dot(ordered, pweight[d], preferred_element_type=f32)
        x = 0.5 * x * (1.0 + lax.erf(x * math.sqrt(0.5)))
        shift = j * part - (j * part) // HS * HS
        x = jnp.where(shift > 0, pltpu.roll(x, block - HS // 2, 1), x)
        x = jnp.where(lane < part, x, tail)
        halves = [
            x[:, n * 2 * HS : (n + 1) * 2 * HS].reshape(N_CTX, CAP, 2 * HS) for n in range(2)
        ]
        outgoing[d] = jnp.concatenate(halves, axis=1).astype(jnp.bfloat16)

        def deliver(n, unused):
            oc = lax.rem(c + n, N_CTX)
            push(outgoing.at[d, oc], incoming.at[me], fr_send, fr_recv, oc, j).start()
            return unused

        if d == 0:
            pltpu.make_async_copy(outgoing.at[0, c], incoming.at[me], fr_recv).start()
        else:
            push(outgoing.at[d, c], incoming.at[me], fr_send, fr_recv, c, j).start()
        lax.fori_loop(1, N_CTX, deliver, 0)
        if d == 4:
            for m in range(3):
                warrive(m)
            for m in range(3, 9):
                wmove(m).start()

    take_text.wait()
    for a in range(2):
        for n in range(4):
            block_cols = slice((4 * a + n) * HS, (4 * a + n + 1) * HS)
            placed[a, n] = jnp.transpose(turned_text[:, block_cols].astype(f32)).astype(
                jnp.bfloat16
            )
    pltpu.make_async_copy(incoming, incoming, fr_recv).wait()

    def row_block(n, across):
        j = add4(y, n)
        tp = j + (4 - side if across else side)
        return push(
            placed.at[:, j], rows.at[t], send.at[n, across], recv.at[t], c, tp
        )

    def gain_block(d):
        return push(gain, gains.at[t], gsend.at[d], grecv.at[t], c, lax.rem(t + d, N_TP))

    pltpu.make_async_copy(gain, gains.at[t], grecv.at[t]).start()
    for d in range(1, N_TP):
        gain_block(d).start()
    arrived = incoming[...].astype(f32)
    slots = devices * CAP
    left = arrived[:, :CAP].reshape(slots, 2 * HS)
    right = arrived[:, CAP:].reshape(slots, 2 * HS)
    edge = part - 2 * HS
    at = right[:, edge : edge + 1] * 32.0 + right[:, edge + 32 : edge + 33]
    at = jnp.transpose(jnp.broadcast_to(at, (slots, HS)))[0:1, :]
    left = left.astype(jnp.bfloat16)
    right = right.astype(jnp.bfloat16)
    group = 2 * HS
    offset = lax.broadcasted_iota(jnp.int32, (group, 1), 0)
    offset = offset // HS * CH + offset % HS
    for n in range(4):
        j = add4(y, n)
        row = offset + j * HS
        hit = jnp.where(row.astype(f32) == at, 1.0, 0.0).astype(jnp.bfloat16)
        new_left = jnp.dot(hit, left, preferred_element_type=f32)
        new_right = jnp.dot(hit, right, preferred_element_type=f32)
        framed = new_right[:, 2 * HS - 1 :] > 0.5
        old = placed[:, j].reshape(group, part).astype(f32)
        placed[:, j, :, : 2 * HS] = (
            jnp.where(framed, new_left, old[:, : 2 * HS]).astype(jnp.bfloat16)
        ).reshape(2, HS, 2 * HS)
        placed[:, j, :, 2 * HS :] = (
            jnp.where(framed, new_right[:, :edge], old[:, 2 * HS :]).astype(jnp.bfloat16)
        ).reshape(2, HS, edge)
        row_block(n, 1).start()
        if n == 0:
            pltpu.make_async_copy(placed.at[:, y], rows.at[t], recv.at[t]).start()
        else:
            row_block(n, 0).start()

    for one in kv_loads:
        one.wait()

    for m in range(3, 9):
        warrive(m)
    for m in range(9, 15):
        wmove(m).start()
    total = jnp.zeros((group, 1), f32)
    for d in range(N_TP):
        j = lax.rem(t + d, N_TP)
        push(gain, gains.at[j], gsend.at[0], grecv.at[j], sibling, t).wait_recv()
        push(rows.at[j], rows.at[j], send.at[0, 0], recv.at[j], sibling, t).wait_recv()
        x = rows[j].reshape(group, part).astype(f32)
        total = total + jnp.sum(x * x, axis=1, keepdims=True)

    keep = pltpu.make_async_copy(rows.at[pl.ds(side, 4)], rows_out, osem)
    keep.start()

    for m in range(9, 15):
        warrive(m)
    for n in range(1, 4):
        share(n).start()
    inverse = lax.rsqrt(total / width + 1e-06)
    for j in range(N_TP):
        x = rows[j].reshape(group, part).astype(f32)
        normed[j] = (x * inverse * gains[j, 0:1, :].astype(f32)).astype(jnp.bfloat16)

    def product(piece):
        total = None
        for j in range(N_TP):
            term = jnp.dot(
                normed[j], piece(slice(j * part, (j + 1) * part)), preferred_element_type=f32
            )
            total = term if total is None else total + term
        return total

    def rotated(x, cos, sin):
        return (x * cos + pltpu.roll(x, HS // 2, 1) * sin).astype(jnp.bfloat16).reshape(2, HS, HS)

    goal = [pair_of(pair, 4 * n + y) for n in range(2)]
    mine = pl.ds(2 * core, 2)

    def kv_push(n, which, m):
        return push(
            kv.at[which, m // 2, :, pl.ds(OFF * n, OFF), :], kv_out.at[pair, mine],
            ksend.at[n, which, m], krecv.at[pair, core], 2 * goal[n] + which, side + m,
        )

    def q_push(n, k, m):
        return push(
            query.at[m, :, :, pl.ds(OFF * n + HALF * k, HALF), :], query_out.at[:, pair, mine],
            qsend.at[n, k, m], qrecv.at[pair, core], 2 * goal[n] + k, side + m,
        )

    def is_here(n, k, m):
        return jnp.logical_and(goal[n] == pair, jnp.logical_and(core == k, y == m))

    cos = cosine[...]
    sin = sine[...]
    for which in range(2):
        out = product(lambda cut: kv_weight[which, cut, :])
        for h in range(2):
            x = out[:, h * HS : (h + 1) * HS]
            kv[which, h] = rotated(x, cos, sin) if which == 0 else x.astype(
                jnp.bfloat16
            ).reshape(2, HS, HS)
        for m in range(4):
            for n in range(2):

                @pl.when(is_here(n, which, m))
                def _():
                    pltpu.make_async_copy(
                        kv.at[which, m // 2, :, pl.ds(OFF * n, OFF), :], kv_out.at[pair, mine],
                        krecv.at[pair, core],
                    ).start()

                @pl.when(jnp.logical_not(is_here(n, which, m)))
                def _():
                    kv_push(n, which, m).start()

    for m0 in range(4):
        m = add4(y, m0)
        shared(m0)
        out = product(
            lambda cut: jnp.concatenate([weight[0, m, cut], weight[1, m, cut]], axis=1)
        )
        for h in range(2):
            query[m, h] = rotated(out[:, h * HS : (h + 1) * HS], cos, sin)
        for n in range(2):
            for k in range(2):
                if m0 == 0:
                    here = jnp.logical_and(goal[n] == pair, core == k)

                    @pl.when(here)
                    def _():
                        pltpu.make_async_copy(
                            query.at[m, :, :, pl.ds(OFF * n + HALF * k, HALF), :],
                            query_out.at[:, pair, mine], qrecv.at[pair, core],
                        ).start()

                    @pl.when(jnp.logical_not(here))
                    def _():
                        q_push(n, k, m).start()

                else:
                    q_push(n, k, m).start()

    for e in range(PAIRS):
        for a in range(2):
            two = pl.ds(2 * a, 2)
            ref = kv_out.at[e, two]
            push(ref, ref, ksend.at[0, 0, 0], krecv.at[e, a], sibling, t).wait_recv()
            ref = query_out.at[:, e, two]
            push(ref, ref, qsend.at[0, 0, 0], qrecv.at[e, a], sibling, t).wait_recv()
    keep.wait()
    pltpu.make_async_copy(
        incoming.at[pl.ds(0, devices - 1)], incoming.at[pl.ds(0, devices - 1)], fr_send
    ).wait()
    for m in range(15):
        wmove(m).wait_send()
    for n in range(4):
        share(n).wait_send()
        row_block(n, 1).wait_send()
        if n:
            row_block(n, 0).wait_send()
    for d in range(1, N_TP):
        gain_block(d).wait_send()
    for n in range(2):
        for k in range(2):
            for m in range(4):

                @pl.when(jnp.logical_not(is_here(n, k, m)))
                def _():
                    kv_push(n, k, m).wait_send()
                    q_push(n, k, m).wait_send()


def intake(
    text_embed, norm_gain, frame_features, frame_positions, span_order, tables,
    projector, query_weight, key_weight, value_weight,
):
    tok_rows, part = text_embed.shape
    depth = query_weight.shape[0]
    devices = N_CTX * N_TP
    vm = pl.BlockSpec(memory_space=pltpu.VMEM)
    anywhere = pl.BlockSpec(memory_space=pl.ANY)
    dma = pltpu.SemaphoreType.DMA
    bf16 = jnp.bfloat16
    return pl.pallas_call(
        intake_kernel,
        out_shape=(
            jax.ShapeDtypeStruct((4, 2, HS, part), bf16),
            jax.ShapeDtypeStruct((2, PAIRS, 4, HALF, HS), bf16),
            jax.ShapeDtypeStruct((PAIRS, 4, OFF, HS), bf16),
        ),
        in_specs=[vm] * 5 + [anywhere] * 6,
        out_specs=(vm, vm, vm),
        scratch_shapes=[
            pltpu.VMEM(frame_features.shape, bf16),
            pltpu.VMEM((part, tok_rows), bf16),
            pltpu.VMEM((N_TP, projector.shape[0], 4 * HS), bf16),
            pltpu.VMEM((N_TP, N_CTX, 2 * CAP, 2 * HS), bf16),
            pltpu.VMEM((devices, 2 * CAP, 2 * HS), bf16),
            pltpu.VMEM((2, 4, HS, part), bf16),
            pltpu.VMEM((N_TP, 2, HS, part), bf16),
            pltpu.VMEM((N_TP, 16, part), bf16),
            pltpu.VMEM((N_TP, 2 * HS, part), bf16),
            pltpu.VMEM((2, 4, depth, HS), bf16),
            pltpu.VMEM((2, depth, 2 * HS), bf16),
            pltpu.VMEM((4, 2, 2, HS, HS), bf16),
            pltpu.VMEM((2, 2, 2, HS, HS), bf16),
            dma((2,)),
            dma((N_TP,)),
            dma,
            dma((2,)),
            dma,
            dma,
            dma((15,)),
            dma((15,)),
            dma((4,)),
            dma((4,)),
            dma((4, 2)),
            dma((N_TP,)),
            dma((N_TP,)),
            dma((N_TP,)),
            dma,
            dma((2, 2, 4)),
            dma((PAIRS, 2)),
            dma((2, 2, 4)),
            dma((PAIRS, 2)),
        ],
        compiler_params=pltpu.CompilerParams(
            collective_id=1, has_side_effects=True, vmem_limit_bytes=56 * 2**20
        ),
        name="intake",
    )(
        jnp.broadcast_to(norm_gain[None, :], (16, part)),
        frame_positions.reshape(1, -1),
        span_order.reshape(1, -1),
        *tables,
        text_embed.T,
        frame_features,
        projector,
        query_weight,
        key_weight,
        value_weight,
    )


def attention_kernel(
    slot_of, span_order, query_in, kv_in, out_weight, rows_in, out,
    query, kv_own, rows, kv, q, summed, largest, limit, attended, heads, weight, product, result,
    isem, send, recv, pass_send, half_send, half_recv, wsend, wrecv, csend, crecv, own_sem,
    hsend, hrecv, rsend, rrecv,
):
    f32 = jnp.float32
    scale = LOG2E / math.sqrt(HS)
    c = lax.axis_index("ctx")
    t = lax.axis_index("tp")
    pair = c // 2
    core = c % 2
    sibling = c + 1 - 2 * core
    base = pair // 4 * 4
    other = 4 - base
    z = pair % 4
    up, down, far = (add4(z, n) for n in (1, 3, 2))
    z_up, z_down, z_far = base + up, base + down, base + far
    keys = kv.shape[2]
    x_own, x_up, x_down, x_far = other + z, other + up, other + down, other + far
    y = lax.rem(t, 4)
    side = t - y
    half = t // 4
    across = 4 - side
    t_up, t_down, t_far = (side + add4(y, n) for n in (1, 3, 2))
    a_own, a_up, a_down, a_far = (across + add4(y, n) for n in (0, 1, 3, 2))
    x_next = 2 * x_own + core
    depth, cols = weight.shape[2:]

    def columns(of_half):
        return out_weight.at[:, pl.ds(pl.multiple_of(cols * (2 * of_half + core), HS), cols)]

    take_kv, take_query, take_rows = (
        pltpu.make_async_copy(src, dst, isem.at[n])
        for n, (src, dst) in enumerate(((kv_in, kv_own), (query_in, query), (rows_in, rows)))
    )
    take_kv.start()
    take_query.start()
    own_copy = pltpu.make_async_copy(columns(half), weight.at[core, t], own_sem)
    own_copy.start()
    take_rows.start()
    barrier = pltpu.get_barrier_semaphore()
    signal(barrier, sibling, t)
    for e in (z_up, z_down, z_far, x_own):
        signal(barrier, 2 * e + core, t)
    signal(barrier, x_next, a_own)
    for j in (t_up, t_down, t_far):
        signal(barrier, c, j)
    first = y == 2 * (pair // 4)
    for n in range(2):
        origin = pair_of(pair, 4 * n + y)
        for k in range(2):
            for d in range(N_TP):
                j = lax.rem(t + d, N_TP)
                if n == 0 and d == 0:

                    @pl.when(jnp.logical_not(jnp.logical_and(first, core == k)))
                    def _():
                        signal(barrier, 2 * origin + k, j)

                else:
                    signal(barrier, 2 * origin + k, j)
    take_kv.wait()
    for j in range(32):
        kv[pair, core, j * OFF : (j + 1) * OFF] = kv_own[slot_of[j]]
    pl.semaphore_wait(barrier, 9 + 32 - jnp.where(first, 1, 0))

    def wmove(m):
        own = weight.at[core, t]
        passed = weight.at[core, a_own]
        if m == 0:
            src, dst, ctx, tp = columns(1 - half), own, x_next, a_own
        else:
            src = dst = own if m < 4 else passed
            ctx, tp = c, (t_up, t_down, t_far)[(m - 1) % 3]
        return push(src, dst, wsend.at[m], wrecv.at[m], ctx, tp)

    def warrive(m):
        ref = weight.at[core, (a_own, t_down, t_up, t_far, a_down, a_up, a_far)[m]]
        push(ref, ref, wsend.at[m], wrecv.at[m], sibling, t).wait_recv()

    def give(g):
        ref = weight.at[core, g]
        return push(ref, ref, csend.at[g], crecv.at[g], sibling, t)

    def transfer(e, to, index):
        block = kv.at[e, core]
        return push(block, block, send.at[index], recv.at[e, core], 2 * to + core, t)

    def share(e):
        block = kv.at[e, core]
        return push(block, block, pass_send.at[e], recv.at[e, core], sibling, t)

    def arrive(e, which):
        block = kv.at[e, which]
        push(block, block, send.at[0], recv.at[e, which], sibling, t).wait_recv()

    share(pair).start()
    moves = (
        (pair, x_own), (pair, z_up), (pair, z_down), (x_own, z_up), (x_own, z_down), (z_far, x_own),
    )

    def pass_half(n):
        e, to = ((z_down, z_up), (z_up, z_down))[n]
        block = kv.at[e, core, pl.ds(keys // 2 * n, keys // 2)]
        return push(block, block, half_send.at[n], half_recv.at[n], 2 * to + core, t)

    def arrive_half(n):
        block = kv.at[z_far, core, pl.ds(keys // 2 * n, keys // 2)]
        push(block, block, half_send.at[n], half_recv.at[n], sibling, t).wait_recv()

    for index in range(3):
        transfer(*moves[index], index).start()
    own_copy.wait()
    for m in (1, 2, 3):
        wmove(m).start()
    take_query.wait()
    for j in range(32):
        q[j * OFF : (j + 1) * OFF] = query[:, slot_of[j]].reshape(2 * HALF, HS)

    group = 8 * HALF
    row = lax.broadcasted_iota(jnp.int32, (group, 1), 0)
    col = lax.broadcasted_iota(jnp.int32, (1, 4 * OFF), 1)

    def starts(index, i, e):
        value = jnp.zeros(index.shape, jnp.int32)
        for a in range(4):
            kind = class_of(slot_of[4 * i + a] // 4, e)
            start = a * CH + HS * lax.rem(kind, 4) + OFF * (kind // 4)
            value = jnp.where(index // OFF == a, start, value)
        return value

    for i in range(8):
        limit[i * group : (i + 1) * group] = starts(row, i, pair) + HALF * core + row % HALF

    def update(e, first_set):
        def chunk(i):
            return slice(i * group, (i + 1) * group), 4 * OFF * (i + 1)

        def scores(i):
            here, width = chunk(i)
            return lax.dot_general(
                q[here], kv[e, 0, :width], (((1,), (1,)), ((), ())), preferred_element_type=f32
            )

        def soft(i, s):
            here, width = chunk(i)
            at = starts(col, i, e) + col % OFF
            edge = jnp.where(at <= limit[here], s[:, width - 4 * OFF :], -1e30)
            s = edge if i == 0 else jnp.concatenate([s[:, : width - 4 * OFF], edge], axis=1)
            top = jnp.max(s, axis=1, keepdims=True)
            if not first_set:
                top = jnp.maximum(top, largest[here])
                summed[here] = summed[here] * jnp.exp2((largest[here] - top) * scale)
            largest[here] = top
            return jnp.exp2((s - top) * scale).astype(jnp.bfloat16)

        def gather(i, weights):
            here, width = chunk(i)
            beside = jnp.concatenate(
                [kv[e, 1, :width], jnp.ones((width, HS), jnp.bfloat16)], axis=1
            )
            new = jnp.dot(weights, beside, preferred_element_type=f32)
            summed[here] = new if first_set else summed[here] + new

        s = scores(7)
        held = None
        for i in range(7, -1, -1):
            ahead = scores(i - 1) if i else None
            weights = soft(i, s)
            if held is not None:
                gather(*held)
            held = (i, weights)
            s = ahead
        gather(*held)

    arrive(pair, 1 - core)
    update(pair, True)
    arrive(x_own, core)
    share(x_own).start()
    arrive(z_down, core)
    pass_half(0).start()
    share(z_down).start()
    arrive(z_up, core)
    pass_half(1).start()
    share(z_up).start()
    wmove(0).start()
    give(t).start()
    order = (x_own, z_up, z_down, z_far, x_up, x_down, x_far)

    def step(n, unused):
        e = order[6]
        for index in range(6):
            e = jnp.where(n == index, order[index], e)

        @pl.when(n == 1)
        def _():
            arrive_half(0)
            arrive_half(1)
            for index in (5, 3, 4):
                transfer(*moves[index], index).start()
            share(z_far).start()

        @pl.when(n == 4)
        def _():
            warrive(0)
            for m in (4, 5, 6):
                wmove(m).start()
            give(a_own).start()
            arrive(x_up, core)
            share(x_up).start()
            arrive(x_down, core)
            share(x_down).start()

        @pl.when(n == 6)
        def _():
            arrive(x_far, core)
            share(x_far).start()

        arrive(e, 1 - core)
        update(e, False)
        return unused

    lax.fori_loop(0, 7, step, 0)

    for i in range(8):
        here = slice(i * group, (i + 1) * group)
        done = (summed[here, :HS] / summed[here, HS : HS + 1]).astype(jnp.bfloat16)
        done = done.reshape(4, 2, HALF, HS)
        for a in range(4):
            attended[0, 4 * i + a] = jnp.concatenate([done[a, 0], done[a, 1]], axis=1)

    def head_push(d, a, n):
        e = lax.rem(pair + d, PAIRS)
        kind = class_of(e, pair)
        at = pl.ds(OFF * (kind // 4) + HALF * core, HALF)
        return push(
            attended.at[1, pl.ds(4 * e + 2 * a, 2)], heads.at[t, :, at, :], hsend.at[d, a, n],
            hrecv.at[t, kind // 4, core], 2 * e + a, lax.rem(4 * n + lax.rem(kind, 4) + side, N_TP),
        )

    def is_here(d, a, n):
        if d or n:
            return jnp.bool_(False)
        return jnp.logical_and(first, core == a)

    for j in range(32):
        attended[1, j] = attended[0, span_order[j]]
    for d in range(PAIRS):
        for n in range(2):
            for a in range(2):
                if d or n:
                    head_push(d, a, n).start()
                else:

                    @pl.when(is_here(d, a, n))
                    def _():
                        pltpu.make_async_copy(
                            attended.at[1, pl.ds(4 * pair + 2 * a, 2)],
                            heads.at[t, :, pl.ds(HALF * core, HALF), :], hrecv.at[t, 0, core],
                        ).start()

                    @pl.when(jnp.logical_not(is_here(d, a, n)))
                    def _():
                        head_push(d, a, n).start()

    for m in range(1, 7):
        warrive(m)
    for g in (t_up, t_down, t_far, a_up, a_down, a_far):
        give(g).start()
    for g in range(N_TP):
        ref = weight.at[1 - core, g]
        push(ref, ref, csend.at[g], crecv.at[g], sibling, t).wait_recv()
    for g in range(N_TP):
        for n in range(2):
            for k in range(2):
                ref = heads.at[g, :, pl.ds(OFF * n + HALF * k, HALF), :]
                push(ref, ref, hsend.at[0, 0, 0], hrecv.at[g, n, k], sibling, t).wait_recv()

    take_rows.wait()

    part = out.shape[-1]
    place = pl.ds(HS * y, HS)

    def send_home(n):
        return push(
            result.at[n], out.at[:, place, :], rsend.at[n], rrecv.at[y], c, side + n
        )

    for n in range(4):
        if n % 2 == 0:
            for begin, end in ((0, 4 * HS), (4 * HS, cols)):
                total = jnp.zeros((2 * HS, end - begin), f32)
                for g in range(N_TP):
                    x = heads[g].reshape(2 * HS, 2 * HS)
                    total = total + jnp.dot(
                        x, weight[n // 2, g, :, begin:end], preferred_element_type=f32
                    ).astype(jnp.bfloat16).astype(f32)
                product[:, begin:end] = total
            total = product[:, : 4 * HS][:, :part]
        else:
            start = part // HS * HS
            total = product[:, start : start + 4 * HS]
            total = pltpu.roll(total, 4 * HS - (part - start), 1)[:, :part]
        placed = rows[n].reshape(2 * HS, part).astype(f32)
        result[n] = (placed + total).astype(jnp.bfloat16).reshape(2, HS, part)

        @pl.when(y == n)
        def _():
            pltpu.make_async_copy(result.at[n], out.at[:, place, :], rrecv.at[y]).start()

        @pl.when(y != n)
        def _():
            send_home(n).start()

    for n in range(4):
        ref = out.at[:, pl.ds(HS * n, HS), :]
        push(ref, ref, rsend.at[0], rrecv.at[n], sibling, t).wait_recv()
    for n in range(2):
        pass_half(n).wait_send()
    for index in range(6):
        transfer(*moves[index], index).wait_send()
    for e in range(PAIRS):
        share(e).wait_send()
    for m in range(7):
        wmove(m).wait_send()
    for g in range(N_TP):
        give(g).wait_send()
    for d in range(PAIRS):
        for n in range(2):
            for a in range(2):
                if d or n:
                    head_push(d, a, n).wait_send()
                else:

                    @pl.when(jnp.logical_not(is_here(d, a, n)))
                    def _():
                        head_push(d, a, n).wait_send()

    for n in range(4):

        @pl.when(y != n)
        def _():
            send_home(n).wait_send()


def attention(slot_of, span_order, query, kv, out_weight, rows):
    vm = pl.BlockSpec(memory_space=pltpu.VMEM)
    sm = pl.BlockSpec(memory_space=pltpu.SMEM)
    anywhere = pl.BlockSpec(memory_space=pl.ANY)
    dma = pltpu.SemaphoreType.DMA
    bf16 = jnp.bfloat16
    keys = 32 * OFF
    depth, width = out_weight.shape
    part = rows.shape[-1]
    return pl.pallas_call(
        attention_kernel,
        out_shape=jax.ShapeDtypeStruct((2, CH, part), bf16),
        in_specs=[sm, sm, anywhere, anywhere, anywhere, anywhere],
        out_specs=vm,
        scratch_shapes=[
            pltpu.VMEM(query.shape, bf16),
            pltpu.VMEM(kv.shape, bf16),
            pltpu.VMEM(rows.shape, bf16),
            pltpu.VMEM((PAIRS, 2, keys, HS), bf16),
            pltpu.VMEM((keys, HS), bf16),
            pltpu.VMEM((keys, 2 * HS), jnp.float32),
            pltpu.VMEM((keys, 1), jnp.float32),
            pltpu.VMEM((keys, 1), jnp.int32),
            pltpu.VMEM((2, 32, HALF, 2 * HS), bf16),
            pltpu.VMEM((N_TP, 2, HS, 2 * HS), bf16),
            pltpu.VMEM((2, N_TP, depth, width // 4), bf16),
            pltpu.VMEM((2 * HS, width // 4), jnp.float32),
            pltpu.VMEM((4, 2, HS, part), bf16),
            dma((3,)),
            dma((6,)),
            dma((PAIRS, 2)),
            dma((PAIRS,)),
            dma((2,)),
            dma((2,)),
            dma((7,)),
            dma((7,)),
            dma((N_TP,)),
            dma((N_TP,)),
            dma,
            dma((PAIRS, 2, 2)),
            dma((N_TP, 2, 2)),
            dma((4,)),
            dma((4,)),
        ],
        compiler_params=pltpu.CompilerParams(
            collective_id=2, has_side_effects=True, vmem_limit_bytes=60 * 2**20
        ),
        name="attention",
    )(slot_of, span_order, query, kv, out_weight, rows)


def per_device(
    text_embed,
    frame_features,
    frame_positions,
    span_order,
    projector,
    norm_gain,
    query_weight,
    key_weight,
    value_weight,
    out_weight,
):
    tok_rows, part = text_embed.shape
    c = lax.axis_index("ctx")
    t = lax.axis_index("tp")
    slots = span_order.shape[0]
    index = jnp.arange(slots, dtype=jnp.int32)
    slot_of = jnp.sum(
        jnp.where(span_order[None, :] == index[:, None], index[None, :], 0), axis=1
    )
    spans = lax.dynamic_slice_in_dim(span_order, 2 * c, 2, 0)
    positions = (
        spans[:, None] * CH + HS * (t % 4) + jnp.arange(HS, dtype=jnp.int32)[None, :]
    ).reshape(-1)
    half = HS // 2
    lane = jnp.arange(HS, dtype=jnp.int32)
    freqs = 1000000.0 ** (-((lane % half).astype(jnp.float32) * 2.0 / HS))
    angles = positions.astype(jnp.float32)[:, None] * freqs[None, :]
    cosine = jnp.cos(angles)
    sine = jnp.where(lane[None, :] < half, -1.0, 1.0) * jnp.sin(angles)
    rows, query, kv = intake(
        text_embed, norm_gain, frame_features, frame_positions, span_order, (cosine, sine),
        projector, query_weight, key_weight, value_weight,
    )
    mixed = attention(
        slot_of, span_order, query.reshape(2, 32, HALF, HS), kv.reshape(32, OFF, HS),
        out_weight, rows,
    )
    return mixed.reshape(tok_rows, part)


def solution(mesh):
    in_specs = (
        P("ctx", "tp"),
        P(("ctx", "tp"), None),
        P(("ctx", "tp")),
        P(),
        P(),
        P("tp"),
        P(None, "tp"),
        P(),
        P(),
        P("tp", None),
    )
    out_specs = P("ctx", "tp")
    return jax.shard_map(
        per_device, mesh=mesh, in_specs=in_specs, out_specs=out_specs, check_vma=False
    )
```

```python
import functools
import math

import jax
import jax.numpy as jnp
from jax import lax
from jax.experimental import pallas as pl
from jax.experimental.pallas import tpu as pltpu
from jax.sharding import PartitionSpec as P

HS = 128
KVH = 4
CAP = 8
CH = 512
N_CTX = 16
N_TP = 8
PAIRS = 8
OFF = 64
HALF = 32
MESH = pl.DeviceIdType.MESH
LOG2E = math.log2(math.e)


def signal(sem, ctx, tp):
    pl.semaphore_signal(sem, inc=1, device_id=(ctx, tp), device_id_type=MESH)


def push(src, dst, send_sem, recv_sem, ctx, tp):
    return pltpu.make_async_remote_copy(
        src_ref=src, dst_ref=dst, send_sem=send_sem, recv_sem=recv_sem,
        device_id=(ctx, tp), device_id_type=MESH,
    )


def add4(a, b):
    return lax.rem(a + b + 4, 4)


def pair_of(e, t):
    x = lax.rem(e // 4 + t // 4, 2)
    return x * 4 + lax.rem(lax.rem(e, 4) + lax.rem(t, 4) + 2 * x, 4)


def class_of(e, pair):
    x = pair // 4
    return lax.rem(e // 4 + x, 2) * 4 + lax.rem(lax.rem(pair, 4) - lax.rem(e, 4) + 2 * x + 4, 4)


def intake_kernel(
    gain, pos_row, order_row, cosine, sine,
    text, frame_features, projector, query_weight, key_weight, value_weight,
    rows_out, query_out, kv_out,
    features, turned_text, pweight, outgoing, incoming, placed, rows, gains, normed, weight, kv_weight, query, kv,
    tsem, psem, own_sem, kv_sem, fr_send, fr_recv, wsend, wrecv, csend, crecv,
    send, recv, gsend, grecv, osem, qsend, qrecv, ksend, krecv,
):
    c = lax.axis_index("ctx")
    t = lax.axis_index("tp")
    pair = c // 2
    core = c % 2
    sibling = c + 1 - 2 * core
    devices = N_CTX * N_TP
    me = c * N_TP + t
    part = text.shape[0]
    width = N_TP * part
    base = pair // 4 * 4
    z = pair % 4
    z_up, z_down, z_far = (base + add4(z, n) for n in (1, 3, 2))
    y = lax.rem(t, 4)
    side = t - y
    half = t // 4
    y_up, y_down, y_far = (add4(y, n) for n in (1, 3, 2))

    own_copy = pltpu.make_async_copy(
        query_weight.at[:, pl.ds(pl.multiple_of(HS * core, HS), HS)], weight.at[core, y], own_sem
    )
    own_copy.start()
    block = 4 * HS
    take_features = pltpu.make_async_copy(frame_features, features, tsem.at[0])
    take_features.start()
    take_text = pltpu.make_async_copy(text, turned_text, tsem.at[1])

    def load(d):
        j = lax.rem(t + d, N_TP)
        start = pl.multiple_of((j * part) // HS * HS, HS)
        return pltpu.make_async_copy(
            projector.at[:, pl.ds(start, block)], pweight.at[d], psem.at[d]
        )

    for d in range(N_TP):
        load(d).start()
    kv_cols = pl.ds(pl.multiple_of(2 * HS * half, HS), 2 * HS)
    kv_loads = [
        pltpu.make_async_copy(ref.at[:, kv_cols], kv_weight.at[n], kv_sem.at[n])
        for n, ref in enumerate((key_weight, value_weight))
    ]
    take_text.start()
    for one in kv_loads:
        one.start()

    barrier = pltpu.get_barrier_semaphore()

    def greet(d, unused):
        other = lax.rem(me + d, devices)
        signal(barrier, other // N_TP, lax.rem(other, N_TP))
        return unused

    lax.fori_loop(1, devices, greet, 0)

    f32 = jnp.float32
    spans = order_row.shape[1]
    tokens = pos_row.shape[1]
    entries = N_CTX * CAP

    def turned(x):
        size = x.shape[1]
        same = lax.broadcasted_iota(jnp.int32, (size, size), 0) == lax.broadcasted_iota(
            jnp.int32, (size, size), 1
        )
        return jnp.sum(jnp.where(same, x, 0.0), axis=1, keepdims=True)

    order_col = turned(order_row[...].astype(f32))
    slot_row = jnp.sum(
        jnp.where(
            order_col == (pos_row[...] // CH).astype(f32),
            lax.broadcasted_iota(jnp.int32, (spans, tokens), 0).astype(f32), 0.0,
        ),
        axis=0, keepdims=True,
    )
    slot_col = turned(slot_row).astype(jnp.int32)
    slot_row = slot_row.astype(jnp.int32)
    first = lax.broadcasted_iota(jnp.int32, (tokens, tokens), 0)
    second = lax.broadcasted_iota(jnp.int32, (tokens, tokens), 1)
    earlier = jnp.logical_and(slot_col // 2 == slot_row // 2, first < second)
    place = jnp.sum(jnp.where(earlier, 1.0, 0.0), axis=0, keepdims=True).astype(jnp.int32)
    entry = slot_row // 2 * CAP + place
    chosen = lax.broadcasted_iota(jnp.int32, (entries, tokens), 0) == entry
    take_features.wait()
    ordered = jnp.dot(
        jnp.where(chosen, 1.0, 0.0).astype(jnp.bfloat16), features[...],
        preferred_element_type=f32,
    ).astype(jnp.bfloat16)
    token_row = (slot_row % 2 * CH + pos_row[...] % CH + 1).astype(f32)
    row_at = jnp.sum(jnp.where(chosen, token_row, 0.0), axis=1, keepdims=True) - 1.0
    row_at = row_at.astype(jnp.int32)
    high = (row_at >> 5).astype(f32)
    low = (row_at & 31).astype(f32)
    lane = lax.broadcasted_iota(jnp.int32, (entries, block), 1)
    tail = jnp.where(lane < part + 32, high, jnp.where(lane < part + 48, low, 1.0))

    pl.semaphore_wait(barrier, devices - 1)

    depth = weight.shape[2]

    def quarter(n):
        return pl.ds(depth // 4 * n, depth // 4)

    def half_quarter(n, second):
        return pl.ds(depth // 4 * n + depth // 8 * second, depth // 8)

    z_next = (add4(z, 1), add4(z, 3))
    y_others = (y_up, y_down, y_far)

    def wmove(m):
        if m < 3:
            ref, ctx, tp = weight.at[core, y, quarter(z)], c, side + y_others[m]
        else:
            n, up = (m - 3) % 6 // 2, (m - 3) % 2
            cut = quarter(z) if m < 9 else half_quarter(z_next[1 - up], up)
            ref, tp = weight.at[core, y_others[n], cut], t
            ctx = 2 * (z_up, z_down)[up] + core
        return push(ref, ref, wsend.at[m], wrecv.at[m], ctx, tp)

    def warrive(m):
        if m < 3:
            ref = weight.at[core, (y_down, y_up, y_far)[m], quarter(z)]
        else:
            n, up = (m - 3) % 6 // 2, (m - 3) % 2
            cut = quarter(z_next[1 - up]) if m < 9 else half_quarter(add4(z, 2), up)
            ref = weight.at[core, y_others[n], cut]
        push(ref, ref, wsend.at[m], wrecv.at[m], sibling, t).wait_recv()

    def share(n):
        ref = weight.at[core, add4(y, n)]
        return push(ref, ref, csend.at[n], crecv.at[n], sibling, t)

    def shared(n):
        ref = weight.at[1 - core, add4(y, n)]
        push(ref, ref, csend.at[n], crecv.at[n], sibling, t).wait_recv()

    own_copy.wait()
    for m in (2, 0, 1):
        wmove(m).start()
    share(0).start()

    for d in range(N_TP):
        j = lax.rem(t + d, N_TP)
        load(d).wait()
        x = jnp.dot(ordered, pweight[d], preferred_element_type=f32)
        x = 0.5 * x * (1.0 + lax.erf(x * math.sqrt(0.5)))
        shift = j * part - (j * part) // HS * HS
        x = jnp.where(shift > 0, pltpu.roll(x, block - HS // 2, 1), x)
        x = jnp.where(lane < part, x, tail)
        halves = [
            x[:, n * 2 * HS : (n + 1) * 2 * HS].reshape(N_CTX, CAP, 2 * HS) for n in range(2)
        ]
        outgoing[d] = jnp.concatenate(halves, axis=1).astype(jnp.bfloat16)

        def deliver(n, unused):
            oc = lax.rem(c + n, N_CTX)
            push(outgoing.at[d, oc], incoming.at[me], fr_send, fr_recv, oc, j).start()
            return unused

        if d == 0:
            pltpu.make_async_copy(outgoing.at[0, c], incoming.at[me], fr_recv).start()
        else:
            push(outgoing.at[d, c], incoming.at[me], fr_send, fr_recv, c, j).start()
        lax.fori_loop(1, N_CTX, deliver, 0)
        if d == 4:
            for m in range(3):
                warrive(m)
            for m in range(3, 9):
                wmove(m).start()

    take_text.wait()
    for a in range(2):
        for n in range(4):
            block_cols = slice((4 * a + n) * HS, (4 * a + n + 1) * HS)
            placed[a, n] = jnp.transpose(turned_text[:, block_cols].astype(f32)).astype(
                jnp.bfloat16
            )
    pltpu.make_async_copy(incoming, incoming, fr_recv).wait()

    def row_block(n, across):
        j = add4(y, n)
        tp = j + (4 - side if across else side)
        return push(
            placed.at[:, j], rows.at[t], send.at[n, across], recv.at[t], c, tp
        )

    def gain_block(d):
        return push(gain, gains.at[t], gsend.at[d], grecv.at[t], c, lax.rem(t + d, N_TP))

    pltpu.make_async_copy(gain, gains.at[t], grecv.at[t]).start()
    for d in range(1, N_TP):
        gain_block(d).start()
    arrived = incoming[...].astype(f32)
    slots = devices * CAP
    left = arrived[:, :CAP].reshape(slots, 2 * HS)
    right = arrived[:, CAP:].reshape(slots, 2 * HS)
    edge = part - 2 * HS
    at = right[:, edge : edge + 1] * 32.0 + right[:, edge + 32 : edge + 33]
    at = jnp.transpose(jnp.broadcast_to(at, (slots, HS)))[0:1, :]
    left = left.astype(jnp.bfloat16)
    right = right.astype(jnp.bfloat16)
    group = 2 * HS
    offset = lax.broadcasted_iota(jnp.int32, (group, 1), 0)
    offset = offset // HS * CH + offset % HS
    for n in range(4):
        j = add4(y, n)
        row = offset + j * HS
        hit = jnp.where(row.astype(f32) == at, 1.0, 0.0).astype(jnp.bfloat16)
        new_left = jnp.dot(hit, left, preferred_element_type=f32)
        new_right = jnp.dot(hit, right, preferred_element_type=f32)
        framed = new_right[:, 2 * HS - 1 :] > 0.5
        old = placed[:, j].reshape(group, part).astype(f32)
        placed[:, j, :, : 2 * HS] = (
            jnp.where(framed, new_left, old[:, : 2 * HS]).astype(jnp.bfloat16)
        ).reshape(2, HS, 2 * HS)
        placed[:, j, :, 2 * HS :] = (
            jnp.where(framed, new_right[:, :edge], old[:, 2 * HS :]).astype(jnp.bfloat16)
        ).reshape(2, HS, edge)
        row_block(n, 1).start()
        if n == 0:
            pltpu.make_async_copy(placed.at[:, y], rows.at[t], recv.at[t]).start()
        else:
            row_block(n, 0).start()

    for one in kv_loads:
        one.wait()

    for m in range(3, 9):
        warrive(m)
    for m in range(9, 15):
        wmove(m).start()
    total = jnp.zeros((group, 1), f32)
    for d in range(N_TP):
        j = lax.rem(t + d, N_TP)
        push(gain, gains.at[j], gsend.at[0], grecv.at[j], sibling, t).wait_recv()
        push(rows.at[j], rows.at[j], send.at[0, 0], recv.at[j], sibling, t).wait_recv()
        x = rows[j].reshape(group, part).astype(f32)
        total = total + jnp.sum(x * x, axis=1, keepdims=True)

    keep = pltpu.make_async_copy(rows.at[pl.ds(side, 4)], rows_out, osem)
    keep.start()

    for m in range(9, 15):
        warrive(m)
    for n in range(1, 4):
        share(n).start()
    inverse = lax.rsqrt(total / width + 1e-06)
    for j in range(N_TP):
        x = rows[j].reshape(group, part).astype(f32)
        normed[j] = (x * inverse * gains[j, 0:1, :].astype(f32)).astype(jnp.bfloat16)

    def product(piece):
        total = None
        for j in range(N_TP):
            term = jnp.dot(
                normed[j], piece(slice(j * part, (j + 1) * part)), preferred_element_type=f32
            )
            total = term if total is None else total + term
        return total

    def rotated(x, cos, sin):
        return (x * cos + pltpu.roll(x, HS // 2, 1) * sin).astype(jnp.bfloat16).reshape(2, HS, HS)

    goal = [pair_of(pair, 4 * n + y) for n in range(2)]
    mine = pl.ds(2 * core, 2)

    def kv_push(n, which, m):
        return push(
            kv.at[which, m // 2, :, pl.ds(OFF * n, OFF), :], kv_out.at[pair, mine],
            ksend.at[n, which, m], krecv.at[pair, core], 2 * goal[n] + which, side + m,
        )

    def q_push(n, k, m):
        return push(
            query.at[m, :, :, pl.ds(OFF * n + HALF * k, HALF), :], query_out.at[:, pair, mine],
            qsend.at[n, k, m], qrecv.at[pair, core], 2 * goal[n] + k, side + m,
        )

    def is_here(n, k, m):
        return jnp.logical_and(goal[n] == pair, jnp.logical_and(core == k, y == m))

    cos = cosine[...]
    sin = sine[...]
    for which in range(2):
        out = product(lambda cut: kv_weight[which, cut, :])
        for h in range(2):
            x = out[:, h * HS : (h + 1) * HS]
            kv[which, h] = rotated(x, cos, sin) if which == 0 else x.astype(
                jnp.bfloat16
            ).reshape(2, HS, HS)
        for m in range(4):
            for n in range(2):

                @pl.when(is_here(n, which, m))
                def _():
                    pltpu.make_async_copy(
                        kv.at[which, m // 2, :, pl.ds(OFF * n, OFF), :], kv_out.at[pair, mine],
                        krecv.at[pair, core],
                    ).start()

                @pl.when(jnp.logical_not(is_here(n, which, m)))
                def _():
                    kv_push(n, which, m).start()

    for m0 in range(4):
        m = add4(y, m0)
        shared(m0)
        out = product(
            lambda cut: jnp.concatenate([weight[0, m, cut], weight[1, m, cut]], axis=1)
        )
        for h in range(2):
            query[m, h] = rotated(out[:, h * HS : (h + 1) * HS], cos, sin)
        for n in range(2):
            for k in range(2):
                if m0 == 0:
                    here = jnp.logical_and(goal[n] == pair, core == k)

                    @pl.when(here)
                    def _():
                        pltpu.make_async_copy(
                            query.at[m, :, :, pl.ds(OFF * n + HALF * k, HALF), :],
                            query_out.at[:, pair, mine], qrecv.at[pair, core],
                        ).start()

                    @pl.when(jnp.logical_not(here))
                    def _():
                        q_push(n, k, m).start()

                else:
                    q_push(n, k, m).start()

    for e in range(PAIRS):
        for a in range(2):
            two = pl.ds(2 * a, 2)
            ref = kv_out.at[e, two]
            push(ref, ref, ksend.at[0, 0, 0], krecv.at[e, a], sibling, t).wait_recv()
            ref = query_out.at[:, e, two]
            push(ref, ref, qsend.at[0, 0, 0], qrecv.at[e, a], sibling, t).wait_recv()
    keep.wait()
    pltpu.make_async_copy(
        incoming.at[pl.ds(0, devices - 1)], incoming.at[pl.ds(0, devices - 1)], fr_send
    ).wait()
    for m in range(15):
        wmove(m).wait_send()
    for n in range(4):
        share(n).wait_send()
        row_block(n, 1).wait_send()
        if n:
            row_block(n, 0).wait_send()
    for d in range(1, N_TP):
        gain_block(d).wait_send()
    for n in range(2):
        for k in range(2):
            for m in range(4):

                @pl.when(jnp.logical_not(is_here(n, k, m)))
                def _():
                    kv_push(n, k, m).wait_send()
                    q_push(n, k, m).wait_send()


def intake(
    text_embed, norm_gain, frame_features, frame_positions, span_order, tables,
    projector, query_weight, key_weight, value_weight,
):
    tok_rows, part = text_embed.shape
    depth = query_weight.shape[0]
    devices = N_CTX * N_TP
    vm = pl.BlockSpec(memory_space=pltpu.VMEM)
    anywhere = pl.BlockSpec(memory_space=pl.ANY)
    dma = pltpu.SemaphoreType.DMA
    bf16 = jnp.bfloat16
    return pl.pallas_call(
        intake_kernel,
        out_shape=(
            jax.ShapeDtypeStruct((4, 2, HS, part), bf16),
            jax.ShapeDtypeStruct((2, PAIRS, 4, HALF, HS), bf16),
            jax.ShapeDtypeStruct((PAIRS, 4, OFF, HS), bf16),
        ),
        in_specs=[vm] * 5 + [anywhere] * 6,
        out_specs=(vm, vm, vm),
        scratch_shapes=[
            pltpu.VMEM(frame_features.shape, bf16),
            pltpu.VMEM((part, tok_rows), bf16),
            pltpu.VMEM((N_TP, projector.shape[0], 4 * HS), bf16),
            pltpu.VMEM((N_TP, N_CTX, 2 * CAP, 2 * HS), bf16),
            pltpu.VMEM((devices, 2 * CAP, 2 * HS), bf16),
            pltpu.VMEM((2, 4, HS, part), bf16),
            pltpu.VMEM((N_TP, 2, HS, part), bf16),
            pltpu.VMEM((N_TP, 16, part), bf16),
            pltpu.VMEM((N_TP, 2 * HS, part), bf16),
            pltpu.VMEM((2, 4, depth, HS), bf16),
            pltpu.VMEM((2, depth, 2 * HS), bf16),
            pltpu.VMEM((4, 2, 2, HS, HS), bf16),
            pltpu.VMEM((2, 2, 2, HS, HS), bf16),
            dma((2,)),
            dma((N_TP,)),
            dma,
            dma((2,)),
            dma,
            dma,
            dma((15,)),
            dma((15,)),
            dma((4,)),
            dma((4,)),
            dma((4, 2)),
            dma((N_TP,)),
            dma((N_TP,)),
            dma((N_TP,)),
            dma,
            dma((2, 2, 4)),
            dma((PAIRS, 2)),
            dma((2, 2, 4)),
            dma((PAIRS, 2)),
        ],
        compiler_params=pltpu.CompilerParams(
            collective_id=1, has_side_effects=True, vmem_limit_bytes=56 * 2**20
        ),
        name="intake",
    )(
        jnp.broadcast_to(norm_gain[None, :], (16, part)),
        frame_positions.reshape(1, -1),
        span_order.reshape(1, -1),
        *tables,
        text_embed.T,
        frame_features,
        projector,
        query_weight,
        key_weight,
        value_weight,
    )


def attention_kernel(
    slot_of, span_order, query_in, kv_in, out_weight, rows_in, out,
    query, kv_own, rows, kv, q, summed, largest, limit, attended, heads, weight, product, result,
    isem, send, recv, pass_send, half_send, half_recv, wsend, wrecv, csend, crecv, own_sem,
    hsend, hrecv, rsend, rrecv,
):
    f32 = jnp.float32
    scale = LOG2E / math.sqrt(HS)
    c = lax.axis_index("ctx")
    t = lax.axis_index("tp")
    pair = c // 2
    core = c % 2
    sibling = c + 1 - 2 * core
    base = pair // 4 * 4
    other = 4 - base
    z = pair % 4
    up, down, far = (add4(z, n) for n in (1, 3, 2))
    z_up, z_down, z_far = base + up, base + down, base + far
    keys = kv.shape[2]
    x_own, x_up, x_down, x_far = other + z, other + up, other + down, other + far
    y = lax.rem(t, 4)
    side = t - y
    half = t // 4
    across = 4 - side
    t_up, t_down, t_far = (side + add4(y, n) for n in (1, 3, 2))
    a_own, a_up, a_down, a_far = (across + add4(y, n) for n in (0, 1, 3, 2))
    x_next = 2 * x_own + core
    depth, cols = weight.shape[2:]

    def columns(of_half):
        return out_weight.at[:, pl.ds(pl.multiple_of(cols * (2 * of_half + core), HS), cols)]

    take_kv, take_query, take_rows = (
        pltpu.make_async_copy(src, dst, isem.at[n])
        for n, (src, dst) in enumerate(((kv_in, kv_own), (query_in, query), (rows_in, rows)))
    )
    take_kv.start()
    take_query.start()
    own_copy = pltpu.make_async_copy(columns(half), weight.at[core, t], own_sem)
    own_copy.start()
    take_rows.start()
    barrier = pltpu.get_barrier_semaphore()
    signal(barrier, sibling, t)
    for e in (z_up, z_down, z_far, x_own):
        signal(barrier, 2 * e + core, t)
    signal(barrier, x_next, a_own)
    for j in (t_up, t_down, t_far):
        signal(barrier, c, j)
    first = y == 2 * (pair // 4)
    for n in range(2):
        origin = pair_of(pair, 4 * n + y)
        for k in range(2):
            for d in range(N_TP):
                j = lax.rem(t + d, N_TP)
                if n == 0 and d == 0:

                    @pl.when(jnp.logical_not(jnp.logical_and(first, core == k)))
                    def _():
                        signal(barrier, 2 * origin + k, j)

                else:
                    signal(barrier, 2 * origin + k, j)
    take_kv.wait()
    for j in range(32):
        kv[pair, core, j * OFF : (j + 1) * OFF] = kv_own[slot_of[j]]
    pl.semaphore_wait(barrier, 9 + 32 - jnp.where(first, 1, 0))

    def wmove(m):
        own = weight.at[core, t]
        passed = weight.at[core, a_own]
        if m == 0:
            src, dst, ctx, tp = columns(1 - half), own, x_next, a_own
        else:
            src = dst = own if m < 4 else passed
            ctx, tp = c, (t_up, t_down, t_far)[(m - 1) % 3]
        return push(src, dst, wsend.at[m], wrecv.at[m], ctx, tp)

    def warrive(m):
        ref = weight.at[core, (a_own, t_down, t_up, t_far, a_down, a_up, a_far)[m]]
        push(ref, ref, wsend.at[m], wrecv.at[m], sibling, t).wait_recv()

    def give(g):
        ref = weight.at[core, g]
        return push(ref, ref, csend.at[g], crecv.at[g], sibling, t)

    def transfer(e, to, index):
        block = kv.at[e, core]
        return push(block, block, send.at[index], recv.at[e, core], 2 * to + core, t)

    def share(e):
        block = kv.at[e, core]
        return push(block, block, pass_send.at[e], recv.at[e, core], sibling, t)

    def arrive(e, which):
        block = kv.at[e, which]
        push(block, block, send.at[0], recv.at[e, which], sibling, t).wait_recv()

    share(pair).start()
    moves = (
        (pair, x_own), (pair, z_up), (pair, z_down), (x_own, z_up), (x_own, z_down), (z_far, x_own),
    )

    def pass_half(n):
        e, to = ((z_down, z_up), (z_up, z_down))[n]
        block = kv.at[e, core, pl.ds(keys // 2 * n, keys // 2)]
        return push(block, block, half_send.at[n], half_recv.at[n], 2 * to + core, t)

    def arrive_half(n):
        block = kv.at[z_far, core, pl.ds(keys // 2 * n, keys // 2)]
        push(block, block, half_send.at[n], half_recv.at[n], sibling, t).wait_recv()

    for index in range(3):
        transfer(*moves[index], index).start()
    own_copy.wait()
    for m in (1, 2, 3):
        wmove(m).start()
    take_query.wait()
    for j in range(32):
        q[j * OFF : (j + 1) * OFF] = query[:, slot_of[j]].reshape(2 * HALF, HS)

    group = 8 * HALF
    row = lax.broadcasted_iota(jnp.int32, (group, 1), 0)
    col = lax.broadcasted_iota(jnp.int32, (1, 4 * OFF), 1)

    def starts(index, i, e):
        value = jnp.zeros(index.shape, jnp.int32)
        for a in range(4):
            kind = class_of(slot_of[4 * i + a] // 4, e)
            start = a * CH + HS * lax.rem(kind, 4) + OFF * (kind // 4)
            value = jnp.where(index // OFF == a, start, value)
        return value

    for i in range(8):
        limit[i * group : (i + 1) * group] = starts(row, i, pair) + HALF * core + row % HALF

    def update(e, first_set):
        def chunk(i):
            return slice(i * group, (i + 1) * group), 4 * OFF * (i + 1)

        def scores(i):
            here, width = chunk(i)
            return lax.dot_general(
                q[here], kv[e, 0, :width], (((1,), (1,)), ((), ())), preferred_element_type=f32
            )

        def soft(i, s):
            here, width = chunk(i)
            at = starts(col, i, e) + col % OFF
            edge = jnp.where(at <= limit[here], s[:, width - 4 * OFF :], -1e30)
            s = edge if i == 0 else jnp.concatenate([s[:, : width - 4 * OFF], edge], axis=1)
            top = jnp.max(s, axis=1, keepdims=True)
            if not first_set:
                top = jnp.maximum(top, largest[here])
                summed[here] = summed[here] * jnp.exp2((largest[here] - top) * scale)
            largest[here] = top
            return jnp.exp2((s - top) * scale).astype(jnp.bfloat16)

        def gather(i, weights):
            here, width = chunk(i)
            beside = jnp.concatenate(
                [kv[e, 1, :width], jnp.ones((width, HS), jnp.bfloat16)], axis=1
            )
            new = jnp.dot(weights, beside, preferred_element_type=f32)
            summed[here] = new if first_set else summed[here] + new

        s = scores(7)
        held = None
        for i in range(7, -1, -1):
            ahead = scores(i - 1) if i else None
            weights = soft(i, s)
            if held is not None:
                gather(*held)
            held = (i, weights)
            s = ahead
        gather(*held)

    arrive(pair, 1 - core)
    update(pair, True)
    arrive(x_own, core)
    share(x_own).start()
    arrive(z_down, core)
    pass_half(0).start()
    share(z_down).start()
    arrive(z_up, core)
    pass_half(1).start()
    share(z_up).start()
    wmove(0).start()
    give(t).start()
    order = (x_own, z_up, z_down, z_far, x_up, x_down, x_far)

    def step(n, unused):
        e = order[6]
        for index in range(6):
            e = jnp.where(n == index, order[index], e)

        @pl.when(n == 1)
        def _():
            arrive_half(0)
            arrive_half(1)
            for index in (5, 3, 4):
                transfer(*moves[index], index).start()
            share(z_far).start()

        @pl.when(n == 4)
        def _():
            arrive(x_up, core)
            share(x_up).start()
            arrive(x_down, core)
            share(x_down).start()

        @pl.when(n == 5)
        def _():
            warrive(0)
            for m in (4, 5, 6):
                wmove(m).start()
            give(a_own).start()

        @pl.when(n == 6)
        def _():
            arrive(x_far, core)
            share(x_far).start()

        arrive(e, 1 - core)
        update(e, False)
        return unused

    lax.fori_loop(0, 7, step, 0)

    for i in range(8):
        here = slice(i * group, (i + 1) * group)
        done = (summed[here, :HS] / summed[here, HS : HS + 1]).astype(jnp.bfloat16)
        done = done.reshape(4, 2, HALF, HS)
        for a in range(4):
            attended[0, 4 * i + a] = jnp.concatenate([done[a, 0], done[a, 1]], axis=1)

    def head_push(d, a, n):
        e = lax.rem(pair + d, PAIRS)
        kind = class_of(e, pair)
        at = pl.ds(OFF * (kind // 4) + HALF * core, HALF)
        return push(
            attended.at[1, pl.ds(4 * e + 2 * a, 2)], heads.at[t, :, at, :], hsend.at[d, a, n],
            hrecv.at[t, kind // 4, core], 2 * e + a, lax.rem(4 * n + lax.rem(kind, 4) + side, N_TP),
        )

    def is_here(d, a, n):
        if d or n:
            return jnp.bool_(False)
        return jnp.logical_and(first, core == a)

    for j in range(32):
        attended[1, j] = attended[0, span_order[j]]
    for d in range(PAIRS):
        for n in range(2):
            for a in range(2):
                if d or n:
                    head_push(d, a, n).start()
                else:

                    @pl.when(is_here(d, a, n))
                    def _():
                        pltpu.make_async_copy(
                            attended.at[1, pl.ds(4 * pair + 2 * a, 2)],
                            heads.at[t, :, pl.ds(HALF * core, HALF), :], hrecv.at[t, 0, core],
                        ).start()

                    @pl.when(jnp.logical_not(is_here(d, a, n)))
                    def _():
                        head_push(d, a, n).start()

    for m in range(1, 7):
        warrive(m)
    for g in (t_up, t_down, t_far, a_up, a_down, a_far):
        give(g).start()
    for g in range(N_TP):
        ref = weight.at[1 - core, g]
        push(ref, ref, csend.at[g], crecv.at[g], sibling, t).wait_recv()
    for g in range(N_TP):
        for n in range(2):
            for k in range(2):
                ref = heads.at[g, :, pl.ds(OFF * n + HALF * k, HALF), :]
                push(ref, ref, hsend.at[0, 0, 0], hrecv.at[g, n, k], sibling, t).wait_recv()

    take_rows.wait()

    part = out.shape[-1]
    place = pl.ds(HS * y, HS)

    def send_home(n):
        return push(
            result.at[n], out.at[:, place, :], rsend.at[n], rrecv.at[y], c, side + n
        )

    for n in range(4):
        if n % 2 == 0:
            for begin, end in ((0, 4 * HS), (4 * HS, cols)):
                total = jnp.zeros((2 * HS, end - begin), f32)
                for g in range(N_TP):
                    x = heads[g].reshape(2 * HS, 2 * HS)
                    total = total + jnp.dot(
                        x, weight[n // 2, g, :, begin:end], preferred_element_type=f32
                    ).astype(jnp.bfloat16).astype(f32)
                product[:, begin:end] = total
            total = product[:, : 4 * HS][:, :part]
        else:
            start = part // HS * HS
            total = product[:, start : start + 4 * HS]
            total = pltpu.roll(total, 4 * HS - (part - start), 1)[:, :part]
        placed = rows[n].reshape(2 * HS, part).astype(f32)
        result[n] = (placed + total).astype(jnp.bfloat16).reshape(2, HS, part)

        @pl.when(y == n)
        def _():
            pltpu.make_async_copy(result.at[n], out.at[:, place, :], rrecv.at[y]).start()

        @pl.when(y != n)
        def _():
            send_home(n).start()

    for n in range(4):
        ref = out.at[:, pl.ds(HS * n, HS), :]
        push(ref, ref, rsend.at[0], rrecv.at[n], sibling, t).wait_recv()
    for n in range(2):
        pass_half(n).wait_send()
    for index in range(6):
        transfer(*moves[index], index).wait_send()
    for e in range(PAIRS):
        share(e).wait_send()
    for m in range(7):
        wmove(m).wait_send()
    for g in range(N_TP):
        give(g).wait_send()
    for d in range(PAIRS):
        for n in range(2):
            for a in range(2):
                if d or n:
                    head_push(d, a, n).wait_send()
                else:

                    @pl.when(jnp.logical_not(is_here(d, a, n)))
                    def _():
                        head_push(d, a, n).wait_send()

    for n in range(4):

        @pl.when(y != n)
        def _():
            send_home(n).wait_send()


def attention(slot_of, span_order, query, kv, out_weight, rows):
    vm = pl.BlockSpec(memory_space=pltpu.VMEM)
    sm = pl.BlockSpec(memory_space=pltpu.SMEM)
    anywhere = pl.BlockSpec(memory_space=pl.ANY)
    dma = pltpu.SemaphoreType.DMA
    bf16 = jnp.bfloat16
    keys = 32 * OFF
    depth, width = out_weight.shape
    part = rows.shape[-1]
    return pl.pallas_call(
        attention_kernel,
        out_shape=jax.ShapeDtypeStruct((2, CH, part), bf16),
        in_specs=[sm, sm, anywhere, anywhere, anywhere, anywhere],
        out_specs=vm,
        scratch_shapes=[
            pltpu.VMEM(query.shape, bf16),
            pltpu.VMEM(kv.shape, bf16),
            pltpu.VMEM(rows.shape, bf16),
            pltpu.VMEM((PAIRS, 2, keys, HS), bf16),
            pltpu.VMEM((keys, HS), bf16),
            pltpu.VMEM((keys, 2 * HS), jnp.float32),
            pltpu.VMEM((keys, 1), jnp.float32),
            pltpu.VMEM((keys, 1), jnp.int32),
            pltpu.VMEM((2, 32, HALF, 2 * HS), bf16),
            pltpu.VMEM((N_TP, 2, HS, 2 * HS), bf16),
            pltpu.VMEM((2, N_TP, depth, width // 4), bf16),
            pltpu.VMEM((2 * HS, width // 4), jnp.float32),
            pltpu.VMEM((4, 2, HS, part), bf16),
            dma((3,)),
            dma((6,)),
            dma((PAIRS, 2)),
            dma((PAIRS,)),
            dma((2,)),
            dma((2,)),
            dma((7,)),
            dma((7,)),
            dma((N_TP,)),
            dma((N_TP,)),
            dma,
            dma((PAIRS, 2, 2)),
            dma((N_TP, 2, 2)),
            dma((4,)),
            dma((4,)),
        ],
        compiler_params=pltpu.CompilerParams(
            collective_id=2, has_side_effects=True, vmem_limit_bytes=60 * 2**20
        ),
        name="attention",
    )(slot_of, span_order, query, kv, out_weight, rows)


def per_device(
    text_embed,
    frame_features,
    frame_positions,
    span_order,
    projector,
    norm_gain,
    query_weight,
    key_weight,
    value_weight,
    out_weight,
):
    tok_rows, part = text_embed.shape
    c = lax.axis_index("ctx")
    t = lax.axis_index("tp")
    slots = span_order.shape[0]
    index = jnp.arange(slots, dtype=jnp.int32)
    slot_of = jnp.sum(
        jnp.where(span_order[None, :] == index[:, None], index[None, :], 0), axis=1
    )
    spans = lax.dynamic_slice_in_dim(span_order, 2 * c, 2, 0)
    positions = (
        spans[:, None] * CH + HS * (t % 4) + jnp.arange(HS, dtype=jnp.int32)[None, :]
    ).reshape(-1)
    half = HS // 2
    lane = jnp.arange(HS, dtype=jnp.int32)
    freqs = 1000000.0 ** (-((lane % half).astype(jnp.float32) * 2.0 / HS))
    angles = positions.astype(jnp.float32)[:, None] * freqs[None, :]
    cosine = jnp.cos(angles)
    sine = jnp.where(lane[None, :] < half, -1.0, 1.0) * jnp.sin(angles)
    rows, query, kv = intake(
        text_embed, norm_gain, frame_features, frame_positions, span_order, (cosine, sine),
        projector, query_weight, key_weight, value_weight,
    )
    mixed = attention(
        slot_of, span_order, query.reshape(2, 32, HALF, HS), kv.reshape(32, OFF, HS),
        out_weight, rows,
    )
    return mixed.reshape(tok_rows, part)


def solution(mesh):
    in_specs = (
        P("ctx", "tp"),
        P(("ctx", "tp"), None),
        P(("ctx", "tp")),
        P(),
        P(),
        P("tp"),
        P(None, "tp"),
        P(),
        P(),
        P("tp", None),
    )
    out_specs = P("ctx", "tp")
    return jax.shard_map(
        per_device, mesh=mesh, in_specs=in_specs, out_specs=out_specs, check_vma=False
    )
```
